128 devices in a mesh: dp: 16 (over x, y), fsdp: 8 (over z, core).
Axes of the slice: x: 4, y: 4, z: 4, core: 2. Of those that a mesh axis runs over, the one named last changes fastest.
Arguments:
- source: bfloat16 [2, 128, 256, 512], P(None, ('dp', 'fsdp')), may hold values from -24 to 24
- target: bfloat16 [2, 128, 256, 512], P(None, ('dp', 'fsdp')), may hold values from -24 to 24
- src_len: int32 [2, 128], P(None, ('dp', 'fsdp')), may hold values from 21 to 256, as said below
- tgt_len: int32 [2, 128], P(None, ('dp', 'fsdp')), may hold values from 21 to 256, as said below
- out_grad: bfloat16 [2, 128, 256, 512], P(None, ('dp', 'fsdp')), may hold values from -6 to 6
- attn_proj: bfloat16 [3, 3, 512, 512], P(None, None, ('dp', 'fsdp')), may hold values from -0.25 to 0.25
- attn_out: bfloat16 [3, 512, 512], P(None, ('dp', 'fsdp')), may hold values from -1 to 1
- attn_bias: bfloat16 [3, 3, 512], P(None, None, ('dp', 'fsdp')), may hold values from -2 to 2
- norm_gain: bfloat16 [5, 512], P(None, ('dp', 'fsdp')), may hold values from 0.25 to 1.75
- norm_shift: bfloat16 [5, 512], P(None, ('dp', 'fsdp')), may hold values from -1.5 to 1.5
- ffn_in: bfloat16 [2, 512, 2048], P(None, ('dp', 'fsdp')), may hold values from -0.25 to 0.25
- ffn_out: bfloat16 [2, 2048, 512], P(None, ('dp', 'fsdp')), may hold values from -0.25 to 0.25
- ffn_bias_in: bfloat16 [2, 2048], P(None, ('dp', 'fsdp')), may hold values from -2 to 2
- ffn_bias_out: bfloat16 [2, 512], P(None, ('dp', 'fsdp')), may hold values from -2 to 2
Outputs:
- dec_out: bfloat16 [2, 128, 256, 512], P(None, ('dp', 'fsdp'))
- source_grad: float32 [2, 128, 256, 512], P(None, ('dp', 'fsdp'))
- target_grad: float32 [2, 128, 256, 512], P(None, ('dp', 'fsdp'))
- g_attn_proj: float32 [3, 3, 512, 512], P(None, None, ('dp', 'fsdp'))
- g_attn_out: float32 [3, 512, 512], P(None, ('dp', 'fsdp'))
- g_attn_bias: float32 [3, 3, 512], P(None, None, ('dp', 'fsdp'))
- g_norm_gain: float32 [5, 512], P(None, ('dp', 'fsdp'))
- g_norm_shift: float32 [5, 512], P(None, ('dp', 'fsdp'))
- g_ffn_in: float32 [2, 512, 2048], P(None, ('dp', 'fsdp'))
- g_ffn_out: float32 [2, 2048, 512], P(None, ('dp', 'fsdp'))
- g_ffn_bias_in: float32 [2, 2048], P(None, ('dp', 'fsdp'))
- g_ffn_bias_out: float32 [2, 512], P(None, ('dp', 'fsdp'))
The draws below stay inside these ranges and needn't reach their ends.
Inputs may be any that keep to these rules, and one draw needn't show every extreme that they name: `src_len`: most sentences are short, a few have up to 256 tokens; 256 is reached by some source sentence in every draw. `tgt_len`: most sentences are short, a few have up to 256 tokens; 256 is reached by some target sentence in every draw.
All inputs are finite; a program needn't handle non-finite values.
Results may differ from the reference program's by a relative error of at most 0.025.
Values may be sent and summed in bfloat16 or wider, within the bound.
No kernel may reach another device: no remote copies, remote signals or barrier semaphores. Data moves between devices by JAX's collectives and lax.ppermute only.
A program may use at most 192 MiB of HBM per device.

```python
import math
import jax
import jax.numpy as jnp
from jax import lax

D = 512
HEADS = 8
HEAD = 64
FF = 2048
SLOTS = 256
MICRO = 2
PAIRS = 128


def ragged_lengths(key):
    shortest = max(1, SLOTS // 12)
    drawn_top = max(shortest + 1, SLOTS // 4 + 1)
    first_key, second_key, third_key, fourth_key = jax.random.split(key, 4)
    drawn = jax.random.randint(first_key, (MICRO, PAIRS), shortest, drawn_top)
    longer = jax.random.randint(second_key, (MICRO, PAIRS), 3 * SLOTS // 4, SLOTS + 1)
    picked = jax.random.randint(third_key, (MICRO, PAIRS), 0, 32) == 0
    lengths = jnp.where(picked, longer, drawn)
    place = jax.random.randint(fourth_key, (), 0, PAIRS)
    return lengths.at[0, place].set(SLOTS).astype(jnp.int32)


def draw_src_len(key, part):
    key = jax.random.fold_in(key, 1)
    return ragged_lengths(key)


def draw_tgt_len(key, part):
    key = jax.random.fold_in(key, 2)
    return ragged_lengths(key)


def with_spikes(result, own_key, source, target, parts, factor):
    owner, partner = [(jnp.arange(result.shape[dim]) // (result.shape[dim] // parts)).reshape([-1 if axis == dim else 1 for axis in range(result.ndim)]) for dim in (source, target)]
    chosen = jax.random.permutation(own_key, parts)[partner]
    strong = (owner == chosen) | (owner == (partner + parts // 2) % parts)
    return jnp.where(strong, factor * result, result)


def block_scale(own_key, extent, shards, low, largest):
    def one(dim, shards_of):
        heights = jax.random.uniform(jax.random.fold_in(jax.random.fold_in(own_key, 6), dim), (shards_of,), jnp.float32, low / len(shards), largest / len(shards))
        return jnp.repeat(jnp.exp(heights), extent[dim] // shards_of).reshape((-1,) + (1,) * (len(extent) - dim - 1))

    factor_of = one(*shards[0])
    for cut in shards[1:]:
        factor_of = factor_of * one(*cut)
    return factor_of


def noise(rng, dims, width, limit, shards=(), held_as=jnp.bfloat16):
    loudness = block_scale(rng, dims, shards, -0.22, 0.18) if shards else 1.0
    drawn = jax.random.normal(rng, dims, jnp.float32) * width * loudness
    return jnp.minimum(jnp.maximum(drawn, -limit), limit).astype(held_as)


def gaussian_with(rng, dims, width, reach, shards, heavy, kind=jnp.bfloat16):
    entries = width * jax.random.normal(rng, dims, jnp.float32)
    if shards:
        entries = entries * block_scale(rng, dims, shards, -0.22, 0.18)
    return jnp.clip(with_spikes(entries, jax.random.fold_in(rng, 3), *heavy), -reach, reach).astype(kind)


def setup_inputs(seed: int = 0) -> dict:
    splits = jax.random.split(jax.random.key(seed), 15)
    source = gaussian_with(splits[0], (MICRO, PAIRS, SLOTS, D), 1.0, 24.0, ((1, 128),), (1, 3, 128, 5.5))
    target = gaussian_with(splits[1], (MICRO, PAIRS, SLOTS, D), 1.0, 24.0, ((1, 128),), (1, 3, 128, 5.5))
    src_len = draw_src_len(jax.random.fold_in(splits[14], 71), 0)
    tgt_len = draw_tgt_len(jax.random.fold_in(splits[14], 71), 0)
    out_grad = noise(splits[4], (MICRO, PAIRS, SLOTS, D), 1.0, 6.0, ((1, 128),))
    attn_proj = noise(splits[5], (3, 3, D, D), D ** -0.5, 0.25, ((2, 128),))
    attn_out = noise(splits[6], (3, D, D), (D // 16) ** -0.5, 1.0, ((1, 128),))
    attn_bias = noise(splits[7], (3, 3, D), 0.3, 2.0, ((2, 128),))
    norm_gain = jnp.clip(1.0 + 0.15 * jax.random.normal(splits[8], (5, D), jnp.float32), 0.25, 1.75).astype(jnp.bfloat16)
    norm_shift = noise(splits[9], (5, D), 0.2, 1.5, ((1, 128),))
    ffn_in = noise(splits[10], (2, D, FF), D ** -0.5, 0.25, ((1, 128),))
    ffn_out = noise(splits[11], (2, FF, D), (FF // 4) ** -0.5, 0.25, ((1, 128),))
    ffn_bias_in = noise(splits[12], (2, FF), 0.3, 2.0, ((1, 128),))
    ffn_bias_out = noise(splits[13], (2, D), 0.3, 2.0, ((1, 128),))
    return {"source": source, "target": target, "src_len": src_len, "tgt_len": tgt_len, "out_grad": out_grad, "attn_proj": attn_proj, "attn_out": attn_out, "attn_bias": attn_bias, "norm_gain": norm_gain, "norm_shift": norm_shift, "ffn_in": ffn_in, "ffn_out": ffn_out, "ffn_bias_in": ffn_bias_in, "ffn_bias_out": ffn_bias_out}


HIGHEST = lax.Precision.HIGHEST
EPSILON = 1e-05
NEGATIVE = -1000000000.0

@jax.custom_vjp
def low(v):
    return lax.optimization_barrier(v.astype(jnp.bfloat16)).astype(jnp.float32)

@jax.custom_vjp
def low_back(v):
    return v

def low_keep(v):
    return (low(v), None)

def low_pass(kept, grad):
    return (grad,)

def back_keep(v):
    return (v, None)

def back_low(kept, grad):
    return (low(grad),)
low.defvjp(low_keep, low_pass)
low_back.defvjp(back_keep, back_low)

def product(left_side, right_side):
    return jnp.matmul(left_side, right_side, precision=HIGHEST)

def layer_norm(residual, norm_gain, norm_shift):
    row_mean = lax.optimization_barrier(jnp.mean(residual, -1, keepdims=True))
    centred = residual - row_mean
    variance = lax.optimization_barrier(jnp.mean(centred * centred, -1, keepdims=True))
    return centred * lax.rsqrt(variance + EPSILON) * norm_gain + norm_shift

def split_heads(values):
    return values.reshape(values.shape[0], values.shape[1], HEADS, HEAD)

def attend(hidden, memory, key_mask, projection, out_weight, biases):
    queries = low(low_back(product(hidden, projection[0]) + biases[0]))
    key_rows = low(low_back(product(memory, projection[1])))
    value_rows = low(low_back(product(memory, projection[2]) + biases[1]))
    raw_scores = jnp.einsum('gqhe,gkhe->ghqk', split_heads(queries), split_heads(key_rows), precision=HIGHEST)
    scores = jnp.where(key_mask[:, None], low_back(raw_scores) * (1.0 / math.sqrt(HEAD)), NEGATIVE)
    row_max = lax.optimization_barrier(jnp.max(scores, -1, keepdims=True))
    exp_scores = jnp.exp(scores - row_max)
    attn_probs = low(exp_scores / lax.optimization_barrier(jnp.sum(exp_scores, -1, keepdims=True)))
    attended = jnp.einsum('ghqk,gkhe->gqhe', attn_probs, split_heads(value_rows), precision=HIGHEST)
    attended = low(low_back(attended.reshape(hidden.shape)))
    return low_back(product(attended, out_weight) + biases[2])

def feed(hidden, w_in, w_out, b_in, b_out):
    pre_active = low_back(product(hidden, w_in) + b_in)
    active = low(jax.nn.gelu(pre_active, approximate=True))
    return low_back(product(active, w_out) + b_out)

def forward(params, source_rows, target_rows, src_len, tgt_len):
    attn_proj, attn_out, attn_bias, norm_gain, norm_shift, ffn_in, ffn_out, ffn_bias_in, ffn_bias_out = params
    positions = jnp.arange(SLOTS, dtype=jnp.int32)
    src_keys = positions[None, None, :] < src_len[:, None, None]
    tgt_keys = (positions[None, None, :] < tgt_len[:, None, None]) & (positions[None, :, None] >= positions[None, None, :])
    hidden = low(source_rows)
    encoded = layer_norm(source_rows + attend(hidden, hidden, src_keys, attn_proj[0], attn_out[0], attn_bias[0]), norm_gain[0], norm_shift[0])
    memory = layer_norm(encoded + feed(low(encoded), ffn_in[0], ffn_out[0], ffn_bias_in[0], ffn_bias_out[0]), norm_gain[1], norm_shift[1])
    hidden = low(target_rows)
    decoded = layer_norm(target_rows + attend(hidden, hidden, tgt_keys, attn_proj[1], attn_out[1], attn_bias[1]), norm_gain[2], norm_shift[2])
    decoded = layer_norm(decoded + attend(low(decoded), low(memory), src_keys, attn_proj[2], attn_out[2], attn_bias[2]), norm_gain[3], norm_shift[3])
    decoded = layer_norm(decoded + feed(low(decoded), ffn_in[1], ffn_out[1], ffn_bias_in[1], ffn_bias_out[1]), norm_gain[4], norm_shift[4])
    return decoded

def reference(source, target, src_len, tgt_len, out_grad, attn_proj, attn_out, attn_bias, norm_gain, norm_shift, ffn_in, ffn_out, ffn_bias_in, ffn_bias_out):
    params = tuple((weight.astype(jnp.float32) for weight in (attn_proj, attn_out, attn_bias, norm_gain, norm_shift, ffn_in, ffn_out, ffn_bias_in, ffn_bias_out)))
    whole = MICRO * PAIRS
    group_size = math.gcd(whole, max(1, 4096 // SLOTS))
    groups = whole // group_size

    def regroup(values):
        return values.reshape((groups, group_size) + values.shape[2:])
    inputs = (regroup(source), regroup(target), regroup(src_len), regroup(tgt_len), regroup(out_grad))
    positions = jnp.arange(SLOTS, dtype=jnp.int32)

    def step(totals, item):
        src_rows, tgt_rows, src_lens, tgt_lens, cotangent = item

        def run(weights, src_float, tgt_float):
            return forward(weights, src_float, tgt_float, src_lens, tgt_lens)
        decoded, pull = jax.vjp(run, params, src_rows.astype(jnp.float32), tgt_rows.astype(jnp.float32))
        live = (positions[None, :] < tgt_lens[:, None]).astype(jnp.float32)
        grad_params, grad_src, grad_tgt = pull(cotangent.astype(jnp.float32) * live[:, :, None])
        totals = jax.tree.map(lambda first, second: first + second, totals, grad_params)
        return (totals, (decoded.astype(jnp.bfloat16), grad_src, grad_tgt))
    zeros = jax.tree.map(jnp.zeros_like, params)
    totals, (decoded, grad_src, grad_tgt) = lax.scan(step, zeros, inputs)
    shape = source.shape
    return (decoded.reshape(shape), grad_src.reshape(shape), grad_tgt.reshape(shape), totals[0], totals[1], totals[2], totals[3], totals[4], totals[5], totals[6], totals[7], totals[8])
```

```python
import functools

import jax
import jax.numpy as jnp
from jax import lax
from jax.experimental import pallas as pl
from jax.experimental.pallas import tpu as pltpu
from jax.sharding import Mesh
from jax.sharding import PartitionSpec as P

BF = jnp.bfloat16
F32 = jnp.float32
EPSILON = 1e-05
NEGATIVE = -1000000000.0
AXES = ("x", "y", "z", "c")
CHIPS = ("x", "y", "z")
ROWS = 256
PAIRS = 2
ALL = ROWS * PAIRS
D = 512
FF = 2048
VMEM = 61 * 1024 * 1024
ATTN_NORMS = (0, 2, 3)
FFN_NORMS = (1, 4)


def nn(a, b):
    return jnp.dot(a, b, preferred_element_type=F32)


def nt(a, b):
    return lax.dot_general(a, b, (((1,), (1,)), ((), ())), preferred_element_type=F32)


def tn(a, b):
    return lax.dot_general(a, b, (((0,), (0,)), ((), ())), preferred_element_type=F32)


def rows_of(b):
    return pl.ds(pl.multiple_of(b * ROWS, ROWS), ROWS)


def start_weights(gathered, stage, sems, pairs):
    copies = []
    for n, pair in enumerate(pairs):
        copy = pltpu.make_async_copy(
            gathered.at[:, pl.ds(512 * pair, 512)], stage.at[n], sems.at[n]
        )
        copy.start()
        copies.append(copy)
    return copies


def split_pair(stage, n, store_a, store_b):
    def body(i, carry):
        both = stage[n, pl.ds(pl.multiple_of(128 * i, 128), 128), :].astype(F32).reshape(8, 16, 512)
        rows = pl.ds(pl.multiple_of(64 * i, 64), 64)
        store_a(rows, both[:, :8].reshape(64, 512).astype(BF))
        store_b(rows, both[:, 8:].reshape(64, 512).astype(BF))
        return carry

    lax.fori_loop(0, 8, body, 0, unroll=2)


def prep_attn(stage, n, copies, dst):
    for half in range(2):
        copies[n + half].wait()

        def put(slot):
            def store(rows, value):
                dst[slot, rows, :] = value

            return store

        split_pair(stage, n + half, put(2 * half), put(2 * half + 1))


def prep_ffn(stage, n, copies, w_in, w_out):
    for half in range(2):
        copies[n + half].wait()

        def put(block):
            def store(rows, value):
                w_in[rows, 512 * block : 512 * block + 512] = value

            return store

        split_pair(stage, n + half, put(2 * half), put(2 * half + 1))
    copies[n + 2].wait()
    copies[n + 3].wait()

    def body(i, carry):
        span = pl.ds(pl.multiple_of(64 * i, 64), 64)
        first = stage[n + 2, span, :].astype(F32).reshape(4, 16, 512)
        second = stage[n + 3, span, :].astype(F32).reshape(4, 16, 512)
        whole = jnp.concatenate([first[:, :8], second[:, :8], first[:, 8:], second[:, 8:]], axis=1)
        w_out[pl.ds(pl.multiple_of(128 * i, 128), 128), :] = whole.reshape(128, 512).astype(BF)
        return carry

    lax.fori_loop(0, 16, body, 0, unroll=2)


def prep_vectors(block, vec, bin_vec):
    lanes = lax.broadcasted_iota(jnp.int32, (128, 512), 0)
    cols = lax.broadcasted_iota(jnp.int32, (128, 512), 1)
    owner = lax.broadcasted_iota(jnp.int32, (16, 8, 512), 0)
    place = lax.broadcasted_iota(jnp.int32, (16, 8, 512), 2)
    for g in range(3):
        pick = jnp.where(lanes == 4 * g + cols % 4, 1.0, 0.0).astype(BF)

        def body(i, total):
            piece = nn(block[pl.ds(pl.multiple_of(128 * i, 128), 128), :], pick).reshape(16, 8, 512)
            return total + jnp.sum(jnp.where(place // 4 == owner + 16 * i, piece, 0.0), axis=0)

        vec[8 * g : 8 * g + 8, :] = lax.fori_loop(0, 8, body, jnp.zeros((8, 512), F32))
    pick = jnp.where(lanes == 16 + cols % 16, 1.0, 0.0).astype(BF)
    for k in range(4):

        def body(i, total):
            piece = nn(block[pl.ds(pl.multiple_of(128 * i, 128), 128), :], pick).reshape(16, 8, 512)
            return total + jnp.sum(
                jnp.where((place + 512 * k) // 16 == owner + 16 * i, piece, 0.0), axis=0
            )

        bin_vec[:, 512 * k : 512 * k + 512] = lax.fori_loop(
            2 * k, 2 * k + 2, body, jnp.zeros((8, 512), F32)
        )


def norm_forward(r, gain, shift):
    c = r - jnp.mean(r, -1, keepdims=True)
    inv = lax.rsqrt(jnp.mean(c * c, -1, keepdims=True) + EPSILON)
    xhat = c * inv
    return xhat * gain + shift, xhat, inv


def norm_backward(g, xhat, inv, gain):
    d_gain = jnp.sum(g * xhat, 0, keepdims=True)
    d_shift = jnp.sum(g, 0, keepdims=True)
    gs = g * gain
    dr = inv * (gs - jnp.mean(gs, -1, keepdims=True) - xhat * jnp.mean(gs * xhat, -1, keepdims=True))
    return dr, d_gain, d_shift


def low_half():
    return lax.broadcasted_iota(jnp.int32, (1, 128), 1) < 64


def attn_forward(b, x, h, m, w, biases, masked, q_ref, k_ref, v_ref, o_ref, e_ref, r_ref):
    rows = rows_of(b)
    q_ref[rows, :] = ((nn(h, w[0]) + biases[0]) * 0.125).astype(BF)
    k_ref[rows, :] = nn(m, w[1]).astype(BF)
    v_ref[rows, :] = (nn(m, w[2]) + biases[1]).astype(BF)
    low = low_half()
    for j in range(4):
        cols = pl.ds(128 * j, 128)
        q = q_ref[rows, cols]
        k = k_ref[rows, cols]
        v = jnp.concatenate([v_ref[rows, cols], jnp.ones((ROWS, 128), BF)], axis=1)
        parts = []
        for half in range(2):
            mine = low if half == 0 else jnp.logical_not(low)
            s = nt(jnp.where(mine, q, jnp.zeros_like(q)), k) + masked
            e = jnp.exp(s - jnp.max(s, -1, keepdims=True)).astype(BF)
            e_ref[8 * b + 2 * j + half] = e
            parts.append(nn(e, v))
        total = jnp.where(low, parts[0][:, 128:], parts[1][:, 128:])
        r = 1.0 / total
        r_ref[rows, cols] = r
        o_ref[rows, cols] = (jnp.where(low, parts[0][:, :128], parts[1][:, :128]) * r).astype(BF)
    return x + (nn(o_ref[rows, :], w[3]) + biases[2])


def attn_backward(b, da, w, q_ref, k_ref, v_ref, o_ref, e_ref, r_ref, dq_ref, dk_ref, dv_ref):
    rows = rows_of(b)
    low = low_half()
    d_o = nt(da, w[3])
    for j in range(4):
        cols = pl.ds(128 * j, 128)
        q = q_ref[rows, cols]
        k = k_ref[rows, cols]
        v = v_ref[rows, cols]
        ds_o = (d_o[:, 128 * j : 128 * j + 128].astype(BF).astype(F32) * r_ref[rows, cols])
        prod = ds_o * o_ref[rows, cols].astype(F32)
        ds_o = ds_o.astype(BF)
        dqs, dks, dvs = [], [], []
        for half in range(2):
            mine = low if half == 0 else jnp.logical_not(low)
            delta = jnp.sum(jnp.where(mine, prod, 0.0), -1, keepdims=True)
            e = e_ref[8 * b + 2 * j + half]
            dp = nt(jnp.where(mine, ds_o, jnp.zeros_like(ds_o)), v)
            ds = (e.astype(F32) * (dp - delta)).astype(BF)
            dvs.append(tn(e, ds_o))
            dqs.append(nn(ds, k))
            dks.append(tn(ds, q))
        dq_ref[rows, cols] = (jnp.where(low, dqs[0], dqs[1]) * 0.125).astype(BF)
        dk_ref[rows, cols] = jnp.where(low, dks[0], dks[1]).astype(BF)
        dv_ref[rows, cols] = jnp.where(low, dvs[0], dvs[1]).astype(BF)


def gelu_both(u):
    c = 0.7978845608028654
    square = u * u
    t = jnp.tanh(c * u * (1.0 + 0.044715 * square))
    half = 0.5 * (1.0 + t)
    act = u * half
    slope = half + (0.5 * c) * u * (1.0 - t * t) * (1.0 + (3.0 * 0.044715) * square)
    return act, slope


def ffn_forward(b, x, h, w_in, w_out, b_in, b_out, act_ref, slope_ref):
    rows = rows_of(b)
    total = x + b_out
    for k in range(4):
        cols = pl.ds(512 * k, 512)
        act, slope = gelu_both(nn(h, w_in[:, cols]) + b_in[:, 512 * k : 512 * k + 512])
        act = act.astype(BF)
        act_ref[rows, cols] = act
        slope_ref[rows, cols] = slope.astype(BF)
        total = total + nn(act, w_out[cols, :])
    return total


def ffn_backward(b, dr, w_in, w_out, act_ref, slope_ref, du_ref, bin_grad):
    rows = rows_of(b)
    df = dr.astype(BF)
    dx = dr
    for k in range(4):
        cols = pl.ds(512 * k, 512)
        du = nt(df, w_out[cols, :]) * slope_ref[rows, cols].astype(F32)
        bin_grad[0:1, cols] += jnp.sum(du, 0, keepdims=True)
        du = du.astype(BF)
        du_ref[rows, cols] = du
        dx = dx + nt(du, w_in[:, cols])
    return dx


def ffn_weight_grads(h_ref, du_ref, act_ref, df_ref, g):
    def inner(j, carry):
        span = pl.ds(pl.multiple_of(128 * j, 128), 128)
        h = h_ref[:, span]
        for k in range(4):
            part = tn(h, du_ref[:, 512 * k : 512 * k + 512])
            g[k % 2, span, 512 * (k // 2) : 512 * (k // 2) + 512] = part.astype(BF)
        return carry

    lax.fori_loop(0, 4, inner, 0)

    def outer(j, carry):
        span = pl.ds(pl.multiple_of(128 * j, 128), 128)
        part = tn(act_ref[:, span], df_ref[...]).reshape(4, 4, 8, 512)
        rows = pl.ds(pl.multiple_of(32 * j, 32), 32)
        for k in range(4):
            at = 1024 + 512 * (k % 2)
            g[k // 2, rows, at : at + 512] = part[:, k].reshape(32, 512).astype(BF)
        return carry

    lax.fori_loop(0, 16, outer, 0)


def attn_weight_grads(h_ref, m_ref, o_ref, da_ref, dq_ref, dk_ref, dv_ref, g):
    def body(j, carry):
        span = pl.ds(pl.multiple_of(128 * j, 128), 128)
        g[0, span, 0:512] = tn(h_ref[:, span], dq_ref[...]).astype(BF)
        m = m_ref[:, span]
        g[1, span, 0:512] = tn(m, dk_ref[...]).astype(BF)
        g[0, span, 512:1024] = tn(m, dv_ref[...]).astype(BF)
        g[1, span, 512:1024] = tn(o_ref[:, span], da_ref[...]).astype(BF)
        return carry

    lax.fori_loop(0, 4, body, 0)


def send_out(g, core, mine, theirs, sems):
    other = pltpu.make_async_copy(g.at[1 - core], theirs, sems.at[0])
    own = pltpu.make_async_copy(g.at[core], mine, sems.at[1])
    other.start()
    own.start()
    return other, own


def forward_kernel(
    scalars, gathered, src, tgt, og,
    dec, grad_d2, vec, bin_vec,
    q0, k0, v0, o0, e0, r0, q1, k1, v1, o1, e1, r1, q2, k2, v2, o2, e2, r2,
    xh0, xh1, xh2, xh3, inv0, inv1, inv2, inv3,
    enc, mem, first, act0, slope0, vec_grad, bin_grad, mine, theirs,
    stage, block, w_attn, w_in, w_out, x32, second, act1, slope1, du, df, g, sems,
):
    copies = start_weights(gathered, stage, sems, list(range(14)))
    tail = pltpu.make_async_copy(gathered.at[:, pl.ds(7168, 128)], block, sems.at[14])
    tail.start()
    tail.wait()
    prep_vectors(block, vec, bin_vec)

    def bias(layer, j):
        return vec[3 * layer + j : 3 * layer + j + 1, :]

    def gain(n):
        return vec[9 + n : 10 + n, :]

    def shift(n):
        return vec[14 + n : 15 + n, :]

    def keys(length):
        place = lax.broadcasted_iota(jnp.int32, (1, ROWS), 1)
        return jnp.where(place < length, 0.0, NEGATIVE)

    def keep(b, r, n, xh, inv_ref):
        z, xhat, inv = norm_forward(r, gain(n), shift(n))
        xh[rows_of(b), :] = xhat.astype(BF)
        inv_ref[rows_of(b), :] = jnp.broadcast_to(inv, (ROWS, 128))
        return z

    def loop(body):
        def step(b, carry):
            body(b)
            return carry

        lax.fori_loop(0, PAIRS, step, 0)

    prep_attn(stage, 0, copies, w_attn)

    def enc_attn(b):
        rows = rows_of(b)
        h = src[rows, :]
        r = attn_forward(
            b, h.astype(F32), h, h, w_attn, [bias(0, j) for j in range(3)],
            keys(scalars[b]), q0, k0, v0, o0, e0, r0,
        )
        z = keep(b, r, 0, xh0, inv0)
        x32[rows, :] = z
        enc[rows, :] = z.astype(BF)

    loop(enc_attn)
    prep_ffn(stage, 6, copies, w_in, w_out)

    def enc_ffn(b):
        rows = rows_of(b)
        r = ffn_forward(
            b, x32[rows, :], enc[rows, :], w_in, w_out, bin_vec[0:1, :],
            vec[19:20, :], act0, slope0,
        )
        mem[rows, :] = keep(b, r, 1, xh1, inv1).astype(BF)

    loop(enc_ffn)
    prep_attn(stage, 2, copies, w_attn)

    def dec_attn(b):
        rows = rows_of(b)
        h = tgt[rows, :]
        at_q = lax.broadcasted_iota(jnp.int32, (ROWS, ROWS), 0)
        at_k = lax.broadcasted_iota(jnp.int32, (ROWS, ROWS), 1)
        live = jnp.logical_and(at_q >= at_k, at_k < scalars[2 + b])
        r = attn_forward(
            b, h.astype(F32), h, h, w_attn, [bias(1, j) for j in range(3)],
            jnp.where(live, 0.0, NEGATIVE), q1, k1, v1, o1, e1, r1,
        )
        z = keep(b, r, 2, xh2, inv2)
        x32[rows, :] = z
        first[rows, :] = z.astype(BF)

    loop(dec_attn)
    prep_attn(stage, 4, copies, w_attn)

    def cross(b):
        rows = rows_of(b)
        r = attn_forward(
            b, x32[rows, :], first[rows, :], mem[rows, :], w_attn,
            [bias(2, j) for j in range(3)], keys(scalars[b]), q2, k2, v2, o2, e2, r2,
        )
        z = keep(b, r, 3, xh3, inv3)
        x32[rows, :] = z
        second[rows, :] = z.astype(BF)

    loop(cross)
    prep_ffn(stage, 10, copies, w_in, w_out)
    vec_grad[...] = jnp.zeros_like(vec_grad)
    bin_grad[...] = jnp.zeros_like(bin_grad)

    def dec_ffn(b):
        rows = rows_of(b)
        r = ffn_forward(
            b, x32[rows, :], second[rows, :], w_in, w_out, bin_vec[1:2, :],
            vec[20:21, :], act1, slope1,
        )
        z, xhat, inv = norm_forward(r, gain(4), shift(4))
        dec[rows, :] = z.astype(BF)
        at = lax.broadcasted_iota(jnp.int32, (ROWS, 1), 0)
        gz = jnp.where(at < scalars[2 + b], og[rows, :].astype(F32), 0.0)
        dr, d_gain, d_shift = norm_backward(gz, xhat, inv, gain(4))
        vec_grad[0:1, :] += d_gain
        vec_grad[1:2, :] += d_shift
        vec_grad[2:3, :] += jnp.sum(dr, 0, keepdims=True)
        df[rows, :] = dr.astype(BF)
        grad_d2[rows, :] = ffn_backward(
            b, dr, w_in, w_out, act1, slope1, du, bin_grad
        )

    loop(dec_ffn)
    ffn_weight_grads(second, du, act1, df, g)
    for copy in send_out(g, scalars[4], mine, theirs, sems.at[pl.ds(15, 2)]):
        copy.wait()


def attn_back_kernel(
    layer, cross, scalars, gathered, vec, grad, xh, inv, q, k, v, o, e, r, h, m_or_none,
    dx, grad_mem, vec_grad, mine, theirs, stage, w, da, dq, dk, dv, g, sems,
):
    m = m_or_none if cross else h
    copies = start_weights(gathered, stage, sems, [2 * layer, 2 * layer + 1])
    prep_attn(stage, 0, copies, w)
    norm = ATTN_NORMS[layer]
    vec_grad[...] = jnp.zeros_like(vec_grad)

    def body(b, carry):
        rows = rows_of(b)
        dr, d_gain, d_shift = norm_backward(
            grad[rows, :], xh[rows, :].astype(F32), inv[rows, 0:1], vec[9 + norm : 10 + norm, :]
        )
        vec_grad[0:1, :] += d_gain
        vec_grad[1:2, :] += d_shift
        vec_grad[2:3, :] += jnp.sum(dr, 0, keepdims=True)
        low = dr.astype(BF)
        da[rows, :] = low
        attn_backward(b, low, w, q, k, v, o, e, r, dq, dk, dv)
        vec_grad[3:4, :] += jnp.sum(dq[rows, :].astype(F32), 0, keepdims=True)
        vec_grad[4:5, :] += jnp.sum(dv[rows, :].astype(F32), 0, keepdims=True)
        to_m = nt(dk[rows, :], w[1]) + nt(dv[rows, :], w[2])
        to_x = dr + nt(dq[rows, :], w[0])
        if cross:
            grad_mem[rows, :] = to_m
            dx[rows, :] = to_x
        else:
            dx[rows, :] = to_x + to_m
        return carry

    lax.fori_loop(0, PAIRS, body, 0)
    attn_weight_grads(h, m, o, da, dq, dk, dv, g)
    for copy in send_out(g, scalars[4], mine, theirs, sems.at[pl.ds(2, 2)]):
        copy.wait()


def ffn_back_kernel(
    scalars, gathered, vec, grad, xh, inv, act, slope, h,
    dx, vec_grad, bin_grad, mine, theirs, stage, w_in, w_out, du, df, g, sems,
):
    copies = start_weights(gathered, stage, sems, [6, 7, 8, 9])
    prep_ffn(stage, 0, copies, w_in, w_out)
    vec_grad[...] = jnp.zeros_like(vec_grad)
    bin_grad[...] = jnp.zeros_like(bin_grad)

    def body(b, carry):
        rows = rows_of(b)
        dr, d_gain, d_shift = norm_backward(
            grad[rows, :], xh[rows, :].astype(F32), inv[rows, 0:1], vec[10:11, :]
        )
        vec_grad[0:1, :] += d_gain
        vec_grad[1:2, :] += d_shift
        vec_grad[2:3, :] += jnp.sum(dr, 0, keepdims=True)
        df[rows, :] = dr.astype(BF)
        dx[rows, :] = ffn_backward(b, dr, w_in, w_out, act, slope, du, bin_grad)
        return carry

    lax.fori_loop(0, PAIRS, body, 0)
    ffn_weight_grads(h, du, act, df, g)
    for copy in send_out(g, scalars[4], mine, theirs, sems.at[pl.ds(4, 2)]):
        copy.wait()


def spec(space):
    return pl.BlockSpec(memory_space=space)


def call(kernel, name, inputs, outs, scratch, flops, spaces_out=None):
    return pl.pallas_call(
        kernel,
        name=name,
        in_specs=[spec(s) for _, s in inputs],
        out_specs=[spec(s) for _, _, s in outs],
        out_shape=[jax.ShapeDtypeStruct(shape, kind) for shape, kind, _ in outs],
        scratch_shapes=scratch,
        compiler_params=pltpu.CompilerParams(vmem_limit_bytes=VMEM),
        cost_estimate=pl.CostEstimate(flops=flops, bytes_accessed=10**7, transcendentals=0),
    )(*[a for a, _ in inputs])


V, H, S = pltpu.VMEM, pl.ANY, pltpu.SMEM
ROW = ((ALL, D), BF, V)
WIDE = ((ALL, FF), BF, V)
LINE = ((ALL, D), F32, V)
INV = ((ALL, 128), F32, V)
EXP = ((8 * PAIRS, ROWS, ROWS), BF, V)


def run_forward(scalars, gathered, src, tgt, og):
    heads = [ROW, ROW, ROW, ROW, EXP, LINE]
    outs = (
        [ROW, LINE, ((32, D), F32, V), ((8, FF), F32, V)]
        + heads * 3
        + [ROW] * 4
        + [INV] * 4
        + [ROW] * 3
        + [WIDE, WIDE, ((8, D), F32, V), ((8, FF), F32, V)]
        + [((D, FF), BF, H)] * 2
    )
    scratch = [
        V((14, 1024, 512), BF), V((1024, 128), BF), V((4, 512, 512), BF),
        V((D, FF), BF), V((FF, D), BF), V((ALL, D), F32), V((ALL, D), BF),
        V((ALL, FF), BF), V((ALL, FF), BF), V((ALL, FF), BF), V((ALL, D), BF),
        V((2, D, FF), BF), pltpu.SemaphoreType.DMA((17,)),
    ]
    return call(
        forward_kernel, "forward",
        [(scalars, S), (gathered, H), (src, V), (tgt, V), (og, V)], outs, scratch, 3 * 10**10,
    )


def run_attn_back(layer, scalars, gathered, vec, grad, xh, inv, heads, h, m):
    cross = m is not None
    inputs = [(scalars, S), (gathered, H), (vec, V), (grad, V), (xh, V), (inv, V)]
    inputs += [(a, V) for a in heads] + [(h, V)] + ([(m, V)] if cross else [])
    outs = [LINE] + ([LINE] if cross else []) + [((8, D), F32, V)] + [((D, 1024), BF, H)] * 2
    scratch = [
        V((2, 1024, 512), BF), V((4, 512, 512), BF), V((ALL, D), BF), V((ALL, D), BF),
        V((ALL, D), BF), V((ALL, D), BF), V((2, D, 1024), BF), pltpu.SemaphoreType.DMA((4,)),
    ]

    def kernel(*refs):
        refs = list(refs)
        if not cross:
            refs.insert(13, None)
            refs.insert(15, None)
        attn_back_kernel(layer, cross, *refs)

    return call(kernel, f"attn_back_{layer}", inputs, outs, scratch, 10**10)


def run_ffn_back(scalars, gathered, vec, grad, xh, inv, act, slope, h):
    inputs = [(scalars, S), (gathered, H)]
    inputs += [(a, V) for a in (vec, grad, xh, inv, act, slope, h)]
    outs = [LINE, ((8, D), F32, V), ((8, FF), F32, V)] + [((D, FF), BF, H)] * 2
    scratch = [
        V((4, 1024, 512), BF), V((D, FF), BF), V((FF, D), BF), V((ALL, FF), BF),
        V((ALL, D), BF), V((2, D, FF), BF), pltpu.SemaphoreType.DMA((6,)),
    ]
    return call(ffn_back_kernel, "ffn_back", inputs, outs, scratch, 10**10)


def pack_shard(c, attn_proj, attn_out, attn_bias, norm_gain, norm_shift, ffn_in, ffn_out, b_in, b_out):
    attn = jnp.concatenate([attn_proj, attn_out[:, None]], axis=1).reshape(12, 4, 512)
    wide = ffn_in.reshape(2, 4, 4, 512).transpose(0, 2, 1, 3).reshape(8, 4, 512)
    both = lax.all_gather(jnp.concatenate([attn, wide]), "c", axis=1, tiled=True)
    half = lax.dynamic_index_in_dim(both.reshape(10, 2, 8, 512), c, 1, False)
    tall = ffn_out.reshape(2, 2, 8, 512)
    blocks = jnp.concatenate([half[:8], tall[0], half[8:], tall[1]])
    vec = jnp.concatenate([attn_bias.reshape(9, 4), norm_gain, norm_shift, b_out])
    vec = jnp.pad(vec, ((0, 3), (0, 0))).reshape(3, 8, 4).transpose(1, 0, 2).reshape(8, 12)
    line = jnp.concatenate(
        [jnp.pad(vec, ((0, 0), (0, 4))), jnp.pad(b_in, ((0, 6), (0, 0)))], axis=1
    )
    line = jnp.pad(line, ((0, 0), (0, 96)))
    return jnp.concatenate([blocks.transpose(1, 0, 2).reshape(8, 7168), line], axis=1)


def vector_block(attn, ffn):
    rows = [attn[i][r] for i in range(3) for r in (3, 4, 2)]
    order = (attn[0], ffn[0][0], attn[1], attn[2], ffn[1][0])
    rows += [a[0] for a in order] + [a[1] for a in order] + [f[0][2] for f in ffn]
    vec = jnp.pad(jnp.stack(rows), ((0, 3), (0, 0)))
    vec = vec.reshape(3, 8, 64, 8).transpose(2, 1, 0, 3).reshape(64, 8, 24)
    wide = jnp.stack([f[1][0] for f in ffn]).reshape(2, 64, 32).transpose(1, 0, 2)
    wide = jnp.pad(wide, ((0, 0), (0, 6), (0, 72)))
    return jnp.concatenate([vec, wide], axis=2).reshape(512, 128).astype(BF)


def swap(a):
    return lax.ppermute(a, "c", [(0, 1), (1, 0)])


def pair_sum(mine, theirs):
    return (mine.astype(F32) + swap(theirs).astype(F32)).astype(BF)


def chip_sum(parts):
    whole = parts[0] if len(parts) == 1 else jnp.concatenate(parts, axis=1)
    whole = lax.all_to_all(whole.reshape(64, 8, -1), CHIPS, 0, 0, tiled=True)
    return jnp.sum(whole.astype(F32), axis=0)


def per_device(source, target, src_len, tgt_len, out_grad, *weights):
    c = lax.axis_index("c")
    gathered = lax.all_gather(pack_shard(c, *weights), AXES, axis=0, tiled=True)
    scalars = jnp.concatenate(
        [src_len.reshape(2), tgt_len.reshape(2), c.astype(jnp.int32)[None], jnp.zeros(3, jnp.int32)]
    )
    src, tgt, og = (a.reshape(ALL, D) for a in (source, target, out_grad))
    outs = run_forward(scalars, gathered, src, tgt, og)
    dec, grad, vec, bin_vec = outs[:4]
    heads = [outs[4 + 6 * i : 10 + 6 * i] for i in range(3)]
    xh, inv = outs[22:26], outs[26:30]
    enc, mem, first, act0, slope0, f1_vec, f1_bin, f1_mine, f1_theirs = outs[30:]
    f1 = pair_sum(f1_mine, f1_theirs)
    sum_f1 = chip_sum([f1])
    d1, grad_mem, a2_vec, a2_mine, a2_theirs = run_attn_back(
        2, scalars, gathered, vec, grad, xh[3], inv[3], heads[2], first, mem
    )
    a2 = pair_sum(a2_mine, a2_theirs)
    d_tgt, a1_vec, a1_mine, a1_theirs = run_attn_back(
        1, scalars, gathered, vec, d1, xh[2], inv[2], heads[1], tgt, None
    )
    a1 = pair_sum(a1_mine, a1_theirs)
    sum_a21 = chip_sum([a2, a1])
    d_enc, f0_vec, f0_bin, f0_mine, f0_theirs = run_ffn_back(
        scalars, gathered, vec, grad_mem, xh[1], inv[1], act0, slope0, enc
    )
    sum_f0 = chip_sum([pair_sum(f0_mine, f0_theirs)])
    d_src, a0_vec, a0_mine, a0_theirs = run_attn_back(
        0, scalars, gathered, vec, d_enc, xh[0], inv[0], heads[0], src, None
    )
    line = vector_block([a0_vec, a1_vec, a2_vec], [(f0_vec, f0_bin), (f1_vec, f1_bin)])
    sum_a0 = chip_sum([pair_sum(a0_mine, a0_theirs), pair_sum(line, line)])

    cut = sum_a0[:, 1024:]
    vecs = cut[:, :24].reshape(8, 3, 2, 4).transpose(1, 0, 2, 3).reshape(24, 2, 4)
    vecs = lax.dynamic_index_in_dim(vecs, c, 1, False)
    g_bin = lax.dynamic_index_in_dim(cut[:2, 24:56].reshape(2, 2, 16), c, 1, False)
    whole = jnp.concatenate([sum_a0[:, :1024], sum_a21[:, 1024:], sum_a21[:, :1024], sum_f0, sum_f1], axis=1)
    attn = whole[:, :3072].reshape(2, 4, 6, 512)
    wide = whole[:, 3072:].reshape(8, 2, 4, 512)
    rows = jnp.concatenate([attn, wide[:, :, :2].reshape(2, 4, 4, 512)], axis=2)
    keep = lax.dynamic_index_in_dim(rows, c, 0, False)
    got = swap(lax.dynamic_index_in_dim(rows, 1 - c, 0, False))
    first_half = jnp.where(c == 0, keep, got)
    second_half = jnp.where(c == 0, got, keep)
    a = first_half[:, :6].reshape(4, 3, 2, 512)
    b = second_half[:, :6].reshape(4, 3, 2, 512)
    g_proj = jnp.stack([a[:, :, 0], b[:, :, 0], a[:, :, 1]], axis=0).transpose(2, 0, 1, 3)
    g_out = b[:, :, 1].transpose(1, 0, 2)
    ia = first_half[:, 6:].reshape(4, 2, 2, 512)
    ib = second_half[:, 6:].reshape(4, 2, 2, 512)
    g_in = jnp.stack([ia, ib], axis=3).transpose(1, 0, 2, 3, 4).reshape(2, 4, 2048)
    g_wout = wide[:, :, 2:].transpose(1, 2, 0, 3).reshape(2, 16, 512)
    shape = source.shape
    return (
        dec.reshape(shape), d_src.reshape(shape), d_tgt.reshape(shape),
        g_proj, g_out, vecs[:9].reshape(3, 3, 4), vecs[9:14], vecs[14:19],
        g_in, g_wout, g_bin, vecs[19:21],
    )


def solution(mesh):
    mesh = Mesh(mesh.devices.reshape(4, 4, 4, 2), AXES)
    rows = P(None, AXES, None, None)
    lens = P(None, AXES)
    weights = (
        P(None, None, AXES, None), P(None, AXES, None), P(None, None, AXES), P(None, AXES),
        P(None, AXES), P(None, AXES, None), P(None, AXES, None), P(None, AXES), P(None, AXES),
    )
    return jax.shard_map(
        per_device,
        mesh=mesh,
        in_specs=(rows, rows, lens, lens, rows) + weights,
        out_specs=(rows, rows, rows) + weights,
        check_vma=False,
    )
```

```python
import functools

import jax
import jax.numpy as jnp
from jax import lax
from jax.experimental import pallas as pl
from jax.experimental.pallas import tpu as pltpu
from jax.sharding import Mesh
from jax.sharding import PartitionSpec as P

BF = jnp.bfloat16
F32 = jnp.float32
EPSILON = 1e-05
NEGATIVE = -1000000000.0
AXES = ("x", "y", "z", "c")
CHIPS = ("x", "y", "z")
ROWS = 256
PAIRS = 2
ALL = ROWS * PAIRS
D = 512
FF = 2048
VMEM = 61 * 1024 * 1024
ATTN_NORMS = (0, 2, 3)
FFN_NORMS = (1, 4)


def nn(a, b):
    return jnp.dot(a, b, preferred_element_type=F32)


def nt(a, b):
    return lax.dot_general(a, b, (((1,), (1,)), ((), ())), preferred_element_type=F32)


def tn(a, b):
    return lax.dot_general(a, b, (((0,), (0,)), ((), ())), preferred_element_type=F32)


def rows_of(b):
    return pl.ds(pl.multiple_of(b * ROWS, ROWS), ROWS)


def split_pair(stage, n, store_a, store_b):
    def body(i, carry):
        both = stage[n, pl.ds(pl.multiple_of(128 * i, 128), 128), :].astype(F32).reshape(8, 16, 512)
        rows = pl.ds(pl.multiple_of(64 * i, 64), 64)
        store_a(rows, both[:, :8].reshape(64, 512).astype(BF))
        store_b(rows, both[:, 8:].reshape(64, 512).astype(BF))
        return carry

    lax.fori_loop(0, 8, body, 0, unroll=2)


def prep_attn(stage, n, copies, dst):
    for half in range(2):
        copies[n + half].wait()

        def put(slot):
            def store(rows, value):
                dst[slot, rows, :] = value

            return store

        split_pair(stage, n + half, put(2 * half), put(2 * half + 1))


def prep_ffn(stage, n, copies, w_in, w_out):
    for half in range(2):
        copies[n + half].wait()

        def put(block):
            def store(rows, value):
                w_in[rows, 512 * block : 512 * block + 512] = value

            return store

        split_pair(stage, n + half, put(2 * half), put(2 * half + 1))
    copies[n + 2].wait()
    copies[n + 3].wait()

    def body(i, carry):
        span = pl.ds(pl.multiple_of(64 * i, 64), 64)
        first = stage[n + 2, span, :].astype(F32).reshape(4, 16, 512)
        second = stage[n + 3, span, :].astype(F32).reshape(4, 16, 512)
        whole = jnp.concatenate([first[:, :8], second[:, :8], first[:, 8:], second[:, 8:]], axis=1)
        w_out[pl.ds(pl.multiple_of(128 * i, 128), 128), :] = whole.reshape(128, 512).astype(BF)
        return carry

    lax.fori_loop(0, 16, body, 0, unroll=2)


def prep_vectors(block, vec, bin_vec):
    device = lax.broadcasted_iota(jnp.int32, (128, 1024), 0)
    row = lax.broadcasted_iota(jnp.int32, (128, 1024), 1)
    lines = nn(jnp.where(row == 8 * device, 1.0, 0.0).astype(BF), block[...]).astype(BF)
    device = lax.broadcasted_iota(jnp.int32, (128, 512), 0)
    place = lax.broadcasted_iota(jnp.int32, (128, 512), 1)
    total = jnp.zeros((32, 512), F32)
    turned = jnp.transpose(lines.astype(F32)).astype(BF)
    for e in range(4):
        spread = jnp.where(place == 4 * device + e, 1.0, 0.0).astype(BF)
        total = total + nn(turned[32 * e : 32 * e + 32], spread)
    vec[...] = total
    for k in range(4):
        near = jnp.where((place + 512 * k) // 16 == device, 1.0, 0.0)
        for j in range(2):
            pick = jnp.where(device == 32 * (place % 4) + 24 + 4 * j + (place % 16) // 4, 1.0, 0.0)
            found = nn(lines, pick.astype(BF)) * near
            bin_vec[j : j + 1, 512 * k : 512 * k + 512] = jnp.sum(found, 0, keepdims=True)


def norm_forward(r, gain, shift):
    c = r - jnp.mean(r, -1, keepdims=True)
    inv = lax.rsqrt(jnp.mean(c * c, -1, keepdims=True) + EPSILON)
    xhat = c * inv
    return xhat * gain + shift, xhat, inv


def norm_backward(g, xhat, inv, gain):
    d_gain = jnp.sum(g * xhat, 0, keepdims=True)
    d_shift = jnp.sum(g, 0, keepdims=True)
    gs = g * gain
    dr = inv * (gs - jnp.mean(gs, -1, keepdims=True) - xhat * jnp.mean(gs * xhat, -1, keepdims=True))
    return dr, d_gain, d_shift


def low_half():
    return lax.broadcasted_iota(jnp.int32, (1, 128), 1) < 64


def blocks(size, total, body):
    def step(i, carry):
        body(pl.ds(pl.multiple_of(i * size, size), size))
        return carry

    lax.fori_loop(0, total // size, step, 0)


def attn_forward(x, h, m, w, biases, mask_of, q_ref, k_ref, v_ref, o_ref, e_ref, r_ref, after):
    for n in range(2):
        cols = pl.ds(256 * n, 256)
        part = slice(256 * n, 256 * n + 256)
        q_ref[:, cols] = ((nn(h[...], w[0, :, cols]) + biases[0][:, part]) * 0.125).astype(BF)
        k_ref[:, cols] = nn(m[...], w[1, :, cols]).astype(BF)
        v_ref[:, cols] = (nn(m[...], w[2, :, cols]) + biases[1][:, part]).astype(BF)
    low = low_half()

    def pair(b, carry):
        rows = rows_of(b)
        masked = mask_of(b)
        for j in range(4):
            cols = pl.ds(128 * j, 128)
            q = q_ref[rows, cols]
            k = k_ref[rows, cols]
            v = jnp.concatenate([v_ref[rows, cols], jnp.ones((ROWS, 128), BF)], axis=1)
            parts = []
            for half in range(2):
                mine = low if half == 0 else jnp.logical_not(low)
                s = nt(jnp.where(mine, q, jnp.zeros_like(q)), k) + masked
                e = jnp.exp(s - jnp.max(s, -1, keepdims=True)).astype(BF)
                e_ref[8 * b + 2 * j + half] = e
                parts.append(nn(e, v))
            r = 1.0 / jnp.where(low, parts[0][:, 128:], parts[1][:, 128:])
            r_ref[rows, cols] = r.astype(BF)
            o = jnp.where(low, parts[0][:, :128], parts[1][:, :128]) * r
            o_ref[rows, cols] = o.astype(BF)
        after(rows, b, x(rows) + (nn(o_ref[rows, :], w[3]) + biases[2]))
        return carry

    lax.fori_loop(0, PAIRS, pair, 0)


def attn_backward(b, d_o, q_ref, k_ref, v_ref, o_ref, e_ref, r_ref, dq_ref, dk_ref, dv_ref):
    rows = rows_of(b)
    low = low_half()
    for j in range(4):
        cols = pl.ds(128 * j, 128)
        q = q_ref[rows, cols]
        k = k_ref[rows, cols]
        v = v_ref[rows, cols]
        ds_o = d_o[rows, cols].astype(F32) * r_ref[rows, cols].astype(F32)
        prod = ds_o * o_ref[rows, cols].astype(F32)
        ds_o = ds_o.astype(BF)
        dqs, dks, dvs = [], [], []
        for half in range(2):
            mine = low if half == 0 else jnp.logical_not(low)
            delta = jnp.sum(jnp.where(mine, prod, 0.0), -1, keepdims=True)
            e = e_ref[8 * b + 2 * j + half]
            dp = nt(jnp.where(mine, ds_o, jnp.zeros_like(ds_o)), v)
            ds = (e.astype(F32) * (dp - delta)).astype(BF)
            dvs.append(tn(e, ds_o))
            dqs.append(nn(ds, k))
            dks.append(tn(ds, q))
        dq_ref[rows, cols] = (jnp.where(low, dqs[0], dqs[1]) * 0.125).astype(BF)
        dk_ref[rows, cols] = jnp.where(low, dks[0], dks[1]).astype(BF)
        dv_ref[rows, cols] = jnp.where(low, dvs[0], dvs[1]).astype(BF)


def gelu_both(u):
    c = 0.7978845608028654
    square = u * u
    t = jnp.tanh(c * u * (1.0 + 0.044715 * square))
    half = 0.5 * (1.0 + t)
    act = u * half
    slope = half + (0.5 * c) * u * (1.0 - t * t) * (1.0 + (3.0 * 0.044715) * square)
    return act, slope


def ffn_forward(x, h, w_in, w_out, b_in, b_out, act_ref, slope_ref, after):
    def hidden(cols):
        act, slope = gelu_both(nn(h[...], w_in[:, cols]) + b_in[:, cols])
        act_ref[:, cols] = act.astype(BF)
        slope_ref[:, cols] = slope.astype(BF)

    blocks(256, FF, hidden)

    def pair(b, carry):
        rows = rows_of(b)
        after(rows, b, x(rows) + (nn(act_ref[rows, :], w_out[...]) + b_out))
        return carry

    lax.fori_loop(0, PAIRS, pair, 0)


def ffn_backward(dr, df, w_in, w_out, slope_ref, du_ref, bin_grad, dx):
    def hidden(cols):
        du = nt(df[...], w_out[cols, :]) * slope_ref[:, cols].astype(F32)
        bin_grad[0:1, cols] = jnp.sum(du, 0, keepdims=True)
        du_ref[:, cols] = du.astype(BF)

    blocks(256, FF, hidden)

    def pair(b, carry):
        rows = rows_of(b)
        dx[rows, :] = dr[rows, :] + nt(du_ref[rows, :], w_in[...])
        return carry

    lax.fori_loop(0, PAIRS, pair, 0)


def turn(src, cols, dst):
    dst[...] = jnp.transpose(src[:, cols])


def ffn_weight_grads(h_ref, du_ref, act_ref, df_ref, g, turned, base=0):
    turn(h_ref, slice(None), turned)

    def inner(k, carry):
        for n in range(2):
            part = nn(turned[...], du_ref[:, pl.ds(pl.multiple_of(512 * k + 256 * n, 256), 256)])
            at = pl.ds(pl.multiple_of(base + 512 * (k // 2) + 256 * n, 256), 256)
            g[k % 2, :, at] = part.astype(BF)
        return carry

    lax.fori_loop(0, 4, inner, 0)

    def outer(j, carry):
        turn(act_ref, pl.ds(pl.multiple_of(512 * j, 512), 512), turned)
        rows = pl.ds(pl.multiple_of(128 * j, 128), 128)
        for n in range(2):
            part = nn(turned[...], df_ref[:, 256 * n : 256 * n + 256]).reshape(16, 4, 8, 256)
            for k in range(4):
                at = base + 1024 + 512 * (k % 2) + 256 * n
                g[k // 2, rows, at : at + 256] = part[:, k].reshape(128, 256).astype(BF)
        return carry

    lax.fori_loop(0, 4, outer, 0)


def attn_weight_grads(h_ref, m_ref, o_ref, da_ref, dq_ref, dk_ref, dv_ref, g, turned, base=0):
    def product(side, at, right):
        for n in range(2):
            cols = slice(256 * n, 256 * n + 256)
            start = base + at + 256 * n
            g[side, :, start : start + 256] = nn(turned[...], right[:, cols]).astype(BF)

    turn(h_ref, slice(None), turned)
    product(0, 0, dq_ref)
    if m_ref is not h_ref:
        turn(m_ref, slice(None), turned)
    product(1, 0, dk_ref)
    product(0, 512, dv_ref)
    turn(o_ref, slice(None), turned)
    product(1, 512, da_ref)


def send_out(g, core, mine, theirs, sems):
    other = pltpu.make_async_copy(g.at[1 - core], theirs, sems.at[0])
    own = pltpu.make_async_copy(g.at[core], mine, sems.at[1])
    other.start()
    own.start()
    return other, own


class Moves:
    def __init__(self, sems):
        self.sems, self.used, self.open = sems, 0, []

    def start(self, src, dst):
        copy = pltpu.make_async_copy(src, dst, self.sems.at[self.used])
        self.used += 1
        copy.start()
        return copy

    def send(self, src, dst):
        self.open.append(self.start(src, dst))

    def finish(self):
        for copy in self.open:
            copy.wait()


def fetch_pair(moves, gathered, stage, pair, slot):
    return moves.start(gathered.at[:, pl.ds(512 * pair, 512)], stage.at[slot])


def forward_kernel(scalars, gathered, src_h, tgt_h, og_h, *refs):
    (
        dec_h, grad_h,
        q0h, k0h, v0h, o0h, e0h, r0h, q1h, k1h, v1h, o1h, e1h, r1h, q2h, k2h, v2h, o2h, e2h, r2h,
        xh0h, xh1h, xh2h, xh3h, inv0h, inv1h, inv2h, inv3h,
        enc_h, mem_h, first_h, act0h, slope0h, mine, theirs, vec, vec_grad, bin_grad,
        dec, grad_d2,
        q0, k0, v0, o0, e0, r0, q1, k1, v1, o1, e1, r1, q2, k2, v2, o2, e2, r2,
        xh0, xh1, xh2, xh3, inv0, inv1, inv2, inv3,
        enc, mem, first, act0, slope0,
        src, tgt, og, bin_vec, stage, block, w_attn, w_in, w_out, x32, second,
        act1, slope1, df, g, turned, sems,
    ) = refs
    moves = Moves(sems)
    tail = moves.start(gathered.at[:, pl.ds(7168, 128)], block)
    src_in = moves.start(src_h, src)
    pairs = {n: fetch_pair(moves, gathered, stage, n, n) for n in (0, 1)}
    for n in range(4):
        pairs[6 + n] = fetch_pair(moves, gathered, stage, 6 + n, 2 + n)
    tgt_in = moves.start(tgt_h, tgt)
    for n in (2, 3):
        pairs[n] = fetch_pair(moves, gathered, stage, n, 4 + n)
    og_in = moves.start(og_h, og)
    tail.wait()
    prep_vectors(block, vec, bin_vec)

    def bias(layer):
        return [vec[3 * layer + j : 3 * layer + j + 1, :] for j in range(3)]

    def gain(n):
        return vec[9 + n : 10 + n, :]

    def shift(n):
        return vec[14 + n : 15 + n, :]

    def source_keys(b):
        place = lax.broadcasted_iota(jnp.int32, (1, ROWS), 1)
        return jnp.where(place < scalars[b], 0.0, NEGATIVE)

    def target_keys(b):
        at_q = lax.broadcasted_iota(jnp.int32, (ROWS, ROWS), 0)
        at_k = lax.broadcasted_iota(jnp.int32, (ROWS, ROWS), 1)
        live = jnp.logical_and(at_q >= at_k, at_k < scalars[2 + b])
        return jnp.where(live, 0.0, NEGATIVE)

    def keeper(n, xh, inv_ref, low, wide):
        def after(rows, b, r):
            z, xhat, inv = norm_forward(r, gain(n), shift(n))
            xh[rows, :] = xhat.astype(BF)
            inv_ref[rows, :] = jnp.broadcast_to(inv, (ROWS, 128))
            low[rows, :] = z.astype(BF)
            if wide is not None:
                wide[rows, :] = z

        return after

    def from_low(ref):
        return lambda rows: ref[rows, :].astype(F32)

    def from_x32(rows):
        return x32[rows, :]

    src_in.wait()
    prep_attn(stage, 0, [pairs[0], pairs[1]], w_attn)
    pairs[4] = fetch_pair(moves, gathered, stage, 4, 0)
    pairs[5] = fetch_pair(moves, gathered, stage, 5, 1)
    attn_forward(
        from_low(src), src, src, w_attn, bias(0), source_keys, q0, k0, v0, o0, e0, r0,
        keeper(0, xh0, inv0, enc, x32),
    )
    for a, b in ((q0, q0h), (k0, k0h), (v0, v0h), (o0, o0h), (e0, e0h), (r0, r0h),
                 (xh0, xh0h), (inv0, inv0h), (enc, enc_h)):
        moves.send(a, b)
    prep_ffn(stage, 2, [None, None] + [pairs[6 + n] for n in range(4)], w_in, w_out)
    for n in range(4):
        pairs[10 + n] = fetch_pair(moves, gathered, stage, 10 + n, 2 + n)
    ffn_forward(
        from_x32, enc, w_in, w_out, bin_vec.at[0:1], vec[19:20, :], act0, slope0,
        keeper(1, xh1, inv1, mem, None),
    )
    for a, b in ((xh1, xh1h), (inv1, inv1h), (mem, mem_h), (act0, act0h), (slope0, slope0h)):
        moves.send(a, b)
    tgt_in.wait()
    prep_attn(stage, 6, [None] * 6 + [pairs[2], pairs[3]], w_attn)
    attn_forward(
        from_low(tgt), tgt, tgt, w_attn, bias(1), target_keys, q1, k1, v1, o1, e1, r1,
        keeper(2, xh2, inv2, first, x32),
    )
    for a, b in ((q1, q1h), (k1, k1h), (v1, v1h), (o1, o1h), (e1, e1h), (r1, r1h),
                 (xh2, xh2h), (inv2, inv2h), (first, first_h)):
        moves.send(a, b)
    prep_attn(stage, 0, [pairs[4], pairs[5]], w_attn)
    attn_forward(
        from_x32, first, mem, w_attn, bias(2), source_keys, q2, k2, v2, o2, e2, r2,
        keeper(3, xh3, inv3, second, x32),
    )
    for a, b in ((q2, q2h), (k2, k2h), (v2, v2h), (o2, o2h), (e2, e2h), (r2, r2h),
                 (xh3, xh3h), (inv3, inv3h)):
        moves.send(a, b)
    prep_ffn(stage, 2, [None, None] + [pairs[10 + n] for n in range(4)], w_in, w_out)
    vec_grad[...] = jnp.zeros_like(vec_grad)
    bin_grad[...] = jnp.zeros_like(bin_grad)
    og_in.wait()

    def last(rows, b, r):
        z, xhat, inv = norm_forward(r, gain(4), shift(4))
        dec[rows, :] = z.astype(BF)
        at = lax.broadcasted_iota(jnp.int32, (ROWS, 1), 0)
        gz = jnp.where(at < scalars[2 + b], og[rows, :].astype(F32), 0.0)
        dr, d_gain, d_shift = norm_backward(gz, xhat, inv, gain(4))
        vec_grad[0:1, :] += d_gain
        vec_grad[1:2, :] += d_shift
        vec_grad[2:3, :] += jnp.sum(dr, 0, keepdims=True)
        df[rows, :] = dr.astype(BF)
        x32[rows, :] = dr

    ffn_forward(
        from_x32, second, w_in, w_out, bin_vec.at[1:2], vec[20:21, :], act1, slope1, last
    )
    moves.send(dec, dec_h)
    ffn_backward(x32, df, w_in, w_out, slope1, slope1, bin_grad, grad_d2)
    moves.send(grad_d2, grad_h)
    ffn_weight_grads(second, slope1, act1, df, g, turned)
    core = scalars[4]
    moves.send(g.at[1 - core], theirs)
    moves.send(g.at[core], mine)
    moves.finish()


def norm_rows(vec_grad, grad, xh, inv, gain, low, wide):
    vec_grad[...] = jnp.zeros_like(vec_grad)

    def pair(b, carry):
        rows = rows_of(b)
        dr, d_gain, d_shift = norm_backward(
            grad[rows, :], xh[rows, :].astype(F32), inv[rows, 0:1], gain
        )
        vec_grad[0:1, :] += d_gain
        vec_grad[1:2, :] += d_shift
        vec_grad[2:3, :] += jnp.sum(dr, 0, keepdims=True)
        low[rows, :] = dr.astype(BF)
        wide[rows, :] = dr
        return carry

    lax.fori_loop(0, PAIRS, pair, 0)


def load_attn(moves, far_refs, near_refs):
    far_refs, near_refs = list(far_refs), list(near_refs)
    first = [moves.start(a, b) for a, b in zip(far_refs[:2], near_refs[:2])]
    heads = [moves.start(a, b) for a, b in zip(far_refs[2:8], near_refs[2:8])]
    rows = [moves.start(a, b) for a, b in zip(far_refs[8:], near_refs[8:])]
    return first, heads, rows


def attn_back(grad, data, weights, w, gain, temps, dx, grad_mem, g, base, vec_grad, copies):
    xh, inv, r, o, q, v, k, e, h = data[:9]
    m = data[9] if len(data) > 9 else h
    da, d_o, dq, dk, dv, turned = temps
    first, heads, rows_in = copies
    for copy in first:
        copy.wait()
    norm_rows(vec_grad, grad, xh, inv, gain, da, dx)
    weights()
    for n in range(2):
        cols = pl.ds(256 * n, 256)
        d_o[:, cols] = nt(da[...], w[3, cols, :]).astype(BF)
    for copy in heads:
        copy.wait()

    def body(b, carry):
        attn_backward(b, d_o, q, k, v, o, e, r, dq, dk, dv)
        rows = rows_of(b)
        vec_grad[3:4, :] += jnp.sum(dq[rows, :].astype(F32), 0, keepdims=True)
        vec_grad[4:5, :] += jnp.sum(dv[rows, :].astype(F32), 0, keepdims=True)
        to_m = nt(dk[rows, :], w[1]) + nt(dv[rows, :], w[2])
        to_x = dx[rows, :] + nt(dq[rows, :], w[0])
        if grad_mem is not None:
            grad_mem[rows, :] = to_m
            dx[rows, :] = to_x
        else:
            dx[rows, :] = to_x + to_m
        return carry

    lax.fori_loop(0, PAIRS, body, 0)
    for copy in rows_in:
        copy.wait()
    attn_weight_grads(h, m, o, da, dq, dk, dv, g, turned, base)


def send_gradients(moves, g, core, mine, theirs):
    moves.send(g.at[1 - core], theirs)
    moves.send(g.at[core], mine)


def middle_kernel(scalars, gathered, vec, grad_h, *refs):
    far_attn, far_ffn = refs[:10], refs[10:15]
    d1_h, denc_h, mine, theirs, attn_vec, ffn_vec, bin_grad = refs[15:22]
    near_attn, near_ffn = refs[22:32], refs[32:37]
    grad, d1, denc, stage, w, w_in, w_out, da, d_o, dq, dk, dv, g, turned, sems = refs[37:]
    moves = Moves(sems)
    grad_in = moves.start(grad_h, grad)
    pairs = [fetch_pair(moves, gathered, stage, 4 + n, n) for n in range(2)]
    copies = load_attn(moves, far_attn, near_attn)
    pairs += [fetch_pair(moves, gathered, stage, 6 + n, 2 + n) for n in range(4)]
    xh1, inv1, slope, act, enc = near_ffn
    ffn_in = [moves.start(a, b) for a, b in zip(far_ffn, near_ffn)]
    bin_grad[...] = jnp.zeros_like(bin_grad)
    grad_in.wait()
    attn_back(
        grad, near_attn, lambda: prep_attn(stage, 0, pairs, w), w, vec[12:13, :],
        (da, d_o, dq, dk, dv, turned), d1, grad, g, 0, attn_vec, copies,
    )
    moves.send(d1, d1_h)
    for copy in ffn_in:
        copy.wait()
    norm_rows(ffn_vec, grad, xh1, inv1, vec[10:11, :], da, grad)
    prep_ffn(stage, 2, [None, None] + pairs[2:], w_in, w_out)
    ffn_backward(grad, da, w_in, w_out, slope, slope, bin_grad, denc)
    moves.send(denc, denc_h)
    ffn_weight_grads(enc, slope, act, da, g, turned, 1024)
    send_gradients(moves, g, scalars[4], mine, theirs)
    moves.finish()


def last_kernel(scalars, gathered, vec, *refs):
    far_data = [refs[10 * i : 10 * i + 10] for i in range(2)]
    dx_h, (mine, theirs), vec_grad = refs[20:22], refs[22:24], refs[24:26]
    near_data = [refs[26 + 10 * i : 36 + 10 * i] for i in range(2)]
    dx = refs[46:48]
    stage, w, da, d_o, dq, dk, dv, g, turned, sems = refs[48:]
    moves = Moves(sems)
    grads, pairs, copies = [], [], []
    for i in range(2):
        grads.append(moves.start(far_data[i][0], near_data[i][0]))
        pairs += [fetch_pair(moves, gathered, stage, 2 * i + n, 2 * i + n) for n in range(2)]
        copies.append(load_attn(moves, far_data[i][1:], near_data[i][1:]))
    for i in range(2):
        norm = 9 + ATTN_NORMS[i]
        grads[i].wait()
        attn_back(
            near_data[i][0], near_data[i][1:], lambda: prep_attn(stage, 2 * i, pairs, w), w,
            vec[norm : norm + 1, :], (da, d_o, dq, dk, dv, turned), dx[i], None, g, 1024 * i,
            vec_grad[i], copies[i],
        )
        moves.send(dx[i], dx_h[i])
    send_gradients(moves, g, scalars[4], mine, theirs)
    moves.finish()


def spec(space):
    return pl.BlockSpec(memory_space=space)


def call(kernel, name, inputs, outs, scratch, after=()):
    taken = len(inputs)
    inputs = inputs + [(a, H) for a in after]

    def body(*refs):
        kernel(*refs[:taken], *refs[len(inputs) :])

    return pl.pallas_call(
        body,
        name=name,
        in_specs=[spec(s) for _, s in inputs],
        out_specs=[spec(s) for _, _, s in outs],
        out_shape=[jax.ShapeDtypeStruct(shape, kind) for shape, kind, _ in outs],
        scratch_shapes=scratch,
        compiler_params=pltpu.CompilerParams(vmem_limit_bytes=VMEM),
        cost_estimate=pl.CostEstimate(flops=10**10, bytes_accessed=10**7, transcendentals=0),
    )(*[a for a, _ in inputs])


V, H, S = pltpu.VMEM, pl.ANY, pltpu.SMEM
ROW = ((ALL, D), BF)
WIDE = ((ALL, FF), BF)
LINE = ((ALL, D), F32)
INV = ((ALL, 128), F32)
EXP = ((8 * PAIRS, ROWS, ROWS), BF)
VEC = ((8, D), F32, V)
BIN = ((8, FF), F32, V)


def far(kinds):
    return [(shape, kind, H) for shape, kind in kinds]


def near(kinds):
    return [V(shape, kind) for shape, kind in kinds]


def run_forward(scalars, gathered, src, tgt, og):
    kept = (
        [ROW, LINE] + [ROW, ROW, ROW, ROW, EXP, ROW] * 3 + [ROW] * 4 + [INV] * 4
        + [ROW] * 3 + [WIDE, WIDE]
    )
    outs = far(kept) + [((D, FF), BF, H)] * 2 + [((32, D), F32, V), VEC, BIN]
    scratch = near(kept) + near([ROW, ROW, ROW]) + [
        V((8, FF), F32), V((8, 1024, 512), BF), V((1024, 128), BF), V((4, 512, 512), BF),
        V((D, FF), BF), V((FF, D), BF), V((ALL, D), F32), V((ALL, D), BF),
        V((ALL, FF), BF), V((ALL, FF), BF), V((ALL, D), BF),
        V((2, D, FF), BF), V((D, ALL), BF), pltpu.SemaphoreType.DMA((64,)),
    ]
    return call(
        forward_kernel, "forward",
        [(scalars, S), (gathered, H), (src, H), (tgt, H), (og, H)], outs, scratch,
    )


ATTN_DATA = [ROW, INV, ROW, ROW, ROW, ROW, ROW, EXP, ROW]


def attn_data(xh, inv, heads, *rows):
    q, k, v, o, e, r = heads
    return [xh, inv, r, o, q, v, k, e, *rows]


def run_middle(scalars, gathered, vec, grad, attn, ffn, after=()):
    kinds = ATTN_DATA + [ROW] + [ROW, INV, WIDE, WIDE, ROW]
    inputs = [(scalars, S), (gathered, H), (vec, V)] + [(a, H) for a in (grad, *attn, *ffn)]
    outs = far([LINE, LINE]) + [((D, 3072), BF, H)] * 2 + [VEC, VEC, BIN]
    scratch = near(kinds) + near([LINE] * 3) + [
        V((6, 1024, 512), BF), V((4, 512, 512), BF), V((D, FF), BF), V((FF, D), BF),
        *near([ROW] * 5), V((2, D, 3072), BF), V((D, ALL), BF), pltpu.SemaphoreType.DMA((40,)),
    ]
    return call(middle_kernel, "middle", inputs, outs, scratch, after)


def run_last(scalars, gathered, vec, data, after=()):
    kinds = ([LINE] + ATTN_DATA) * 2
    inputs = [(scalars, S), (gathered, H), (vec, V)] + [(a, H) for a in data]
    outs = far([LINE, LINE]) + [((D, 2048), BF, H)] * 2 + [VEC, VEC]
    scratch = near(kinds) + near([LINE] * 2) + [
        V((4, 1024, 512), BF), V((4, 512, 512), BF), *near([ROW] * 5), V((2, D, 2048), BF),
        V((D, ALL), BF), pltpu.SemaphoreType.DMA((40,)),
    ]
    return call(last_kernel, "last", inputs, outs, scratch, after)


def pack_shard(c, attn_proj, attn_out, attn_bias, norm_gain, norm_shift, ffn_in, ffn_out, b_in, b_out):
    attn = jnp.concatenate([attn_proj, attn_out[:, None]], axis=1).reshape(12, 4, 512)
    wide = ffn_in.reshape(2, 4, 4, 512).transpose(0, 2, 1, 3).reshape(8, 4, 512)
    both = lax.all_gather(jnp.concatenate([attn, wide]), "c", axis=1, tiled=True)
    half = lax.dynamic_index_in_dim(both.reshape(10, 2, 8, 512), c, 1, False)
    tall = ffn_out.reshape(2, 2, 8, 512)
    blocks = jnp.concatenate([half[:8], tall[0], half[8:], tall[1]])
    vec = [attn_bias.reshape(9, 4), norm_gain, norm_shift, b_out, jnp.zeros((3, 4), BF)]
    line = jnp.concatenate(vec + [b_in.reshape(8, 4)]).T.reshape(1, 128)
    line = jnp.pad(line, ((0, 7), (0, 0)))
    return jnp.concatenate([blocks.transpose(1, 0, 2).reshape(8, 7168), line], axis=1)


def vector_block(attn, ffn):
    rows = [attn[i][r] for i in range(3) for r in (3, 4, 2)]
    order = (attn[0], ffn[0][0], attn[1], attn[2], ffn[1][0])
    rows += [a[0] for a in order] + [a[1] for a in order] + [f[0][2] for f in ffn]
    vec = jnp.pad(jnp.stack(rows), ((0, 3), (0, 0)))
    vec = vec.reshape(3, 8, 64, 8).transpose(2, 1, 0, 3).reshape(64, 8, 24)
    wide = jnp.stack([f[1][0] for f in ffn]).reshape(2, 64, 32).transpose(1, 0, 2)
    wide = jnp.pad(wide, ((0, 0), (0, 6), (0, 72)))
    return jnp.concatenate([vec, wide], axis=2).reshape(512, 128).astype(BF)


def swap(a):
    return lax.ppermute(a, "c", [(0, 1), (1, 0)])


def pair_sum(mine, theirs):
    return (mine.astype(F32) + swap(theirs).astype(F32)).astype(BF)


def chip_sum(parts):
    whole = parts[0] if len(parts) == 1 else jnp.concatenate(parts, axis=1)
    whole = lax.all_to_all(whole.reshape(64, 8, -1), CHIPS, 0, 0, tiled=True)
    return jnp.sum(whole.astype(F32), axis=0)


def ring_sum(whole):
    return lax.psum_scatter(whole, "x", scatter_dimension=0, tiled=True)


def plane_sum(whole):
    whole = lax.all_to_all(whole.reshape(16, 8, -1), ("y", "z"), 0, 0, tiled=True)
    return jnp.sum(whole.astype(F32), axis=0)


def per_device(source, target, src_len, tgt_len, out_grad, *weights):
    c = lax.axis_index("c")
    gathered = lax.all_gather(pack_shard(c, *weights), AXES, axis=0, tiled=True)
    scalars = jnp.concatenate(
        [src_len.reshape(2), tgt_len.reshape(2), c.astype(jnp.int32)[None], jnp.zeros(3, jnp.int32)]
    )
    src, tgt, og = (a.reshape(ALL, D) for a in (source, target, out_grad))
    outs = run_forward(scalars, gathered, src, tgt, og)
    dec, grad = outs[:2]
    heads = [outs[2 + 6 * i : 8 + 6 * i] for i in range(3)]
    xh, inv = outs[20:24], outs[24:28]
    enc, mem, first, act0, slope0, f1_mine, f1_theirs, vec, f1_vec, f1_bin = outs[28:]
    f1 = pair_sum(f1_mine, f1_theirs)
    f1_x = ring_sum(f1)
    d1, d_enc, mid_mine, mid_theirs, a2_vec, f0_vec, f0_bin = run_middle(
        scalars, gathered, vec, grad, attn_data(xh[3], inv[3], heads[2], first, mem),
        [xh[1], inv[1], slope0, act0, enc], (f1,),
    )
    mid = pair_sum(mid_mine, mid_theirs)
    mid_x = ring_sum(mid)
    data = [d_enc, *attn_data(xh[0], inv[0], heads[0], src)]
    data += [d1, *attn_data(xh[2], inv[2], heads[1], tgt)]
    d_src, d_tgt, end_mine, end_theirs, a0_vec, a1_vec = run_last(
        scalars, gathered, vec, data, (mid, f1_x)
    )
    line = vector_block([a0_vec, a1_vec, a2_vec], [(f0_vec, f0_bin), (f1_vec, f1_bin)])
    sum_end = chip_sum([pair_sum(end_mine, end_theirs), pair_sum(line, line)])
    mid_x, sum_end = lax.optimization_barrier((mid_x, sum_end))
    sum_rest = plane_sum(jnp.concatenate([mid_x, f1_x], axis=1))

    cut = sum_end[:, 2048:]
    vecs = cut[:, :24].reshape(8, 3, 2, 4).transpose(1, 0, 2, 3).reshape(24, 2, 4)
    vecs = lax.dynamic_index_in_dim(vecs, c, 1, False)
    g_bin = lax.dynamic_index_in_dim(cut[:2, 24:56].reshape(2, 2, 16), c, 1, False)
    whole = jnp.concatenate([sum_end[:, :2048], sum_rest], axis=1)
    attn = whole[:, :3072].reshape(2, 4, 6, 512)
    wide = whole[:, 3072:].reshape(8, 2, 4, 512)
    rows = jnp.concatenate([attn, wide[:, :, :2].reshape(2, 4, 4, 512)], axis=2)
    keep = lax.dynamic_index_in_dim(rows, c, 0, False)
    got = swap(lax.dynamic_index_in_dim(rows, 1 - c, 0, False))
    first_half = jnp.where(c == 0, keep, got)
    second_half = jnp.where(c == 0, got, keep)
    a = first_half[:, :6].reshape(4, 3, 2, 512)
    b = second_half[:, :6].reshape(4, 3, 2, 512)
    g_proj = jnp.stack([a[:, :, 0], b[:, :, 0], a[:, :, 1]], axis=0).transpose(2, 0, 1, 3)
    g_out = b[:, :, 1].transpose(1, 0, 2)
    ia = first_half[:, 6:].reshape(4, 2, 2, 512)
    ib = second_half[:, 6:].reshape(4, 2, 2, 512)
    g_in = jnp.stack([ia, ib], axis=3).transpose(1, 0, 2, 3, 4).reshape(2, 4, 2048)
    g_wout = wide[:, :, 2:].transpose(1, 2, 0, 3).reshape(2, 16, 512)
    shape = source.shape
    return (
        dec.reshape(shape), d_src.reshape(shape), d_tgt.reshape(shape),
        g_proj, g_out, vecs[:9].reshape(3, 3, 4), vecs[9:14], vecs[14:19],
        g_in, g_wout, g_bin, vecs[19:21],
    )


def solution(mesh):
    mesh = Mesh(mesh.devices.reshape(4, 4, 4, 2), AXES)
    rows = P(None, AXES, None, None)
    lens = P(None, AXES)
    weights = (
        P(None, None, AXES, None), P(None, AXES, None), P(None, None, AXES), P(None, AXES),
        P(None, AXES), P(None, AXES, None), P(None, AXES, None), P(None, AXES), P(None, AXES),
    )
    return jax.shard_map(
        per_device,
        mesh=mesh,
        in_specs=(rows, rows, lens, lens, rows) + weights,
        out_specs=(rows, rows, rows) + weights,
        check_vma=False,
    )
```

```python
import functools

import jax
import jax.numpy as jnp
from jax import lax
from jax.experimental import pallas as pl
from jax.experimental.pallas import tpu as pltpu
from jax.sharding import Mesh
from jax.sharding import PartitionSpec as P

BF = jnp.bfloat16
F32 = jnp.float32
EPSILON = 1e-05
NEGATIVE = -1000000000.0
AXES = ("x", "y", "z", "c")
CHIPS = ("x", "y", "z")
ROWS = 256
PAIRS = 2
ALL = ROWS * PAIRS
D = 512
FF = 2048
VMEM = 61 * 1024 * 1024
ATTN_NORMS = (0, 2, 3)
FFN_NORMS = (1, 4)


def nn(a, b):
    return jnp.dot(a, b, preferred_element_type=F32)


def nt(a, b):
    return lax.dot_general(a, b, (((1,), (1,)), ((), ())), preferred_element_type=F32)


def tn(a, b):
    return lax.dot_general(a, b, (((0,), (0,)), ((), ())), preferred_element_type=F32)


def rows_of(b):
    return pl.ds(pl.multiple_of(b * ROWS, ROWS), ROWS)


def split_pair(stage, n, store_a, store_b):
    def body(i, carry):
        both = stage[n, pl.ds(pl.multiple_of(128 * i, 128), 128), :].astype(F32).reshape(8, 16, 512)
        rows = pl.ds(pl.multiple_of(64 * i, 64), 64)
        store_a(rows, both[:, :8].reshape(64, 512).astype(BF))
        store_b(rows, both[:, 8:].reshape(64, 512).astype(BF))
        return carry

    lax.fori_loop(0, 8, body, 0, unroll=2)


def prep_attn(stage, n, copies, dst):
    for half in range(2):
        copies[n + half].wait()

        def put(slot):
            def store(rows, value):
                dst[slot, rows, :] = value

            return store

        split_pair(stage, n + half, put(2 * half), put(2 * half + 1))


def prep_ffn(stage, n, copies, w_in, w_out):
    for half in range(2):
        copies[n + half].wait()

        def put(block):
            def store(rows, value):
                w_in[rows, 512 * block : 512 * block + 512] = value

            return store

        split_pair(stage, n + half, put(2 * half), put(2 * half + 1))
    copies[n + 2].wait()
    copies[n + 3].wait()

    def body(i, carry):
        span = pl.ds(pl.multiple_of(64 * i, 64), 64)
        first = stage[n + 2, span, :].astype(F32).reshape(4, 16, 512)
        second = stage[n + 3, span, :].astype(F32).reshape(4, 16, 512)
        whole = jnp.concatenate([first[:, :8], second[:, :8], first[:, 8:], second[:, 8:]], axis=1)
        w_out[pl.ds(pl.multiple_of(128 * i, 128), 128), :] = whole.reshape(128, 512).astype(BF)
        return carry

    lax.fori_loop(0, 16, body, 0, unroll=2)


def vector_kernel(block, vec, bin_vec):
    lines = block[...]
    turned = jnp.transpose(lines.astype(F32)).astype(BF)
    device = lax.broadcasted_iota(jnp.int32, (128, 512), 0)
    place = lax.broadcasted_iota(jnp.int32, (128, 512), 1)
    total = jnp.zeros((32, 512), F32)
    for e in range(4):
        spread = jnp.where(place == 4 * device + e, 1.0, 0.0).astype(BF)
        total = total + nn(turned[32 * e : 32 * e + 32], spread)
    vec[...] = total
    bin_vec[...] = jnp.zeros_like(bin_vec)
    for k in range(4):
        near_by = jnp.where((place + 512 * k) // 16 == device, 1.0, 0.0)
        for j in range(2):
            pick = jnp.where(device == 32 * (place % 4) + 24 + 4 * j + (place % 16) // 4, 1.0, 0.0)
            found = nn(lines, pick.astype(BF)) * near_by
            bin_vec[j : j + 1, 512 * k : 512 * k + 512] = jnp.sum(found, 0, keepdims=True)


def norm_forward(r, gain, shift):
    c = r - jnp.mean(r, -1, keepdims=True)
    inv = lax.rsqrt(jnp.mean(c * c, -1, keepdims=True) + EPSILON)
    xhat = c * inv
    return xhat * gain + shift, xhat, inv


def norm_backward(g, xhat, inv, gain):
    d_gain = jnp.sum(g * xhat, 0, keepdims=True)
    d_shift = jnp.sum(g, 0, keepdims=True)
    gs = g * gain
    dr = inv * (gs - jnp.mean(gs, -1, keepdims=True) - xhat * jnp.mean(gs * xhat, -1, keepdims=True))
    return dr, d_gain, d_shift


def low_half():
    return lax.broadcasted_iota(jnp.int32, (1, 128), 1) < 64


def blocks(size, total, body):
    def step(i, carry):
        body(pl.ds(pl.multiple_of(i * size, size), size))
        return carry

    lax.fori_loop(0, total // size, step, 0, unroll=4)


def attn_forward(x, h, m, w, biases, mask_of, q_ref, k_ref, v_ref, o_ref, e_ref, r_ref, after):
    for n in range(2):
        cols = pl.ds(256 * n, 256)
        part = slice(256 * n, 256 * n + 256)
        q_ref[:, cols] = ((nn(h[...], w[0, :, cols]) + biases[0][:, part]) * 0.125).astype(BF)
        k_ref[:, cols] = nn(m[...], w[1, :, cols]).astype(BF)
        v_ref[:, cols] = (nn(m[...], w[2, :, cols]) + biases[1][:, part]).astype(BF)
    low = low_half()

    def pair(b, carry):
        rows = rows_of(b)
        masked = mask_of(b)
        for j in range(4):
            cols = pl.ds(128 * j, 128)
            q = q_ref[rows, cols]
            k = k_ref[rows, cols]
            v = jnp.concatenate([v_ref[rows, cols], jnp.ones((ROWS, 128), BF)], axis=1)
            parts = []
            for half in range(2):
                mine = low if half == 0 else jnp.logical_not(low)
                s = nt(jnp.where(mine, q, jnp.zeros_like(q)), k) + masked
                e = jnp.exp(s - jnp.max(s, -1, keepdims=True)).astype(BF)
                e_ref[8 * b + 2 * j + half] = e
                parts.append(nn(e, v))
            r = 1.0 / jnp.where(low, parts[0][:, 128:], parts[1][:, 128:])
            r_ref[rows, cols] = r.astype(BF)
            o = jnp.where(low, parts[0][:, :128], parts[1][:, :128]) * r
            o_ref[rows, cols] = o.astype(BF)
        after(rows, b, x(rows) + (nn(o_ref[rows, :], w[3]) + biases[2]))
        return carry

    lax.fori_loop(0, PAIRS, pair, 0, unroll=True)


def attn_backward(b, d_o, q_ref, k_ref, v_ref, o_ref, e_ref, r_ref, dq_ref, dk_ref, dv_ref):
    rows = rows_of(b)
    low = low_half()
    for j in range(4):
        cols = pl.ds(128 * j, 128)
        q = q_ref[rows, cols]
        k = k_ref[rows, cols]
        v = v_ref[rows, cols]
        ds_o = d_o[rows, cols].astype(F32) * r_ref[rows, cols].astype(F32)
        prod = ds_o * o_ref[rows, cols].astype(F32)
        ds_o = ds_o.astype(BF)
        dqs, dks, dvs = [], [], []
        for half in range(2):
            mine = low if half == 0 else jnp.logical_not(low)
            delta = jnp.sum(jnp.where(mine, prod, 0.0), -1, keepdims=True)
            e = e_ref[8 * b + 2 * j + half]
            dp = nt(jnp.where(mine, ds_o, jnp.zeros_like(ds_o)), v)
            ds = (e.astype(F32) * (dp - delta)).astype(BF)
            dvs.append(tn(e, ds_o))
            dqs.append(nn(ds, k))
            dks.append(tn(ds, q))
        dq_ref[rows, cols] = (jnp.where(low, dqs[0], dqs[1]) * 0.125).astype(BF)
        dk_ref[rows, cols] = jnp.where(low, dks[0], dks[1]).astype(BF)
        dv_ref[rows, cols] = jnp.where(low, dvs[0], dvs[1]).astype(BF)


def gelu_both(u):
    c = 0.7978845608028654
    square = u * u
    t = jnp.tanh(c * u * (1.0 + 0.044715 * square))
    half = 0.5 * (1.0 + t)
    act = u * half
    slope = half + (0.5 * c) * u * (1.0 - t * t) * (1.0 + (3.0 * 0.044715) * square)
    return act, slope


def ffn_forward(x, h, w_in, w_out, b_in, b_out, act_ref, slope_ref, after):
    def hidden(cols):
        act, slope = gelu_both(nn(h[...], w_in[:, cols]) + b_in[:, cols])
        act_ref[:, cols] = act.astype(BF)
        slope_ref[:, cols] = slope.astype(BF)

    blocks(256, FF, hidden)

    def pair(b, carry):
        rows = rows_of(b)
        after(rows, b, x(rows) + (nn(act_ref[rows, :], w_out[...]) + b_out))
        return carry

    lax.fori_loop(0, PAIRS, pair, 0, unroll=True)


def ffn_backward(dr, df, w_in, w_out, slope_ref, du_ref, bin_grad, dx):
    def hidden(cols):
        du = nt(df[...], w_out[cols, :]) * slope_ref[:, cols].astype(F32)
        bin_grad[0:1, cols] = jnp.sum(du, 0, keepdims=True)
        du_ref[:, cols] = du.astype(BF)

    blocks(256, FF, hidden)

    def pair(b, carry):
        rows = rows_of(b)
        dx[rows, :] = dr[rows, :] + nt(du_ref[rows, :], w_in[...])
        return carry

    lax.fori_loop(0, PAIRS, pair, 0, unroll=True)


def turn(src, cols, dst):
    dst[...] = jnp.transpose(src[:, cols])


def ffn_weight_grads(h_ref, du_ref, act_ref, df_ref, g, turned, base, inner_done):
    turn(h_ref, slice(None), turned)

    def inner(k, carry):
        for n in range(2):
            part = nn(turned[...], du_ref[:, pl.ds(pl.multiple_of(512 * k + 256 * n, 256), 256)])
            at = pl.ds(pl.multiple_of(base + 512 * (k // 2) + 256 * n, 256), 256)
            g[k % 2, :, at] = part.astype(BF)
        return carry

    lax.fori_loop(0, 4, inner, 0, unroll=True)
    inner_done()

    def outer(j, carry):
        turn(act_ref, pl.ds(pl.multiple_of(512 * j, 512), 512), turned)
        rows = pl.ds(pl.multiple_of(128 * j, 128), 128)
        for n in range(2):
            part = nn(turned[...], df_ref[:, 256 * n : 256 * n + 256]).reshape(16, 4, 8, 256)
            for k in range(4):
                at = base + 1024 + 512 * (k % 2) + 256 * n
                g[k // 2, rows, at : at + 256] = part[:, k].reshape(128, 256).astype(BF)
        return carry

    lax.fori_loop(0, 4, outer, 0, unroll=2)


def planes_first(part):
    wide = part.shape[-1]
    return part.reshape(4, 16, 8, wide).transpose(1, 0, 2, 3).reshape(512, wide)


def attn_weight_grads(h_ref, m_ref, o_ref, da_ref, dq_ref, dk_ref, dv_ref, g, turned, base, order):
    def product(side, at, right):
        for n in range(2):
            cols = slice(256 * n, 256 * n + 256)
            start = base + at + 256 * n
            g[side, :, start : start + 256] = order(nn(turned[...], right[:, cols])).astype(BF)

    turn(h_ref, slice(None), turned)
    product(0, 0, dq_ref)
    if m_ref is not h_ref:
        turn(m_ref, slice(None), turned)
    product(1, 0, dk_ref)
    product(0, 512, dv_ref)
    turn(o_ref, slice(None), turned)
    product(1, 512, da_ref)


def send_out(g, core, mine, theirs, sems):
    other = pltpu.make_async_copy(g.at[1 - core], theirs, sems.at[0])
    own = pltpu.make_async_copy(g.at[core], mine, sems.at[1])
    other.start()
    own.start()
    return other, own


class Moves:
    def __init__(self, sems):
        self.sems, self.used, self.open = sems, 0, []

    def start(self, src, dst):
        copy = pltpu.make_async_copy(src, dst, self.sems.at[self.used])
        self.used += 1
        copy.start()
        return copy

    def send(self, src, dst):
        self.open.append(self.start(src, dst))

    def finish(self):
        for copy in self.open:
            copy.wait()


def fetch_pair(moves, gathered, stage, pair, slot):
    return moves.start(gathered.at[:, pl.ds(512 * pair, 512)], stage.at[slot])


def forward_kernel(scalars, gathered, vec, bin_vec, src_h, tgt_h, og_h, *refs):
    (
        dec_h, grad_h,
        q0h, k0h, v0h, o0h, e0h, r0h, q1h, k1h, v1h, o1h, e1h, r1h, q2h, k2h, v2h, o2h, e2h, r2h,
        xh0h, xh1h, xh2h, xh3h, inv0h, inv1h, inv2h, inv3h,
        enc_h, mem_h, first_h, act0h, slope0h, mine, theirs, vec_grad, bin_grad,
        dec, grad_d2,
        q0, k0, v0, o0, e0, r0, q1, k1, v1, o1, e1, r1, q2, k2, v2, o2, e2, r2,
        xh0, xh1, xh2, xh3, inv0, inv1, inv2, inv3,
        enc, mem, first, act0, slope0,
        src, tgt, og, stage, w_attn, w_in, w_out, x32, second,
        act1, slope1, df, g, turned, sems,
    ) = refs
    moves = Moves(sems)
    pairs = {n: fetch_pair(moves, gathered, stage, n, n) for n in (0, 1)}
    src_in = moves.start(src_h, src)

    def bias(layer):
        return [vec[3 * layer + j : 3 * layer + j + 1, :] for j in range(3)]

    def gain(n):
        return vec[9 + n : 10 + n, :]

    def shift(n):
        return vec[14 + n : 15 + n, :]

    def source_keys(b):
        place = lax.broadcasted_iota(jnp.int32, (1, ROWS), 1)
        return jnp.where(place < scalars[b], 0.0, NEGATIVE)

    def target_keys(b):
        at_q = lax.broadcasted_iota(jnp.int32, (ROWS, ROWS), 0)
        at_k = lax.broadcasted_iota(jnp.int32, (ROWS, ROWS), 1)
        live = jnp.logical_and(at_q >= at_k, at_k < scalars[2 + b])
        return jnp.where(live, 0.0, NEGATIVE)

    def keeper(n, xh, inv_ref, low, wide):
        def after(rows, b, r):
            z, xhat, inv = norm_forward(r, gain(n), shift(n))
            xh[rows, :] = xhat.astype(BF)
            inv_ref[rows, :] = jnp.broadcast_to(inv, (ROWS, 128))
            low[rows, :] = z.astype(BF)
            if wide is not None:
                wide[rows, :] = z

        return after

    def from_low(ref):
        return lambda rows: ref[rows, :].astype(F32)

    def from_x32(rows):
        return x32[rows, :]

    src_in.wait()
    prep_attn(stage, 0, [pairs[0], pairs[1]], w_attn)
    for n in range(4):
        pairs[6 + n] = fetch_pair(moves, gathered, stage, 6 + n, 2 + n)
    tgt_in = moves.start(tgt_h, tgt)
    for n in (2, 3):
        pairs[n] = fetch_pair(moves, gathered, stage, n, 4 + n)
    og_in = moves.start(og_h, og)
    pairs[4] = fetch_pair(moves, gathered, stage, 4, 0)
    pairs[5] = fetch_pair(moves, gathered, stage, 5, 1)
    attn_forward(
        from_low(src), src, src, w_attn, bias(0), source_keys, q0, k0, v0, o0, e0, r0,
        keeper(0, xh0, inv0, enc, x32),
    )
    for a, b in ((q0, q0h), (k0, k0h), (v0, v0h), (o0, o0h), (e0, e0h), (r0, r0h),
                 (xh0, xh0h), (inv0, inv0h), (enc, enc_h)):
        moves.send(a, b)
    prep_ffn(stage, 2, [None, None] + [pairs[6 + n] for n in range(4)], w_in, w_out)
    for n in range(4):
        pairs[10 + n] = fetch_pair(moves, gathered, stage, 10 + n, 2 + n)
    ffn_forward(
        from_x32, enc, w_in, w_out, bin_vec.at[0:1], vec[19:20, :], act0, slope0,
        keeper(1, xh1, inv1, mem, None),
    )
    for a, b in ((xh1, xh1h), (inv1, inv1h), (mem, mem_h), (act0, act0h), (slope0, slope0h)):
        moves.send(a, b)
    tgt_in.wait()
    prep_attn(stage, 6, [None] * 6 + [pairs[2], pairs[3]], w_attn)
    attn_forward(
        from_low(tgt), tgt, tgt, w_attn, bias(1), target_keys, q1, k1, v1, o1, e1, r1,
        keeper(2, xh2, inv2, first, x32),
    )
    for a, b in ((q1, q1h), (k1, k1h), (v1, v1h), (o1, o1h), (e1, e1h), (r1, r1h),
                 (xh2, xh2h), (inv2, inv2h), (first, first_h)):
        moves.send(a, b)
    prep_attn(stage, 0, [pairs[4], pairs[5]], w_attn)
    attn_forward(
        from_x32, first, mem, w_attn, bias(2), source_keys, q2, k2, v2, o2, e2, r2,
        keeper(3, xh3, inv3, second, x32),
    )
    for a, b in ((q2, q2h), (k2, k2h), (v2, v2h), (o2, o2h), (e2, e2h), (r2, r2h),
                 (xh3, xh3h), (inv3, inv3h)):
        moves.send(a, b)
    prep_ffn(stage, 2, [None, None] + [pairs[10 + n] for n in range(4)], w_in, w_out)
    vec_grad[...] = jnp.zeros_like(vec_grad)
    bin_grad[...] = jnp.zeros_like(bin_grad)
    og_in.wait()

    def last(rows, b, r):
        z, xhat, inv = norm_forward(r, gain(4), shift(4))
        dec[rows, :] = z.astype(BF)
        at = lax.broadcasted_iota(jnp.int32, (ROWS, 1), 0)
        gz = jnp.where(at < scalars[2 + b], og[rows, :].astype(F32), 0.0)
        dr, d_gain, d_shift = norm_backward(gz, xhat, inv, gain(4))
        vec_grad[0:1, :] += d_gain
        vec_grad[1:2, :] += d_shift
        vec_grad[2:3, :] += jnp.sum(dr, 0, keepdims=True)
        df[rows, :] = dr.astype(BF)
        x32[rows, :] = dr

    ffn_forward(
        from_x32, second, w_in, w_out, bin_vec.at[1:2], vec[20:21, :], act1, slope1, last
    )
    moves.send(dec, dec_h)
    ffn_backward(x32, df, w_in, w_out, slope1, slope1, bin_grad, grad_d2)
    moves.send(grad_d2, grad_h)
    core = scalars[4]

    def inner_done():
        send_gradients(moves, g, core, mine, theirs, 0, 1024)

    ffn_weight_grads(second, slope1, act1, df, g, turned, 0, inner_done)
    send_gradients(moves, g, core, mine, theirs, 1024, 1024)
    moves.finish()


def norm_rows(vec_grad, grad, xh, inv, gain, low, wide):
    vec_grad[...] = jnp.zeros_like(vec_grad)

    def pair(b, carry):
        rows = rows_of(b)
        dr, d_gain, d_shift = norm_backward(
            grad[rows, :], xh[rows, :].astype(F32), inv[rows, 0:1], gain
        )
        vec_grad[0:1, :] += d_gain
        vec_grad[1:2, :] += d_shift
        vec_grad[2:3, :] += jnp.sum(dr, 0, keepdims=True)
        low[rows, :] = dr.astype(BF)
        wide[rows, :] = dr
        return carry

    lax.fori_loop(0, PAIRS, pair, 0, unroll=True)


def load_attn(moves, far_refs, near_refs):
    far_refs, near_refs = list(far_refs), list(near_refs)
    first = [moves.start(a, b) for a, b in zip(far_refs[:2], near_refs[:2])]
    heads = [moves.start(a, b) for a, b in zip(far_refs[2:8], near_refs[2:8])]
    rows = [moves.start(a, b) for a, b in zip(far_refs[8:], near_refs[8:])]
    return first, heads, rows


def attn_back(grad, data, weights, w, gain, temps, dx, grad_mem, g, base, vec_grad, copies, arrived, order):
    xh, inv, r, o, q, v, k, e, h = data[:9]
    m = data[9] if len(data) > 9 else h
    da, d_o, dq, dk, dv, turned = temps
    first, heads, rows_in = copies
    for copy in first:
        copy.wait()
    norm_rows(vec_grad, grad, xh, inv, gain, da, dx)
    weights()
    for n in range(2):
        cols = pl.ds(256 * n, 256)
        d_o[:, cols] = nt(da[...], w[3, cols, :]).astype(BF)
    for copy in heads:
        copy.wait()
    arrived()

    def body(b, carry):
        attn_backward(b, d_o, q, k, v, o, e, r, dq, dk, dv)
        rows = rows_of(b)
        vec_grad[3:4, :] += jnp.sum(dq[rows, :].astype(F32), 0, keepdims=True)
        vec_grad[4:5, :] += jnp.sum(dv[rows, :].astype(F32), 0, keepdims=True)
        to_m = nt(dk[rows, :], w[1]) + nt(dv[rows, :], w[2])
        to_x = dx[rows, :] + nt(dq[rows, :], w[0])
        if grad_mem is not None:
            grad_mem[rows, :] = to_m
            dx[rows, :] = to_x
        else:
            dx[rows, :] = to_x + to_m
        return carry

    lax.fori_loop(0, PAIRS, body, 0, unroll=True)
    for copy in rows_in:
        copy.wait()
    attn_weight_grads(h, m, o, da, dq, dk, dv, g, turned, base, order)


def send_gradients(moves, g, core, mine, theirs, at, size):
    cols = pl.ds(at, size)
    moves.send(g.at[1 - core, :, cols], theirs.at[:, cols])
    moves.send(g.at[core, :, cols], mine.at[:, cols])


def middle_kernel(scalars, gathered, vec, grad_h, *refs):
    far_attn, far_ffn = refs[:10], refs[10:15]
    d1_h, denc_h, mine, theirs, attn_vec, ffn_vec, bin_grad = refs[15:22]
    near_attn, near_ffn = refs[22:32], refs[32:37]
    grad, d1, denc, stage, w, w_in, w_out, da, d_o, dq, dk, dv, g, turned, sems = refs[37:]
    moves = Moves(sems)
    grad_in = moves.start(grad_h, grad)
    pairs = [fetch_pair(moves, gathered, stage, 4 + n, n) for n in range(2)]
    copies = load_attn(moves, far_attn, near_attn)
    xh1, inv1, slope, act, enc = near_ffn
    ffn_in = []

    def arrived():
        pairs.extend([fetch_pair(moves, gathered, stage, 6 + n, 2 + n) for n in range(4)])
        ffn_in.extend([moves.start(a, b) for a, b in zip(far_ffn, near_ffn)])

    bin_grad[...] = jnp.zeros_like(bin_grad)
    grad_in.wait()
    attn_back(
        grad, near_attn, lambda: prep_attn(stage, 0, pairs, w), w, vec[12:13, :],
        (da, d_o, dq, dk, dv, turned), d1, grad, g, 0, attn_vec, copies, arrived, lambda part: part,
    )
    core = scalars[4]
    send_gradients(moves, g, core, mine, theirs, 0, 1024)
    moves.send(d1, d1_h)
    for copy in ffn_in:
        copy.wait()
    norm_rows(ffn_vec, grad, xh1, inv1, vec[10:11, :], da, grad)
    prep_ffn(stage, 2, [None, None] + pairs[2:], w_in, w_out)
    ffn_backward(grad, da, w_in, w_out, slope, slope, bin_grad, denc)
    moves.send(denc, denc_h)

    def inner_done():
        send_gradients(moves, g, core, mine, theirs, 1024, 1024)

    ffn_weight_grads(enc, slope, act, da, g, turned, 1024, inner_done)
    send_gradients(moves, g, core, mine, theirs, 2048, 1024)
    moves.finish()


def write_vectors(attn, ffn, ffn_bins, g, at):
    rows = [attn[i][r : r + 1, :] for i in range(3) for r in (3, 4, 2)]
    order = (attn[0], ffn[0], attn[1], attn[2], ffn[1])
    rows += [a[0:1, :] for a in order] + [a[1:2, :] for a in order] + [f[2:3, :] for f in ffn]
    whole = jnp.concatenate(rows + [jnp.zeros((3, 512), F32)], axis=0)
    wide = jnp.concatenate([f[0:1, :] for f in ffn_bins] + [jnp.zeros((6, FF), F32)], axis=0)
    lane = lax.broadcasted_iota(jnp.int32, (8, 128), 1)
    tiles = []
    for p in [16 * x + yz for yz in range(16) for x in range(4)]:
        cols = slice(128 * (p // 16), 128 * (p // 16) + 128)
        tile = jnp.zeros((8, 128), F32)
        for n in range(3):
            turned = pltpu.roll(whole[8 * n : 8 * n + 8, cols], (8 * n - 8 * (p % 16)) % 128, 1)
            tile = jnp.where(lane // 8 == n, turned, tile)
        cols = slice(128 * (p // 4), 128 * (p // 4) + 128)
        turned = pltpu.roll(wide[:, cols], (32 - 32 * (p % 4)) % 128, 1)
        tiles.append(jnp.where(lane // 32 == 1, turned, tile))
    block = jnp.concatenate(tiles, axis=0).astype(BF)
    for side in range(2):
        g[side, :, at : at + 128] = block


def last_kernel(scalars, gathered, vec, a2_vec, f0_vec, f1_vec, f0_bin, f1_bin, *refs):
    far_data = [refs[10 * i : 10 * i + 10] for i in range(2)]
    dx_h, (mine, theirs) = refs[20:22], refs[22:24]
    near_data = [refs[24 + 10 * i : 34 + 10 * i] for i in range(2)]
    dx, vec_grad = refs[44:46], refs[46:48]
    stage, w, da, d_o, dq, dk, dv, g, turned, sems = refs[48:]
    moves = Moves(sems)
    grads, pairs, copies = [], [], []
    core = scalars[4]

    def start():
        i = len(grads)
        if i < 2:
            grads.append(moves.start(far_data[i][0], near_data[i][0]))
            slots = range(2 * i, 2 * i + 2)
            pairs.extend([fetch_pair(moves, gathered, stage, n, n) for n in slots])
            copies.append(load_attn(moves, far_data[i][1:], near_data[i][1:]))

    start()
    for i in range(2):
        norm = 9 + ATTN_NORMS[i]
        grads[i].wait()
        attn_back(
            near_data[i][0], near_data[i][1:], lambda: prep_attn(stage, 2 * i, pairs, w), w,
            vec[norm : norm + 1, :], (da, d_o, dq, dk, dv, turned), dx[i], None, g, 1024 * i,
            vec_grad[i], copies[i], start, planes_first,
        )
        if i == 1:
            write_vectors((*vec_grad, a2_vec), (f0_vec, f1_vec), (f0_bin, f1_bin), g, 2048)
        send_gradients(moves, g, core, mine, theirs, 1024 * i, 1024 + 128 * i)
        moves.send(dx[i], dx_h[i])
    moves.finish()


def spec(space):
    return pl.BlockSpec(memory_space=space)


def call(kernel, name, inputs, outs, scratch, after=()):
    taken = len(inputs)
    inputs = inputs + [(a, H) for a in after]

    def body(*refs):
        kernel(*refs[:taken], *refs[len(inputs) :])

    return pl.pallas_call(
        body,
        name=name,
        in_specs=[spec(s) for _, s in inputs],
        out_specs=[spec(s) for _, _, s in outs],
        out_shape=[jax.ShapeDtypeStruct(shape, kind) for shape, kind, _ in outs],
        scratch_shapes=scratch,
        compiler_params=pltpu.CompilerParams(vmem_limit_bytes=VMEM),
        cost_estimate=pl.CostEstimate(flops=10**10, bytes_accessed=10**7, transcendentals=0),
    )(*[a for a, _ in inputs])


V, H, S = pltpu.VMEM, pl.ANY, pltpu.SMEM
ROW = ((ALL, D), BF)
WIDE = ((ALL, FF), BF)
LINE = ((ALL, D), F32)
INV = ((ALL, 128), F32)
EXP = ((8 * PAIRS, ROWS, ROWS), BF)
VEC = ((8, D), F32, V)
BIN = ((8, FF), F32, V)


def far(kinds):
    return [(shape, kind, H) for shape, kind in kinds]


def near(kinds):
    return [V(shape, kind) for shape, kind in kinds]


def run_vectors(block):
    return call(vector_kernel, "vectors", [(block, V)], [((32, D), F32, V), BIN], [])


def run_forward(scalars, gathered, vec, bin_vec, src, tgt, og):
    kept = (
        [ROW, LINE] + [ROW, ROW, ROW, ROW, EXP, ROW] * 3 + [ROW] * 4 + [INV] * 4
        + [ROW] * 3 + [WIDE, WIDE]
    )
    outs = far(kept) + [((D, FF), BF, H)] * 2 + [VEC, BIN]
    scratch = near(kept) + near([ROW, ROW, ROW]) + [
        V((8, 1024, 512), BF), V((4, 512, 512), BF),
        V((D, FF), BF), V((FF, D), BF), V((ALL, D), F32), V((ALL, D), BF),
        V((ALL, FF), BF), V((ALL, FF), BF), V((ALL, D), BF),
        V((2, D, FF), BF), V((D, ALL), BF), pltpu.SemaphoreType.DMA((64,)),
    ]
    return call(
        forward_kernel, "forward",
        [(scalars, S), (gathered, H), (vec, V), (bin_vec, V), (src, H), (tgt, H), (og, H)], outs, scratch,
    )


ATTN_DATA = [ROW, INV, ROW, ROW, ROW, ROW, ROW, EXP, ROW]


def attn_data(xh, inv, heads, *rows):
    q, k, v, o, e, r = heads
    return [xh, inv, r, o, q, v, k, e, *rows]


def run_middle(scalars, gathered, vec, grad, attn, ffn, after=()):
    kinds = ATTN_DATA + [ROW] + [ROW, INV, WIDE, WIDE, ROW]
    inputs = [(scalars, S), (gathered, H), (vec, V)] + [(a, H) for a in (grad, *attn, *ffn)]
    outs = far([LINE, LINE]) + [((D, 3072), BF, H)] * 2 + [VEC, VEC, BIN]
    scratch = near(kinds) + near([LINE] * 3) + [
        V((6, 1024, 512), BF), V((4, 512, 512), BF), V((D, FF), BF), V((FF, D), BF),
        *near([ROW] * 5), V((2, D, 3072), BF), V((D, ALL), BF), pltpu.SemaphoreType.DMA((40,)),
    ]
    return call(middle_kernel, "middle", inputs, outs, scratch, after)


def run_last(scalars, gathered, vec, sums, data, after=()):
    kinds = ([LINE] + ATTN_DATA) * 2
    inputs = [(scalars, S), (gathered, H), (vec, V)]
    inputs += [(a, V) for a in sums] + [(a, H) for a in data]
    outs = far([LINE, LINE]) + [((D, 2176), BF, H)] * 2
    scratch = near(kinds) + near([LINE] * 2) + [V((8, D), F32), V((8, D), F32)] + [
        V((4, 1024, 512), BF), V((4, 512, 512), BF), *near([ROW] * 5), V((2, D, 2176), BF),
        V((D, ALL), BF), pltpu.SemaphoreType.DMA((40,)),
    ]
    return call(last_kernel, "last", inputs, outs, scratch, after)


def pack_shard(c, attn_proj, attn_out, attn_bias, norm_gain, norm_shift, ffn_in, ffn_out, b_in, b_out):
    attn = jnp.concatenate([attn_proj, attn_out[:, None]], axis=1).reshape(12, 4, 512)
    wide = ffn_in.reshape(2, 4, 4, 512).transpose(0, 2, 1, 3).reshape(8, 4, 512)
    both = lax.all_gather(jnp.concatenate([attn, wide]), "c", axis=1, tiled=True)
    half = lax.dynamic_index_in_dim(both.reshape(10, 2, 8, 512), c, 1, False)
    tall = ffn_out.reshape(2, 2, 8, 512)
    blocks = jnp.concatenate([half[:8], tall[0], half[8:], tall[1]])
    vec = [attn_bias.reshape(9, 4), norm_gain, norm_shift, b_out, jnp.zeros((3, 4), BF)]
    line = jnp.concatenate(vec + [b_in.reshape(8, 4)]).T.reshape(1, 128)
    return blocks.transpose(1, 0, 2).reshape(8, 7168), line


def swap(a):
    return lax.ppermute(a, "c", [(0, 1), (1, 0)])


def pair_sum(mine, theirs):
    return (mine.astype(F32) + swap(theirs).astype(F32)).astype(BF)


def ring_sum(whole):
    return lax.psum_scatter(whole, "x", scatter_dimension=0, tiled=True)


def plane_sum(whole):
    whole = whole.reshape(16, -1, whole.shape[1])
    whole = lax.all_to_all(whole, ("y", "z"), 0, 0, tiled=True)
    return jnp.sum(whole.astype(F32), axis=0)


def line_sum(whole):
    blocks = whole.reshape(4, 8, -1)
    x = lax.axis_index("x")
    total = lax.dynamic_index_in_dim(blocks, x, 0, False)
    for k in range(1, 4):
        part = lax.dynamic_index_in_dim(blocks, (x + k) % 4, 0, False).astype(BF)
        part = lax.ppermute(part, "x", [(i, (i + k) % 4) for i in range(4)])
        total = total + part.astype(F32)
    return total


def per_device(source, target, src_len, tgt_len, out_grad, *weights):
    c = lax.axis_index("c")
    shard, line = pack_shard(c, *weights)
    gathered = lax.all_gather(shard, AXES, axis=0, tiled=True)
    vec, bin_vec = run_vectors(lax.all_gather(line, AXES, axis=0, tiled=True))
    scalars = jnp.concatenate(
        [src_len.reshape(2), tgt_len.reshape(2), c.astype(jnp.int32)[None], jnp.zeros(3, jnp.int32)]
    )
    src, tgt, og = (a.reshape(ALL, D) for a in (source, target, out_grad))
    outs = run_forward(scalars, gathered, vec, bin_vec, src, tgt, og)
    dec, grad = outs[:2]
    heads = [outs[2 + 6 * i : 8 + 6 * i] for i in range(3)]
    xh, inv = outs[20:24], outs[24:28]
    enc, mem, first, act0, slope0, f1_mine, f1_theirs, f1_vec, f1_bin = outs[28:]
    f1 = pair_sum(f1_mine, f1_theirs)
    f1_x = ring_sum(f1)
    d1, d_enc, mid_mine, mid_theirs, a2_vec, f0_vec, f0_bin = run_middle(
        scalars, gathered, vec, grad, attn_data(xh[3], inv[3], heads[2], first, mem),
        [xh[1], inv[1], slope0, act0, enc], (f1,),
    )
    mid = pair_sum(mid_mine, mid_theirs)
    mid_x = ring_sum(mid)
    data = [d_enc, *attn_data(xh[0], inv[0], heads[0], src)]
    data += [d1, *attn_data(xh[2], inv[2], heads[1], tgt)]
    d_src, d_tgt, end_mine, end_theirs = run_last(
        scalars, gathered, vec, (a2_vec, f0_vec, f1_vec, f0_bin, f1_bin), data, (mid, f1_x)
    )
    end = plane_sum(pair_sum(end_mine, end_theirs))
    mid_x, end = lax.optimization_barrier((mid_x, end))
    sum_end = line_sum(end)
    sum_rest = plane_sum(jnp.concatenate([mid_x, f1_x], axis=1))

    cut = sum_end[:, 2048:]
    vecs = cut[:, :24].reshape(8, 3, 2, 4).transpose(1, 0, 2, 3).reshape(24, 2, 4)
    vecs = lax.dynamic_index_in_dim(vecs, c, 1, False)
    g_bin = lax.dynamic_index_in_dim(cut[:2, 32:64].reshape(2, 2, 16), c, 1, False)
    whole = jnp.concatenate([sum_end[:, :2048], sum_rest], axis=1)
    attn = whole[:, :3072].reshape(2, 4, 6, 512)
    wide = whole[:, 3072:].reshape(8, 2, 4, 512)
    rows = jnp.concatenate([attn, wide[:, :, :2].reshape(2, 4, 4, 512)], axis=2)
    keep = lax.dynamic_index_in_dim(rows, c, 0, False)
    got = swap(lax.dynamic_index_in_dim(rows, 1 - c, 0, False))
    first_half = jnp.where(c == 0, keep, got)
    second_half = jnp.where(c == 0, got, keep)
    a = first_half[:, :6].reshape(4, 3, 2, 512)
    b = second_half[:, :6].reshape(4, 3, 2, 512)
    g_proj = jnp.stack([a[:, :, 0], b[:, :, 0], a[:, :, 1]], axis=0).transpose(2, 0, 1, 3)
    g_out = b[:, :, 1].transpose(1, 0, 2)
    ia = first_half[:, 6:].reshape(4, 2, 2, 512)
    ib = second_half[:, 6:].reshape(4, 2, 2, 512)
    g_in = jnp.stack([ia, ib], axis=3).transpose(1, 0, 2, 3, 4).reshape(2, 4, 2048)
    g_wout = wide[:, :, 2:].transpose(1, 2, 0, 3).reshape(2, 16, 512)
    shape = source.shape
    return (
        dec.reshape(shape), d_src.reshape(shape), d_tgt.reshape(shape),
        g_proj, g_out, vecs[:9].reshape(3, 3, 4), vecs[9:14], vecs[14:19],
        g_in, g_wout, g_bin, vecs[19:21],
    )


def solution(mesh):
    mesh = Mesh(mesh.devices.reshape(4, 4, 4, 2), AXES)
    rows = P(None, AXES, None, None)
    lens = P(None, AXES)
    weights = (
        P(None, None, AXES, None), P(None, AXES, None), P(None, None, AXES), P(None, AXES),
        P(None, AXES), P(None, AXES, None), P(None, AXES, None), P(None, AXES), P(None, AXES),
    )
    return jax.shard_map(
        per_device,
        mesh=mesh,
        in_specs=(rows, rows, lens, lens, rows) + weights,
        out_specs=(rows, rows, rows) + weights,
        check_vma=False,
    )
```

```python
import functools

import jax
import jax.numpy as jnp
from jax import lax
from jax.experimental import pallas as pl
from jax.experimental.pallas import tpu as pltpu
from jax.sharding import Mesh
from jax.sharding import PartitionSpec as P

BF = jnp.bfloat16
F32 = jnp.float32
EPSILON = 1e-05
NEGATIVE = -1000000000.0
AXES = ("x", "y", "z", "c")
CHIPS = ("x", "y", "z")
ROWS = 256
PAIRS = 2
ALL = ROWS * PAIRS
D = 512
FF = 2048
VMEM = 61 * 1024 * 1024
ATTN_NORMS = (0, 2, 3)
FFN_NORMS = (1, 4)


def nn(a, b):
    return jnp.dot(a, b, preferred_element_type=F32)


def nt(a, b):
    return lax.dot_general(a, b, (((1,), (1,)), ((), ())), preferred_element_type=F32)


def tn(a, b):
    return lax.dot_general(a, b, (((0,), (0,)), ((), ())), preferred_element_type=F32)


def rows_of(b):
    return pl.ds(pl.multiple_of(b * ROWS, ROWS), ROWS)


def split_pair(stage, n, store_a, store_b):
    def body(i, carry):
        both = stage[n, pl.ds(pl.multiple_of(128 * i, 128), 128), :].astype(F32).reshape(8, 16, 512)
        rows = pl.ds(pl.multiple_of(64 * i, 64), 64)
        store_a(rows, both[:, :8].reshape(64, 512).astype(BF))
        store_b(rows, both[:, 8:].reshape(64, 512).astype(BF))
        return carry

    lax.fori_loop(0, 8, body, 0, unroll=8)


def prep_attn(stage, n, copies, dst):
    for half in range(2):
        copies[n + half].wait()

        def put(slot):
            def store(rows, value):
                dst[slot, rows, :] = value

            return store

        split_pair(stage, n + half, put(2 * half), put(2 * half + 1))


def prep_ffn(stage, n, copies, w_in, w_out):
    for half in range(2):
        copies[n + half].wait()

        def put(block):
            def store(rows, value):
                w_in[rows, 512 * block : 512 * block + 512] = value

            return store

        split_pair(stage, n + half, put(2 * half), put(2 * half + 1))
    copies[n + 2].wait()
    copies[n + 3].wait()

    def body(i, carry):
        span = pl.ds(pl.multiple_of(64 * i, 64), 64)
        first = stage[n + 2, span, :].astype(F32).reshape(4, 16, 512)
        second = stage[n + 3, span, :].astype(F32).reshape(4, 16, 512)
        whole = jnp.concatenate([first[:, :8], second[:, :8], first[:, 8:], second[:, 8:]], axis=1)
        w_out[pl.ds(pl.multiple_of(128 * i, 128), 128), :] = whole.reshape(128, 512).astype(BF)
        return carry

    lax.fori_loop(0, 16, body, 0, unroll=8)


def vector_kernel(block, vec, bin_vec):
    lines = block[...]
    turned = jnp.transpose(lines.astype(F32)).astype(BF)
    device = lax.broadcasted_iota(jnp.int32, (128, 512), 0)
    place = lax.broadcasted_iota(jnp.int32, (128, 512), 1)
    total = jnp.zeros((32, 512), F32)
    for e in range(4):
        spread = jnp.where(place == 4 * device + e, 1.0, 0.0).astype(BF)
        total = total + nn(turned[32 * e : 32 * e + 32], spread)
    vec[...] = total
    bin_vec[...] = jnp.zeros_like(bin_vec)
    for k in range(4):
        near_by = jnp.where((place + 512 * k) // 16 == device, 1.0, 0.0)
        for j in range(2):
            pick = jnp.where(device == 32 * (place % 4) + 24 + 4 * j + (place % 16) // 4, 1.0, 0.0)
            found = nn(lines, pick.astype(BF)) * near_by
            bin_vec[j : j + 1, 512 * k : 512 * k + 512] = jnp.sum(found, 0, keepdims=True)


def norm_forward(r, gain, shift):
    c = r - jnp.mean(r, -1, keepdims=True)
    inv = lax.rsqrt(jnp.mean(c * c, -1, keepdims=True) + EPSILON)
    xhat = c * inv
    return xhat * gain + shift, xhat, inv


def norm_backward(g, xhat, inv, gain):
    d_gain = jnp.sum(g * xhat, 0, keepdims=True)
    d_shift = jnp.sum(g, 0, keepdims=True)
    gs = g * gain
    dr = inv * (gs - jnp.mean(gs, -1, keepdims=True) - xhat * jnp.mean(gs * xhat, -1, keepdims=True))
    return dr, d_gain, d_shift


def low_half():
    return lax.broadcasted_iota(jnp.int32, (1, 128), 1) < 64


def blocks(size, total, body):
    def step(i, carry):
        body(pl.ds(pl.multiple_of(i * size, size), size))
        return carry

    lax.fori_loop(0, total // size, step, 0, unroll=8)


def attn_forward(x, h, m, w, biases, mask_of, q_ref, k_ref, v_ref, o_ref, e_ref, r_ref, after):
    for n in range(2):
        cols = pl.ds(256 * n, 256)
        part = slice(256 * n, 256 * n + 256)
        q_ref[:, cols] = ((nn(h[...], w[0, :, cols]) + biases[0][:, part]) * 0.125).astype(BF)
        k_ref[:, cols] = nn(m[...], w[1, :, cols]).astype(BF)
        v_ref[:, cols] = (nn(m[...], w[2, :, cols]) + biases[1][:, part]).astype(BF)
    low = low_half()

    def pair(b, carry):
        rows = rows_of(b)
        masked = mask_of(b)
        for j in range(4):
            cols = pl.ds(128 * j, 128)
            q = q_ref[rows, cols]
            k = k_ref[rows, cols]
            v = jnp.concatenate([v_ref[rows, cols], jnp.ones((ROWS, 128), BF)], axis=1)
            parts = []
            for half in range(2):
                mine = low if half == 0 else jnp.logical_not(low)
                s = nt(jnp.where(mine, q, jnp.zeros_like(q)), k) + masked
                e = jnp.exp(s - jnp.max(s, -1, keepdims=True)).astype(BF)
                e_ref[8 * b + 2 * j + half] = e
                parts.append(nn(e, v))
            r = 1.0 / jnp.where(low, parts[0][:, 128:], parts[1][:, 128:])
            r_ref[rows, cols] = r.astype(BF)
            o = jnp.where(low, parts[0][:, :128], parts[1][:, :128]) * r
            o_ref[rows, cols] = o.astype(BF)
        after(rows, b, x(rows) + (nn(o_ref[rows, :], w[3]) + biases[2]))
        return carry

    lax.fori_loop(0, PAIRS, pair, 0, unroll=True)


def attn_backward(b, d_o, q_ref, k_ref, v_ref, o_ref, e_ref, r_ref, dq_ref, dk_ref, dv_ref):
    rows = rows_of(b)
    low = low_half()
    for j in range(4):
        cols = pl.ds(128 * j, 128)
        q = q_ref[rows, cols]
        k = k_ref[rows, cols]
        v = v_ref[rows, cols]
        ds_o = d_o[rows, cols].astype(F32) * r_ref[rows, cols].astype(F32)
        prod = ds_o * o_ref[rows, cols].astype(F32)
        ds_o = ds_o.astype(BF)
        dqs, dks, dvs = [], [], []
        for half in range(2):
            mine = low if half == 0 else jnp.logical_not(low)
            delta = jnp.sum(jnp.where(mine, prod, 0.0), -1, keepdims=True)
            e = e_ref[8 * b + 2 * j + half]
            dp = nt(jnp.where(mine, ds_o, jnp.zeros_like(ds_o)), v)
            ds = (e.astype(F32) * (dp - delta)).astype(BF)
            dvs.append(tn(e, ds_o))
            dqs.append(nn(ds, k))
            dks.append(tn(ds, q))
        dq_ref[rows, cols] = (jnp.where(low, dqs[0], dqs[1]) * 0.125).astype(BF)
        dk_ref[rows, cols] = jnp.where(low, dks[0], dks[1]).astype(BF)
        dv_ref[rows, cols] = jnp.where(low, dvs[0], dvs[1]).astype(BF)


def gelu_both(u):
    c = 0.7978845608028654
    square = u * u
    t = jnp.tanh(c * u * (1.0 + 0.044715 * square))
    half = 0.5 * (1.0 + t)
    act = u * half
    slope = half + (0.5 * c) * u * (1.0 - t * t) * (1.0 + (3.0 * 0.044715) * square)
    return act, slope


def ffn_forward(x, h, w_in, w_out, b_in, b_out, act_ref, slope_ref, after):
    def hidden(cols):
        act, slope = gelu_both(nn(h[...], w_in[:, cols]) + b_in[:, cols])
        act_ref[:, cols] = act.astype(BF)
        slope_ref[:, cols] = slope.astype(BF)

    blocks(256, FF, hidden)

    def pair(b, carry):
        rows = rows_of(b)
        after(rows, b, x(rows) + (nn(act_ref[rows, :], w_out[...]) + b_out))
        return carry

    lax.fori_loop(0, PAIRS, pair, 0, unroll=True)


def ffn_backward(dr, df, w_in, w_out, slope_ref, du_ref, bin_grad, dx):
    def hidden(cols):
        du = nt(df[...], w_out[cols, :]) * slope_ref[:, cols].astype(F32)
        bin_grad[0:1, cols] = jnp.sum(du, 0, keepdims=True)
        du_ref[:, cols] = du.astype(BF)

    blocks(256, FF, hidden)

    def pair(b, carry):
        rows = rows_of(b)
        dx[rows, :] = dr[rows, :] + nt(du_ref[rows, :], w_in[...])
        return carry

    lax.fori_loop(0, PAIRS, pair, 0, unroll=True)


def turn(src, cols, dst):
    dst[...] = jnp.transpose(src[:, cols])


def ffn_weight_grads(h_ref, du_ref, act_ref, df_ref, g, turned, base, inner_done):
    turn(h_ref, slice(None), turned)

    def inner(k, carry):
        for n in range(2):
            part = nn(turned[...], du_ref[:, pl.ds(pl.multiple_of(512 * k + 256 * n, 256), 256)])
            at = pl.ds(pl.multiple_of(base + 512 * (k // 2) + 256 * n, 256), 256)
            g[k % 2, :, at] = part.astype(BF)
        return carry

    lax.fori_loop(0, 4, inner, 0, unroll=True)
    inner_done()

    def outer(j, carry):
        turn(act_ref, pl.ds(pl.multiple_of(512 * j, 512), 512), turned)
        rows = pl.ds(pl.multiple_of(128 * j, 128), 128)
        for n in range(2):
            part = nn(turned[...], df_ref[:, 256 * n : 256 * n + 256]).reshape(16, 4, 8, 256)
            for k in range(4):
                at = base + 1024 + 512 * (k % 2) + 256 * n
                g[k // 2, rows, at : at + 256] = part[:, k].reshape(128, 256).astype(BF)
        return carry

    lax.fori_loop(0, 4, outer, 0, unroll=4)


def planes_first(part):
    wide = part.shape[-1]
    return part.reshape(4, 16, 8, wide).transpose(1, 0, 2, 3).reshape(512, wide)


def attn_weight_grads(h_ref, m_ref, o_ref, da_ref, dq_ref, dk_ref, dv_ref, g, turned, base, order):
    def product(side, at, right):
        for n in range(2):
            cols = slice(256 * n, 256 * n + 256)
            start = base + at + 256 * n
            g[side, :, start : start + 256] = order(nn(turned[...], right[:, cols])).astype(BF)

    turn(h_ref, slice(None), turned)
    product(0, 0, dq_ref)
    if m_ref is not h_ref:
        turn(m_ref, slice(None), turned)
    product(1, 0, dk_ref)
    product(0, 512, dv_ref)
    turn(o_ref, slice(None), turned)
    product(1, 512, da_ref)


def send_out(g, core, mine, theirs, sems):
    other = pltpu.make_async_copy(g.at[1 - core], theirs, sems.at[0])
    own = pltpu.make_async_copy(g.at[core], mine, sems.at[1])
    other.start()
    own.start()
    return other, own


class Moves:
    def __init__(self, sems):
        self.sems, self.used, self.open = sems, 0, []

    def start(self, src, dst):
        copy = pltpu.make_async_copy(src, dst, self.sems.at[self.used])
        self.used += 1
        copy.start()
        return copy

    def send(self, src, dst):
        self.open.append(self.start(src, dst))

    def finish(self):
        for copy in self.open:
            copy.wait()


def fetch_pair(moves, gathered, stage, pair, slot):
    return moves.start(gathered.at[:, pl.ds(512 * pair, 512)], stage.at[slot])


def forward_kernel(scalars, gathered, vec, bin_vec, src_h, tgt_h, og_h, *refs):
    (
        dec_h, grad_h,
        q0h, k0h, v0h, o0h, e0h, r0h, q1h, k1h, v1h, o1h, e1h, r1h, q2h, k2h, v2h, o2h, e2h, r2h,
        xh0h, xh1h, xh2h, xh3h, inv0h, inv1h, inv2h, inv3h,
        enc_h, mem_h, first_h, act0h, slope0h, mine, theirs, vec_grad, bin_grad,
        dec, grad_d2,
        q0, k0, v0, o0, e0, r0, q1, k1, v1, o1, e1, r1, q2, k2, v2, o2, e2, r2,
        xh0, xh1, xh2, xh3, inv0, inv1, inv2, inv3,
        enc, mem, first, act0, slope0,
        src, tgt, og, stage, w_attn, w_in, w_out, x32, second,
        act1, slope1, df, g, turned, sems,
    ) = refs
    moves = Moves(sems)
    pairs = {n: fetch_pair(moves, gathered, stage, n, n) for n in (0, 1)}
    src_in = moves.start(src_h, src)

    def bias(layer):
        return [vec[3 * layer + j : 3 * layer + j + 1, :] for j in range(3)]

    def gain(n):
        return vec[9 + n : 10 + n, :]

    def shift(n):
        return vec[14 + n : 15 + n, :]

    def source_keys(b):
        place = lax.broadcasted_iota(jnp.int32, (1, ROWS), 1)
        return jnp.where(place < scalars[b], 0.0, NEGATIVE)

    def target_keys(b):
        at_q = lax.broadcasted_iota(jnp.int32, (ROWS, ROWS), 0)
        at_k = lax.broadcasted_iota(jnp.int32, (ROWS, ROWS), 1)
        live = jnp.logical_and(at_q >= at_k, at_k < scalars[2 + b])
        return jnp.where(live, 0.0, NEGATIVE)

    def keeper(n, xh, inv_ref, low, wide):
        def after(rows, b, r):
            z, xhat, inv = norm_forward(r, gain(n), shift(n))
            xh[rows, :] = xhat.astype(BF)
            inv_ref[rows, :] = jnp.broadcast_to(inv, (ROWS, 128))
            low[rows, :] = z.astype(BF)
            if wide is not None:
                wide[rows, :] = z

        return after

    def from_low(ref):
        return lambda rows: ref[rows, :].astype(F32)

    def from_x32(rows):
        return x32[rows, :]

    src_in.wait()
    prep_attn(stage, 0, [pairs[0], pairs[1]], w_attn)
    for n in range(4):
        pairs[6 + n] = fetch_pair(moves, gathered, stage, 6 + n, 2 + n)
    tgt_in = moves.start(tgt_h, tgt)
    for n in (2, 3):
        pairs[n] = fetch_pair(moves, gathered, stage, n, 4 + n)
    og_in = moves.start(og_h, og)
    pairs[4] = fetch_pair(moves, gathered, stage, 4, 0)
    pairs[5] = fetch_pair(moves, gathered, stage, 5, 1)
    attn_forward(
        from_low(src), src, src, w_attn, bias(0), source_keys, q0, k0, v0, o0, e0, r0,
        keeper(0, xh0, inv0, enc, x32),
    )
    for a, b in ((q0, q0h), (k0, k0h), (v0, v0h), (o0, o0h), (e0, e0h), (r0, r0h),
                 (xh0, xh0h), (inv0, inv0h), (enc, enc_h)):
        moves.send(a, b)
    prep_ffn(stage, 2, [None, None] + [pairs[6 + n] for n in range(4)], w_in, w_out)
    for n in range(4):
        pairs[10 + n] = fetch_pair(moves, gathered, stage, 10 + n, 2 + n)
    ffn_forward(
        from_x32, enc, w_in, w_out, bin_vec.at[0:1], vec[19:20, :], act0, slope0,
        keeper(1, xh1, inv1, mem, None),
    )
    for a, b in ((xh1, xh1h), (inv1, inv1h), (mem, mem_h), (act0, act0h), (slope0, slope0h)):
        moves.send(a, b)
    tgt_in.wait()
    prep_attn(stage, 6, [None] * 6 + [pairs[2], pairs[3]], w_attn)
    attn_forward(
        from_low(tgt), tgt, tgt, w_attn, bias(1), target_keys, q1, k1, v1, o1, e1, r1,
        keeper(2, xh2, inv2, first, x32),
    )
    for a, b in ((q1, q1h), (k1, k1h), (v1, v1h), (o1, o1h), (e1, e1h), (r1, r1h),
                 (xh2, xh2h), (inv2, inv2h), (first, first_h)):
        moves.send(a, b)
    prep_attn(stage, 0, [pairs[4], pairs[5]], w_attn)
    attn_forward(
        from_x32, first, mem, w_attn, bias(2), source_keys, q2, k2, v2, o2, e2, r2,
        keeper(3, xh3, inv3, second, x32),
    )
    for a, b in ((q2, q2h), (k2, k2h), (v2, v2h), (o2, o2h), (e2, e2h), (r2, r2h),
                 (xh3, xh3h), (inv3, inv3h)):
        moves.send(a, b)
    prep_ffn(stage, 2, [None, None] + [pairs[10 + n] for n in range(4)], w_in, w_out)
    vec_grad[...] = jnp.zeros_like(vec_grad)
    bin_grad[...] = jnp.zeros_like(bin_grad)
    og_in.wait()

    def last(rows, b, r):
        z, xhat, inv = norm_forward(r, gain(4), shift(4))
        dec[rows, :] = z.astype(BF)
        at = lax.broadcasted_iota(jnp.int32, (ROWS, 1), 0)
        gz = jnp.where(at < scalars[2 + b], og[rows, :].astype(F32), 0.0)
        dr, d_gain, d_shift = norm_backward(gz, xhat, inv, gain(4))
        vec_grad[0:1, :] += d_gain
        vec_grad[1:2, :] += d_shift
        vec_grad[2:3, :] += jnp.sum(dr, 0, keepdims=True)
        df[rows, :] = dr.astype(BF)
        x32[rows, :] = dr

    ffn_forward(
        from_x32, second, w_in, w_out, bin_vec.at[1:2], vec[20:21, :], act1, slope1, last
    )
    moves.send(dec, dec_h)
    ffn_backward(x32, df, w_in, w_out, slope1, slope1, bin_grad, grad_d2)
    moves.send(grad_d2, grad_h)
    core = scalars[4]

    def inner_done():
        send_gradients(moves, g, core, mine, theirs, 0, 1024)

    ffn_weight_grads(second, slope1, act1, df, g, turned, 0, inner_done)
    send_gradients(moves, g, core, mine, theirs, 1024, 1024)
    moves.finish()


def norm_rows(vec_grad, grad, xh, inv, gain, low, wide):
    vec_grad[...] = jnp.zeros_like(vec_grad)

    def pair(b, carry):
        rows = rows_of(b)
        dr, d_gain, d_shift = norm_backward(
            grad[rows, :], xh[rows, :].astype(F32), inv[rows, 0:1], gain
        )
        vec_grad[0:1, :] += d_gain
        vec_grad[1:2, :] += d_shift
        vec_grad[2:3, :] += jnp.sum(dr, 0, keepdims=True)
        low[rows, :] = dr.astype(BF)
        wide[rows, :] = dr
        return carry

    lax.fori_loop(0, PAIRS, pair, 0, unroll=True)


def load_attn(moves, far_refs, near_refs):
    far_refs, near_refs = list(far_refs), list(near_refs)
    first = [moves.start(a, b) for a, b in zip(far_refs[:2], near_refs[:2])]
    heads = [moves.start(a, b) for a, b in zip(far_refs[2:8], near_refs[2:8])]
    rows = [moves.start(a, b) for a, b in zip(far_refs[8:], near_refs[8:])]
    return first, heads, rows


def attn_back(grad, data, weights, w, gain, temps, dx, grad_mem, g, base, vec_grad, copies, arrived, order):
    xh, inv, r, o, q, v, k, e, h = data[:9]
    m = data[9] if len(data) > 9 else h
    da, d_o, dq, dk, dv, turned = temps
    first, heads, rows_in = copies
    for copy in first:
        copy.wait()
    norm_rows(vec_grad, grad, xh, inv, gain, da, dx)
    weights()
    for n in range(2):
        cols = pl.ds(256 * n, 256)
        d_o[:, cols] = nt(da[...], w[3, cols, :]).astype(BF)
    for copy in heads:
        copy.wait()
    arrived()

    def body(b, carry):
        attn_backward(b, d_o, q, k, v, o, e, r, dq, dk, dv)
        rows = rows_of(b)
        vec_grad[3:4, :] += jnp.sum(dq[rows, :].astype(F32), 0, keepdims=True)
        vec_grad[4:5, :] += jnp.sum(dv[rows, :].astype(F32), 0, keepdims=True)
        to_m = nt(dk[rows, :], w[1]) + nt(dv[rows, :], w[2])
        to_x = dx[rows, :] + nt(dq[rows, :], w[0])
        if grad_mem is not None:
            grad_mem[rows, :] = to_m
            dx[rows, :] = to_x
        else:
            dx[rows, :] = to_x + to_m
        return carry

    lax.fori_loop(0, PAIRS, body, 0, unroll=True)
    for copy in rows_in:
        copy.wait()
    attn_weight_grads(h, m, o, da, dq, dk, dv, g, turned, base, order)


def send_gradients(moves, g, core, mine, theirs, at, size):
    cols = pl.ds(at, size)
    moves.send(g.at[1 - core, :, cols], theirs.at[:, cols])
    moves.send(g.at[core, :, cols], mine.at[:, cols])


def middle_kernel(scalars, gathered, vec, grad_h, *refs):
    far_attn, far_ffn = refs[:10], refs[10:15]
    d1_h, denc_h, mine, theirs, attn_vec, ffn_vec, bin_grad = refs[15:22]
    near_attn, near_ffn = refs[22:32], refs[32:37]
    grad, d1, denc, stage, w, w_in, w_out, da, d_o, dq, dk, dv, g, turned, sems = refs[37:]
    moves = Moves(sems)
    grad_in = moves.start(grad_h, grad)
    pairs = [fetch_pair(moves, gathered, stage, 4 + n, n) for n in range(2)]
    copies = load_attn(moves, far_attn, near_attn)
    xh1, inv1, slope, act, enc = near_ffn
    ffn_in = []

    def arrived():
        pairs.extend([fetch_pair(moves, gathered, stage, 6 + n, 2 + n) for n in range(4)])
        ffn_in.extend([moves.start(a, b) for a, b in zip(far_ffn, near_ffn)])

    bin_grad[...] = jnp.zeros_like(bin_grad)
    grad_in.wait()
    attn_back(
        grad, near_attn, lambda: prep_attn(stage, 0, pairs, w), w, vec[12:13, :],
        (da, d_o, dq, dk, dv, turned), d1, grad, g, 0, attn_vec, copies, arrived, lambda part: part,
    )
    core = scalars[4]
    send_gradients(moves, g, core, mine, theirs, 0, 1024)
    moves.send(d1, d1_h)
    for copy in ffn_in:
        copy.wait()
    norm_rows(ffn_vec, grad, xh1, inv1, vec[10:11, :], da, grad)
    prep_ffn(stage, 2, [None, None] + pairs[2:], w_in, w_out)
    ffn_backward(grad, da, w_in, w_out, slope, slope, bin_grad, denc)
    moves.send(denc, denc_h)

    def inner_done():
        send_gradients(moves, g, core, mine, theirs, 1024, 1024)

    ffn_weight_grads(enc, slope, act, da, g, turned, 1024, inner_done)
    send_gradients(moves, g, core, mine, theirs, 2048, 1024)
    moves.finish()


def write_vectors(attn, ffn, ffn_bins, g, at):
    rows = [attn[i][r : r + 1, :] for i in range(3) for r in (3, 4, 2)]
    order = (attn[0], ffn[0], attn[1], attn[2], ffn[1])
    rows += [a[0:1, :] for a in order] + [a[1:2, :] for a in order] + [f[2:3, :] for f in ffn]
    whole = jnp.concatenate(rows + [jnp.zeros((3, 512), F32)], axis=0)
    wide = jnp.concatenate([f[0:1, :] for f in ffn_bins] + [jnp.zeros((6, FF), F32)], axis=0)
    lane = lax.broadcasted_iota(jnp.int32, (8, 128), 1)
    tiles = []
    for p in [16 * x + yz for yz in range(16) for x in range(4)]:
        cols = slice(128 * (p // 16), 128 * (p // 16) + 128)
        tile = jnp.zeros((8, 128), F32)
        for n in range(3):
            turned = pltpu.roll(whole[8 * n : 8 * n + 8, cols], (8 * n - 8 * (p % 16)) % 128, 1)
            tile = jnp.where(lane // 8 == n, turned, tile)
        cols = slice(128 * (p // 4), 128 * (p // 4) + 128)
        turned = pltpu.roll(wide[:, cols], (32 - 32 * (p % 4)) % 128, 1)
        tiles.append(jnp.where(lane // 32 == 1, turned, tile))
    block = jnp.concatenate(tiles, axis=0).astype(BF)
    for side in range(2):
        g[side, :, at : at + 128] = block


def last_kernel(scalars, gathered, vec, a2_vec, f0_vec, f1_vec, f0_bin, f1_bin, *refs):
    far_data = [refs[10 * i : 10 * i + 10] for i in range(2)]
    dx_h, (mine, theirs) = refs[20:22], refs[22:24]
    near_data = [refs[24 + 10 * i : 34 + 10 * i] for i in range(2)]
    dx, vec_grad = refs[44:46], refs[46:48]
    stage, w, da, d_o, dq, dk, dv, g, turned, sems = refs[48:]
    moves = Moves(sems)
    grads, pairs, copies = [], [], []
    core = scalars[4]

    def start():
        i = len(grads)
        if i < 2:
            grads.append(moves.start(far_data[i][0], near_data[i][0]))
            slots = range(2 * i, 2 * i + 2)
            pairs.extend([fetch_pair(moves, gathered, stage, n, n) for n in slots])
            copies.append(load_attn(moves, far_data[i][1:], near_data[i][1:]))

    start()
    for i in range(2):
        norm = 9 + ATTN_NORMS[i]
        grads[i].wait()
        attn_back(
            near_data[i][0], near_data[i][1:], lambda: prep_attn(stage, 2 * i, pairs, w), w,
            vec[norm : norm + 1, :], (da, d_o, dq, dk, dv, turned), dx[i], None, g, 1024 * i,
            vec_grad[i], copies[i], start, planes_first,
        )
        if i == 1:
            write_vectors((*vec_grad, a2_vec), (f0_vec, f1_vec), (f0_bin, f1_bin), g, 2048)
        send_gradients(moves, g, core, mine, theirs, 1024 * i, 1024 + 128 * i)
        moves.send(dx[i], dx_h[i])
    moves.finish()


def spec(space):
    return pl.BlockSpec(memory_space=space)


def call(kernel, name, inputs, outs, scratch, after=()):
    taken = len(inputs)
    inputs = inputs + [(a, H) for a in after]

    def body(*refs):
        kernel(*refs[:taken], *refs[len(inputs) :])

    return pl.pallas_call(
        body,
        name=name,
        in_specs=[spec(s) for _, s in inputs],
        out_specs=[spec(s) for _, _, s in outs],
        out_shape=[jax.ShapeDtypeStruct(shape, kind) for shape, kind, _ in outs],
        scratch_shapes=scratch,
        compiler_params=pltpu.CompilerParams(vmem_limit_bytes=VMEM),
        cost_estimate=pl.CostEstimate(flops=10**10, bytes_accessed=10**7, transcendentals=0),
    )(*[a for a, _ in inputs])


V, H, S = pltpu.VMEM, pl.ANY, pltpu.SMEM
ROW = ((ALL, D), BF)
WIDE = ((ALL, FF), BF)
LINE = ((ALL, D), F32)
INV = ((ALL, 128), F32)
EXP = ((8 * PAIRS, ROWS, ROWS), BF)
VEC = ((8, D), F32, V)
BIN = ((8, FF), F32, V)


def far(kinds):
    return [(shape, kind, H) for shape, kind in kinds]


def near(kinds):
    return [V(shape, kind) for shape, kind in kinds]


def run_vectors(block):
    return call(vector_kernel, "vectors", [(block, V)], [((32, D), F32, V), BIN], [])


def run_forward(scalars, gathered, vec, bin_vec, src, tgt, og):
    kept = (
        [ROW, LINE] + [ROW, ROW, ROW, ROW, EXP, ROW] * 3 + [ROW] * 4 + [INV] * 4
        + [ROW] * 3 + [WIDE, WIDE]
    )
    outs = far(kept) + [((D, FF), BF, H)] * 2 + [VEC, BIN]
    scratch = near(kept) + near([ROW, ROW, ROW]) + [
        V((8, 1024, 512), BF), V((4, 512, 512), BF),
        V((D, FF), BF), V((FF, D), BF), V((ALL, D), F32), V((ALL, D), BF),
        V((ALL, FF), BF), V((ALL, FF), BF), V((ALL, D), BF),
        V((2, D, FF), BF), V((D, ALL), BF), pltpu.SemaphoreType.DMA((64,)),
    ]
    return call(
        forward_kernel, "forward",
        [(scalars, S), (gathered, H), (vec, V), (bin_vec, V), (src, H), (tgt, H), (og, H)], outs, scratch,
    )


ATTN_DATA = [ROW, INV, ROW, ROW, ROW, ROW, ROW, EXP, ROW]


def attn_data(xh, inv, heads, *rows):
    q, k, v, o, e, r = heads
    return [xh, inv, r, o, q, v, k, e, *rows]


def run_middle(scalars, gathered, vec, grad, attn, ffn, after=()):
    kinds = ATTN_DATA + [ROW] + [ROW, INV, WIDE, WIDE, ROW]
    inputs = [(scalars, S), (gathered, H), (vec, V)] + [(a, H) for a in (grad, *attn, *ffn)]
    outs = far([LINE, LINE]) + [((D, 3072), BF, H)] * 2 + [VEC, VEC, BIN]
    scratch = near(kinds) + near([LINE] * 3) + [
        V((6, 1024, 512), BF), V((4, 512, 512), BF), V((D, FF), BF), V((FF, D), BF),
        *near([ROW] * 5), V((2, D, 3072), BF), V((D, ALL), BF), pltpu.SemaphoreType.DMA((40,)),
    ]
    return call(middle_kernel, "middle", inputs, outs, scratch, after)


def run_last(scalars, gathered, vec, sums, data, after=()):
    kinds = ([LINE] + ATTN_DATA) * 2
    inputs = [(scalars, S), (gathered, H), (vec, V)]
    inputs += [(a, V) for a in sums] + [(a, H) for a in data]
    outs = far([LINE, LINE]) + [((D, 2176), BF, H)] * 2
    scratch = near(kinds) + near([LINE] * 2) + [V((8, D), F32), V((8, D), F32)] + [
        V((4, 1024, 512), BF), V((4, 512, 512), BF), *near([ROW] * 5), V((2, D, 2176), BF),
        V((D, ALL), BF), pltpu.SemaphoreType.DMA((40,)),
    ]
    return call(last_kernel, "last", inputs, outs, scratch, after)


def pack_shard(c, attn_proj, attn_out, attn_bias, norm_gain, norm_shift, ffn_in, ffn_out, b_in, b_out):
    attn = jnp.concatenate([attn_proj, attn_out[:, None]], axis=1).reshape(12, 4, 512)
    wide = ffn_in.reshape(2, 4, 4, 512).transpose(0, 2, 1, 3).reshape(8, 4, 512)
    both = lax.all_gather(jnp.concatenate([attn, wide]), "c", axis=1, tiled=True)
    half = lax.dynamic_index_in_dim(both.reshape(10, 2, 8, 512), c, 1, False)
    tall = ffn_out.reshape(2, 2, 8, 512)
    blocks = jnp.concatenate([half[:8], tall[0], half[8:], tall[1]])
    vec = [attn_bias.reshape(9, 4), norm_gain, norm_shift, b_out, jnp.zeros((3, 4), BF)]
    line = jnp.concatenate(vec + [b_in.reshape(8, 4)]).T.reshape(1, 128)
    return blocks.transpose(1, 0, 2).reshape(8, 7168), line


def swap(a):
    return lax.ppermute(a, "c", [(0, 1), (1, 0)])


def pair_sum(mine, theirs):
    return (mine.astype(F32) + swap(theirs).astype(F32)).astype(BF)


def ring_sum(whole):
    return lax.psum_scatter(whole, "x", scatter_dimension=0, tiled=True)


def plane_sum(whole):
    whole = whole.reshape(16, -1, whole.shape[1])
    whole = lax.all_to_all(whole, ("y", "z"), 0, 0, tiled=True)
    return jnp.sum(whole.astype(F32), axis=0)


def line_sum(whole):
    blocks = whole.reshape(4, 8, -1)
    x = lax.axis_index("x")
    total = lax.dynamic_index_in_dim(blocks, x, 0, False)
    for k in range(1, 4):
        part = lax.dynamic_index_in_dim(blocks, (x + k) % 4, 0, False).astype(BF)
        part = lax.ppermute(part, "x", [(i, (i + k) % 4) for i in range(4)])
        total = total + part.astype(F32)
    return total


def per_device(source, target, src_len, tgt_len, out_grad, *weights):
    c = lax.axis_index("c")
    shard, line = pack_shard(c, *weights)
    gathered = lax.all_gather(shard, AXES, axis=0, tiled=True)
    vec, bin_vec = run_vectors(lax.all_gather(line, AXES, axis=0, tiled=True))
    scalars = jnp.concatenate(
        [src_len.reshape(2), tgt_len.reshape(2), c.astype(jnp.int32)[None], jnp.zeros(3, jnp.int32)]
    )
    src, tgt, og = (a.reshape(ALL, D) for a in (source, target, out_grad))
    outs = run_forward(scalars, gathered, vec, bin_vec, src, tgt, og)
    dec, grad = outs[:2]
    heads = [outs[2 + 6 * i : 8 + 6 * i] for i in range(3)]
    xh, inv = outs[20:24], outs[24:28]
    enc, mem, first, act0, slope0, f1_mine, f1_theirs, f1_vec, f1_bin = outs[28:]
    f1 = pair_sum(f1_mine, f1_theirs)
    f1_x = ring_sum(f1)
    d1, d_enc, mid_mine, mid_theirs, a2_vec, f0_vec, f0_bin = run_middle(
        scalars, gathered, vec, grad, attn_data(xh[3], inv[3], heads[2], first, mem),
        [xh[1], inv[1], slope0, act0, enc], (f1,),
    )
    mid = pair_sum(mid_mine, mid_theirs)
    mid_x = ring_sum(mid)
    data = [d_enc, *attn_data(xh[0], inv[0], heads[0], src)]
    data += [d1, *attn_data(xh[2], inv[2], heads[1], tgt)]
    d_src, d_tgt, end_mine, end_theirs = run_last(
        scalars, gathered, vec, (a2_vec, f0_vec, f1_vec, f0_bin, f1_bin), data, (mid, f1_x)
    )
    end = plane_sum(pair_sum(end_mine, end_theirs))
    mid_x, end = lax.optimization_barrier((mid_x, end))
    sum_end = line_sum(end)
    sum_rest = plane_sum(jnp.concatenate([mid_x, f1_x], axis=1))

    cut = sum_end[:, 2048:]
    vecs = cut[:, :24].reshape(8, 3, 2, 4).transpose(1, 0, 2, 3).reshape(24, 2, 4)
    vecs = lax.dynamic_index_in_dim(vecs, c, 1, False)
    g_bin = lax.dynamic_index_in_dim(cut[:2, 32:64].reshape(2, 2, 16), c, 1, False)
    whole = jnp.concatenate([sum_end[:, :2048], sum_rest], axis=1)
    attn = whole[:, :3072].reshape(2, 4, 6, 512)
    wide = whole[:, 3072:].reshape(8, 2, 4, 512)
    rows = jnp.concatenate([attn, wide[:, :, :2].reshape(2, 4, 4, 512)], axis=2)
    keep = lax.dynamic_index_in_dim(rows, c, 0, False)
    got = swap(lax.dynamic_index_in_dim(rows, 1 - c, 0, False))
    first_half = jnp.where(c == 0, keep, got)
    second_half = jnp.where(c == 0, got, keep)
    a = first_half[:, :6].reshape(4, 3, 2, 512)
    b = second_half[:, :6].reshape(4, 3, 2, 512)
    g_proj = jnp.stack([a[:, :, 0], b[:, :, 0], a[:, :, 1]], axis=0).transpose(2, 0, 1, 3)
    g_out = b[:, :, 1].transpose(1, 0, 2)
    ia = first_half[:, 6:].reshape(4, 2, 2, 512)
    ib = second_half[:, 6:].reshape(4, 2, 2, 512)
    g_in = jnp.stack([ia, ib], axis=3).transpose(1, 0, 2, 3, 4).reshape(2, 4, 2048)
    g_wout = wide[:, :, 2:].transpose(1, 2, 0, 3).reshape(2, 16, 512)
    shape = source.shape
    return (
        dec.reshape(shape), d_src.reshape(shape), d_tgt.reshape(shape),
        g_proj, g_out, vecs[:9].reshape(3, 3, 4), vecs[9:14], vecs[14:19],
        g_in, g_wout, g_bin, vecs[19:21],
    )


def solution(mesh):
    mesh = Mesh(mesh.devices.reshape(4, 4, 4, 2), AXES)
    rows = P(None, AXES, None, None)
    lens = P(None, AXES)
    weights = (
        P(None, None, AXES, None), P(None, AXES, None), P(None, None, AXES), P(None, AXES),
        P(None, AXES), P(None, AXES, None), P(None, AXES, None), P(None, AXES), P(None, AXES),
    )
    return jax.shard_map(
        per_device,
        mesh=mesh,
        in_specs=(rows, rows, lens, lens, rows) + weights,
        out_specs=(rows, rows, rows) + weights,
        check_vma=False,
    )
```

```python
import functools

import jax
import jax.numpy as jnp
from jax import lax
from jax.experimental import pallas as pl
from jax.experimental.pallas import tpu as pltpu
from jax.sharding import Mesh
from jax.sharding import PartitionSpec as P

BF = jnp.bfloat16
F32 = jnp.float32
EPSILON = 1e-05
NEGATIVE = -1000000000.0
AXES = ("x", "y", "z", "c")
CHIPS = ("x", "y", "z")
ROWS = 256
PAIRS = 2
ALL = ROWS * PAIRS
D = 512
FF = 2048
VMEM = 61 * 1024 * 1024
ATTN_NORMS = (0, 2, 3)
FFN_NORMS = (1, 4)


def nn(a, b):
    return jnp.dot(a, b, preferred_element_type=F32)


def nt(a, b):
    return lax.dot_general(a, b, (((1,), (1,)), ((), ())), preferred_element_type=F32)


def tn(a, b):
    return lax.dot_general(a, b, (((0,), (0,)), ((), ())), preferred_element_type=F32)


def rows_of(b):
    return pl.ds(pl.multiple_of(b * ROWS, ROWS), ROWS)


def split_pair(stage, n, store_a, store_b):
    def body(i, carry):
        both = stage[n, pl.ds(pl.multiple_of(128 * i, 128), 128), :].astype(F32).reshape(8, 16, 512)
        rows = pl.ds(pl.multiple_of(64 * i, 64), 64)
        store_a(rows, both[:, :8].reshape(64, 512).astype(BF))
        store_b(rows, both[:, 8:].reshape(64, 512).astype(BF))
        return carry

    lax.fori_loop(0, 8, body, 0, unroll=8)


def prep_attn(stage, n, copies, dst):
    for half in range(2):
        copies[n + half].wait()

        def put(slot):
            def store(rows, value):
                dst[slot, rows, :] = value

            return store

        split_pair(stage, n + half, put(2 * half), put(2 * half + 1))


def prep_ffn(stage, n, copies, w_in, w_out):
    for half in range(2):
        copies[n + half].wait()

        def put(block):
            def store(rows, value):
                w_in[rows, 512 * block : 512 * block + 512] = value

            return store

        split_pair(stage, n + half, put(2 * half), put(2 * half + 1))
    copies[n + 2].wait()
    copies[n + 3].wait()

    def body(i, carry):
        span = pl.ds(pl.multiple_of(64 * i, 64), 64)
        first = stage[n + 2, span, :].astype(F32).reshape(4, 16, 512)
        second = stage[n + 3, span, :].astype(F32).reshape(4, 16, 512)
        whole = jnp.concatenate([first[:, :8], second[:, :8], first[:, 8:], second[:, 8:]], axis=1)
        w_out[pl.ds(pl.multiple_of(128 * i, 128), 128), :] = whole.reshape(128, 512).astype(BF)
        return carry

    lax.fori_loop(0, 16, body, 0, unroll=8)


def vector_kernel(block, vec, bin_vec):
    lines = block[...]
    turned = jnp.transpose(lines.astype(F32)).astype(BF)
    device = lax.broadcasted_iota(jnp.int32, (128, 512), 0)
    place = lax.broadcasted_iota(jnp.int32, (128, 512), 1)
    total = jnp.zeros((32, 512), F32)
    for e in range(4):
        spread = jnp.where(place == 4 * device + e, 1.0, 0.0).astype(BF)
        total = total + nn(turned[32 * e : 32 * e + 32], spread)
    vec[...] = total
    bin_vec[...] = jnp.zeros_like(bin_vec)
    for k in range(4):
        near_by = jnp.where((place + 512 * k) // 16 == device, 1.0, 0.0)
        for j in range(2):
            pick = jnp.where(device == 32 * (place % 4) + 24 + 4 * j + (place % 16) // 4, 1.0, 0.0)
            found = nn(lines, pick.astype(BF)) * near_by
            bin_vec[j : j + 1, 512 * k : 512 * k + 512] = jnp.sum(found, 0, keepdims=True)


def norm_forward(r, gain, shift):
    c = r - jnp.mean(r, -1, keepdims=True)
    inv = lax.rsqrt(jnp.mean(c * c, -1, keepdims=True) + EPSILON)
    xhat = c * inv
    return xhat * gain + shift, xhat, inv


def norm_backward(g, xhat, inv, gain):
    d_gain = jnp.sum(g * xhat, 0, keepdims=True)
    d_shift = jnp.sum(g, 0, keepdims=True)
    gs = g * gain
    dr = inv * (gs - jnp.mean(gs, -1, keepdims=True) - xhat * jnp.mean(gs * xhat, -1, keepdims=True))
    return dr, d_gain, d_shift


def low_half():
    return lax.broadcasted_iota(jnp.int32, (1, 128), 1) < 64


def blocks(size, total, body):
    def step(i, carry):
        body(pl.ds(pl.multiple_of(i * size, size), size))
        return carry

    lax.fori_loop(0, total // size, step, 0, unroll=8)


def attn_forward(x, h, m, w, biases, mask_of, q_ref, k_ref, v_ref, o_ref, e_ref, r_ref, after):
    for n in range(2):
        cols = pl.ds(256 * n, 256)
        part = slice(256 * n, 256 * n + 256)
        q_ref[:, cols] = ((nn(h[...], w[0, :, cols]) + biases[0][:, part]) * 0.125).astype(BF)
        k_ref[:, cols] = nn(m[...], w[1, :, cols]).astype(BF)
        v_ref[:, cols] = (nn(m[...], w[2, :, cols]) + biases[1][:, part]).astype(BF)
    low = low_half()

    def pair(b, carry):
        rows = rows_of(b)
        masked = mask_of(b)
        for j in range(4):
            cols = pl.ds(128 * j, 128)
            q = q_ref[rows, cols]
            k = k_ref[rows, cols]
            v = jnp.concatenate([v_ref[rows, cols], jnp.ones((ROWS, 128), BF)], axis=1)
            parts = []
            for half in range(2):
                mine = low if half == 0 else jnp.logical_not(low)
                s = nt(jnp.where(mine, q, jnp.zeros_like(q)), k) + masked
                e = jnp.exp(s - jnp.max(s, -1, keepdims=True)).astype(BF)
                e_ref[8 * b + 2 * j + half] = e
                parts.append(nn(e, v))
            r = 1.0 / jnp.where(low, parts[0][:, 128:], parts[1][:, 128:])
            r_ref[rows, cols] = r.astype(BF)
            o = jnp.where(low, parts[0][:, :128], parts[1][:, :128]) * r
            o_ref[rows, cols] = o.astype(BF)
        after(rows, b, x(rows) + (nn(o_ref[rows, :], w[3]) + biases[2]))
        return carry

    lax.fori_loop(0, PAIRS, pair, 0, unroll=True)


def attn_backward(b, d_o, q_ref, k_ref, v_ref, o_ref, e_ref, r_ref, dq_ref, dk_ref, dv_ref):
    rows = rows_of(b)
    low = low_half()
    for j in range(4):
        cols = pl.ds(128 * j, 128)
        q = q_ref[rows, cols]
        k = k_ref[rows, cols]
        v = v_ref[rows, cols]
        ds_o = d_o[rows, cols].astype(F32) * r_ref[rows, cols].astype(F32)
        prod = ds_o * o_ref[rows, cols].astype(F32)
        ds_o = ds_o.astype(BF)
        dqs, dks, dvs = [], [], []
        for half in range(2):
            mine = low if half == 0 else jnp.logical_not(low)
            delta = jnp.sum(jnp.where(mine, prod, 0.0), -1, keepdims=True)
            e = e_ref[8 * b + 2 * j + half]
            dp = nt(jnp.where(mine, ds_o, jnp.zeros_like(ds_o)), v)
            ds = (e.astype(F32) * (dp - delta)).astype(BF)
            dvs.append(tn(e, ds_o))
            dqs.append(nn(ds, k))
            dks.append(tn(ds, q))
        dq_ref[rows, cols] = (jnp.where(low, dqs[0], dqs[1]) * 0.125).astype(BF)
        dk_ref[rows, cols] = jnp.where(low, dks[0], dks[1]).astype(BF)
        dv_ref[rows, cols] = jnp.where(low, dvs[0], dvs[1]).astype(BF)


def gelu_both(u):
    c = 0.7978845608028654
    square = u * u
    t = jnp.tanh(c * u * (1.0 + 0.044715 * square))
    half = 0.5 * (1.0 + t)
    act = u * half
    slope = half + (0.5 * c) * u * (1.0 - t * t) * (1.0 + (3.0 * 0.044715) * square)
    return act, slope


def ffn_forward(x, h, w_in, w_out, b_in, b_out, act_ref, slope_ref, after):
    def hidden(cols):
        act, slope = gelu_both(nn(h[...], w_in[:, cols]) + b_in[:, cols])
        act_ref[:, cols] = act.astype(BF)
        slope_ref[:, cols] = slope.astype(BF)

    blocks(256, FF, hidden)

    def pair(b, carry):
        rows = rows_of(b)
        after(rows, b, x(rows) + (nn(act_ref[rows, :], w_out[...]) + b_out))
        return carry

    lax.fori_loop(0, PAIRS, pair, 0, unroll=True)


def ffn_backward(dr, df, w_in, w_out, slope_ref, du_ref, bin_grad, dx):
    def hidden(cols):
        du = nt(df[...], w_out[cols, :]) * slope_ref[:, cols].astype(F32)
        bin_grad[0:1, cols] = jnp.sum(du, 0, keepdims=True)
        du_ref[:, cols] = du.astype(BF)

    blocks(256, FF, hidden)

    def pair(b, carry):
        rows = rows_of(b)
        dx[rows, :] = dr[rows, :] + nt(du_ref[rows, :], w_in[...])
        return carry

    lax.fori_loop(0, PAIRS, pair, 0, unroll=True)


def turn(src, cols, dst):
    dst[...] = jnp.transpose(src[:, cols])


def ffn_weight_grads(h_ref, du_ref, act_ref, df_ref, g, turned, base, inner_done):
    turn(h_ref, slice(None), turned)

    def inner(k, carry):
        for n in range(2):
            part = nn(turned[...], du_ref[:, pl.ds(pl.multiple_of(512 * k + 256 * n, 256), 256)])
            at = pl.ds(pl.multiple_of(base + 512 * (k // 2) + 256 * n, 256), 256)
            g[k % 2, :, at] = part.astype(BF)
        return carry

    lax.fori_loop(0, 4, inner, 0, unroll=True)
    inner_done()

    def outer(j, carry):
        turn(act_ref, pl.ds(pl.multiple_of(512 * j, 512), 512), turned)
        rows = pl.ds(pl.multiple_of(128 * j, 128), 128)
        for n in range(2):
            part = nn(turned[...], df_ref[:, 256 * n : 256 * n + 256]).reshape(16, 4, 8, 256)
            for k in range(4):
                at = base + 1024 + 512 * (k % 2) + 256 * n
                g[k // 2, rows, at : at + 256] = part[:, k].reshape(128, 256).astype(BF)
        return carry

    lax.fori_loop(0, 4, outer, 0, unroll=4)


def planes_first(part):
    wide = part.shape[-1]
    return part.reshape(4, 16, 8, wide).transpose(1, 0, 2, 3).reshape(512, wide)


def as_is(part):
    return part


def attn_weight_grads(h_ref, m_ref, o_ref, da_ref, dq_ref, dk_ref, dv_ref, g, turned, base, order):
    def product(side, at, right):
        for n in range(2):
            cols = slice(256 * n, 256 * n + 256)
            start = base + at + 256 * n
            g[side, :, start : start + 256] = order(nn(turned[...], right[:, cols])).astype(BF)

    turn(h_ref, slice(None), turned)
    product(0, 0, dq_ref)
    if m_ref is not h_ref:
        turn(m_ref, slice(None), turned)
    product(1, 0, dk_ref)
    product(0, 512, dv_ref)
    turn(o_ref, slice(None), turned)
    product(1, 512, da_ref)


def send_out(g, core, mine, theirs, sems):
    other = pltpu.make_async_copy(g.at[1 - core], theirs, sems.at[0])
    own = pltpu.make_async_copy(g.at[core], mine, sems.at[1])
    other.start()
    own.start()
    return other, own


class Moves:
    def __init__(self, sems):
        self.sems, self.used, self.open = sems, 0, []

    def start(self, src, dst):
        copy = pltpu.make_async_copy(src, dst, self.sems.at[self.used])
        self.used += 1
        copy.start()
        return copy

    def send(self, src, dst):
        self.open.append(self.start(src, dst))

    def finish(self):
        for copy in self.open:
            copy.wait()


def fetch_pair(moves, gathered, stage, pair, slot):
    return moves.start(gathered.at[:, pl.ds(512 * pair, 512)], stage.at[slot])


def forward_kernel(scalars, gathered, vec, bin_vec, src_h, tgt_h, og_h, *refs):
    (
        dec_h, grad_h,
        q0h, k0h, v0h, o0h, e0h, r0h, q1h, k1h, v1h, o1h, e1h, r1h, q2h, k2h, v2h, o2h, e2h, r2h,
        xh0h, xh1h, xh2h, xh3h, inv0h, inv1h, inv2h, inv3h,
        enc_h, mem_h, first_h, act0h, slope0h, mine, theirs, vec_grad, bin_grad,
        dec, grad_d2,
        q0, k0, v0, o0, e0, r0, q1, k1, v1, o1, e1, r1, q2, k2, v2, o2, e2, r2,
        xh0, xh1, xh2, xh3, inv0, inv1, inv2, inv3,
        enc, mem, first, act0, slope0,
        src, tgt, og, stage, w_attn, w_in, w_out, x32, second,
        act1, slope1, df, g, turned, sems,
    ) = refs
    moves = Moves(sems)
    pairs = {n: fetch_pair(moves, gathered, stage, n, n) for n in (0, 1)}
    src_in = moves.start(src_h, src)

    def bias(layer):
        return [vec[3 * layer + j : 3 * layer + j + 1, :] for j in range(3)]

    def gain(n):
        return vec[9 + n : 10 + n, :]

    def shift(n):
        return vec[14 + n : 15 + n, :]

    def source_keys(b):
        place = lax.broadcasted_iota(jnp.int32, (1, ROWS), 1)
        return jnp.where(place < scalars[b], 0.0, NEGATIVE)

    def target_keys(b):
        at_q = lax.broadcasted_iota(jnp.int32, (ROWS, ROWS), 0)
        at_k = lax.broadcasted_iota(jnp.int32, (ROWS, ROWS), 1)
        live = jnp.logical_and(at_q >= at_k, at_k < scalars[2 + b])
        return jnp.where(live, 0.0, NEGATIVE)

    def keeper(n, xh, inv_ref, low, wide):
        def after(rows, b, r):
            z, xhat, inv = norm_forward(r, gain(n), shift(n))
            xh[rows, :] = xhat.astype(BF)
            inv_ref[rows, :] = jnp.broadcast_to(inv, (ROWS, 128))
            low[rows, :] = z.astype(BF)
            if wide is not None:
                wide[rows, :] = z

        return after

    def from_low(ref):
        return lambda rows: ref[rows, :].astype(F32)

    def from_x32(rows):
        return x32[rows, :]

    src_in.wait()
    prep_attn(stage, 0, [pairs[0], pairs[1]], w_attn)
    for n in range(4):
        pairs[6 + n] = fetch_pair(moves, gathered, stage, 6 + n, 2 + n)
    tgt_in = moves.start(tgt_h, tgt)
    for n in (2, 3):
        pairs[n] = fetch_pair(moves, gathered, stage, n, 4 + n)
    og_in = moves.start(og_h, og)
    pairs[4] = fetch_pair(moves, gathered, stage, 4, 0)
    pairs[5] = fetch_pair(moves, gathered, stage, 5, 1)
    attn_forward(
        from_low(src), src, src, w_attn, bias(0), source_keys, q0, k0, v0, o0, e0, r0,
        keeper(0, xh0, inv0, enc, x32),
    )
    for a, b in ((q0, q0h), (k0, k0h), (v0, v0h), (o0, o0h), (e0, e0h), (r0, r0h),
                 (xh0, xh0h), (inv0, inv0h), (enc, enc_h)):
        moves.send(a, b)
    prep_ffn(stage, 2, [None, None] + [pairs[6 + n] for n in range(4)], w_in, w_out)
    for n in range(4):
        pairs[10 + n] = fetch_pair(moves, gathered, stage, 10 + n, 2 + n)
    ffn_forward(
        from_x32, enc, w_in, w_out, bin_vec.at[0:1], vec[19:20, :], act0, slope0,
        keeper(1, xh1, inv1, mem, None),
    )
    for a, b in ((xh1, xh1h), (inv1, inv1h), (mem, mem_h), (act0, act0h), (slope0, slope0h)):
        moves.send(a, b)
    tgt_in.wait()
    prep_attn(stage, 6, [None] * 6 + [pairs[2], pairs[3]], w_attn)
    attn_forward(
        from_low(tgt), tgt, tgt, w_attn, bias(1), target_keys, q1, k1, v1, o1, e1, r1,
        keeper(2, xh2, inv2, first, x32),
    )
    for a, b in ((q1, q1h), (k1, k1h), (v1, v1h), (o1, o1h), (e1, e1h), (r1, r1h),
                 (xh2, xh2h), (inv2, inv2h), (first, first_h)):
        moves.send(a, b)
    prep_attn(stage, 0, [pairs[4], pairs[5]], w_attn)
    attn_forward(
        from_x32, first, mem, w_attn, bias(2), source_keys, q2, k2, v2, o2, e2, r2,
        keeper(3, xh3, inv3, second, x32),
    )
    for a, b in ((q2, q2h), (k2, k2h), (v2, v2h), (o2, o2h), (e2, e2h), (r2, r2h),
                 (xh3, xh3h), (inv3, inv3h)):
        moves.send(a, b)
    prep_ffn(stage, 2, [None, None] + [pairs[10 + n] for n in range(4)], w_in, w_out)
    vec_grad[...] = jnp.zeros_like(vec_grad)
    bin_grad[...] = jnp.zeros_like(bin_grad)
    og_in.wait()

    def last(rows, b, r):
        z, xhat, inv = norm_forward(r, gain(4), shift(4))
        dec[rows, :] = z.astype(BF)
        at = lax.broadcasted_iota(jnp.int32, (ROWS, 1), 0)
        gz = jnp.where(at < scalars[2 + b], og[rows, :].astype(F32), 0.0)
        dr, d_gain, d_shift = norm_backward(gz, xhat, inv, gain(4))
        vec_grad[0:1, :] += d_gain
        vec_grad[1:2, :] += d_shift
        vec_grad[2:3, :] += jnp.sum(dr, 0, keepdims=True)
        df[rows, :] = dr.astype(BF)
        x32[rows, :] = dr

    ffn_forward(
        from_x32, second, w_in, w_out, bin_vec.at[1:2], vec[20:21, :], act1, slope1, last
    )
    moves.send(dec, dec_h)
    ffn_backward(x32, df, w_in, w_out, slope1, slope1, bin_grad, grad_d2)
    moves.send(grad_d2, grad_h)
    core = scalars[4]

    def inner_done():
        send_gradients(moves, g, core, mine, theirs, 0, 1024)

    ffn_weight_grads(second, slope1, act1, df, g, turned, 0, inner_done)
    send_gradients(moves, g, core, mine, theirs, 1024, 1024)
    moves.finish()


def norm_rows(vec_grad, grad, xh, inv, gain, low, wide):
    vec_grad[...] = jnp.zeros_like(vec_grad)

    def pair(b, carry):
        rows = rows_of(b)
        dr, d_gain, d_shift = norm_backward(
            grad[rows, :], xh[rows, :].astype(F32), inv[rows, 0:1], gain
        )
        vec_grad[0:1, :] += d_gain
        vec_grad[1:2, :] += d_shift
        vec_grad[2:3, :] += jnp.sum(dr, 0, keepdims=True)
        low[rows, :] = dr.astype(BF)
        wide[rows, :] = dr
        return carry

    lax.fori_loop(0, PAIRS, pair, 0, unroll=True)


def load_attn(moves, far_refs, near_refs):
    far_refs, near_refs = list(far_refs), list(near_refs)
    first = [moves.start(a, b) for a, b in zip(far_refs[:2], near_refs[:2])]
    heads = [moves.start(a, b) for a, b in zip(far_refs[2:8], near_refs[2:8])]
    rows = [moves.start(a, b) for a, b in zip(far_refs[8:], near_refs[8:])]
    return first, heads, rows


def attn_back(grad, data, weights, w, gain, temps, dx, grad_mem, g, base, vec_grad, copies, arrived, order):
    xh, inv, r, o, q, v, k, e, h = data[:9]
    m = data[9] if len(data) > 9 else h
    da, d_o, dq, dk, dv, turned = temps
    first, heads, rows_in = copies
    for copy in first:
        copy.wait()
    norm_rows(vec_grad, grad, xh, inv, gain, da, dx)
    weights()
    for n in range(2):
        cols = pl.ds(256 * n, 256)
        d_o[:, cols] = nt(da[...], w[3, cols, :]).astype(BF)
    for copy in heads:
        copy.wait()
    arrived()

    def body(b, carry):
        attn_backward(b, d_o, q, k, v, o, e, r, dq, dk, dv)
        rows = rows_of(b)
        vec_grad[3:4, :] += jnp.sum(dq[rows, :].astype(F32), 0, keepdims=True)
        vec_grad[4:5, :] += jnp.sum(dv[rows, :].astype(F32), 0, keepdims=True)
        to_m = nt(dk[rows, :], w[1]) + nt(dv[rows, :], w[2])
        to_x = dx[rows, :] + nt(dq[rows, :], w[0])
        if grad_mem is not None:
            grad_mem[rows, :] = to_m
            dx[rows, :] = to_x
        else:
            dx[rows, :] = to_x + to_m
        return carry

    lax.fori_loop(0, PAIRS, body, 0, unroll=True)
    for copy in rows_in:
        copy.wait()
    attn_weight_grads(h, m, o, da, dq, dk, dv, g, turned, base, order)


def send_gradients(moves, g, core, mine, theirs, at, size):
    cols = pl.ds(at, size)
    moves.send(g.at[1 - core, :, cols], theirs.at[:, cols])
    moves.send(g.at[core, :, cols], mine.at[:, cols])


def middle_kernel(scalars, gathered, vec, grad_h, *refs):
    far_cross, far_self, far_ffn = refs[:10], refs[10:19], refs[19:24]
    dtgt_h, denc_h, mine, theirs, cross_vec, self_vec, ffn_vec, bin_grad = refs[24:32]
    near_cross, near_self, near_ffn = refs[32:42], refs[42:51], refs[51:56]
    grad, d1, dtgt, denc, stage, w, w_in, w_out, da, d_o, dq, dk, dv, g, turned, sems = refs[56:]
    moves = Moves(sems)
    core = scalars[4]
    temps = (da, d_o, dq, dk, dv, turned)
    grad_in = moves.start(grad_h, grad)
    cross_pairs = [fetch_pair(moves, gathered, stage, 4 + n, n) for n in range(2)]
    cross_copies = load_attn(moves, far_cross, near_cross)
    self_pairs, self_copies, ffn_pairs, ffn_in = [], [], [None, None], []

    def then_self():
        self_pairs.extend([fetch_pair(moves, gathered, stage, 2 + n, 6 + n) for n in range(2)])
        self_copies.extend(load_attn(moves, far_self, near_self))

    def then_ffn():
        ffn_pairs.extend([fetch_pair(moves, gathered, stage, 6 + n, 2 + n) for n in range(4)])
        ffn_in.extend([moves.start(a, b) for a, b in zip(far_ffn, near_ffn)])

    bin_grad[...] = jnp.zeros_like(bin_grad)
    grad_in.wait()
    attn_back(
        grad, near_cross, lambda: prep_attn(stage, 0, cross_pairs, w), w, vec[12:13, :], temps,
        d1, grad, g, 0, cross_vec, cross_copies, then_self, as_is,
    )
    send_gradients(moves, g, core, mine, theirs, 0, 1024)
    attn_back(
        d1, near_self, lambda: prep_attn(stage, 6, [None] * 6 + self_pairs, w), w, vec[11:12, :],
        temps, dtgt, None, g, 1024, self_vec, self_copies, then_ffn, as_is,
    )
    send_gradients(moves, g, core, mine, theirs, 1024, 1024)
    moves.send(dtgt, dtgt_h)
    for copy in ffn_in:
        copy.wait()
    xh1, inv1, slope, act, enc = near_ffn
    norm_rows(ffn_vec, grad, xh1, inv1, vec[10:11, :], da, grad)
    prep_ffn(stage, 2, ffn_pairs, w_in, w_out)
    ffn_backward(grad, da, w_in, w_out, slope, slope, bin_grad, denc)
    moves.send(denc, denc_h)

    def inner_done():
        send_gradients(moves, g, core, mine, theirs, 2048, 1024)

    ffn_weight_grads(enc, slope, act, da, g, turned, 2048, inner_done)
    send_gradients(moves, g, core, mine, theirs, 3072, 1024)
    moves.finish()


def write_vectors(attn, ffn, ffn_bins, g, at):
    rows = [attn[i][r : r + 1, :] for i in range(3) for r in (3, 4, 2)]
    order = (attn[0], ffn[0], attn[1], attn[2], ffn[1])
    rows += [a[0:1, :] for a in order] + [a[1:2, :] for a in order] + [f[2:3, :] for f in ffn]
    whole = jnp.concatenate(rows + [jnp.zeros((3, 512), F32)], axis=0)
    wide = jnp.concatenate([f[0:1, :] for f in ffn_bins] + [jnp.zeros((6, FF), F32)], axis=0)
    lane = lax.broadcasted_iota(jnp.int32, (8, 128), 1)
    tiles = []
    for p in [16 * x + yz for yz in range(16) for x in range(4)]:
        cols = slice(128 * (p // 16), 128 * (p // 16) + 128)
        tile = jnp.zeros((8, 128), F32)
        for n in range(3):
            turned = pltpu.roll(whole[8 * n : 8 * n + 8, cols], (8 * n - 8 * (p % 16)) % 128, 1)
            tile = jnp.where(lane // 8 == n, turned, tile)
        cols = slice(128 * (p // 4), 128 * (p // 4) + 128)
        turned = pltpu.roll(wide[:, cols], (32 - 32 * (p % 4)) % 128, 1)
        tiles.append(jnp.where(lane // 32 == 1, turned, tile))
    block = jnp.concatenate(tiles, axis=0).astype(BF)
    for side in range(2):
        g[side, :, at : at + 128] = block


def last_kernel(scalars, gathered, vec, a1_vec, a2_vec, f0_vec, f1_vec, f0_bin, f1_bin, *refs):
    far_data, (dx_h, mine, theirs), near_data = refs[:10], refs[10:13], refs[13:23]
    dx, vec_grad, stage, w, da, d_o, dq, dk, dv, g, turned, sems = refs[23:]
    moves = Moves(sems)
    grad_in = moves.start(far_data[0], near_data[0])
    pairs = [fetch_pair(moves, gathered, stage, n, n) for n in range(2)]
    copies = load_attn(moves, far_data[1:], near_data[1:])
    grad_in.wait()
    attn_back(
        near_data[0], near_data[1:], lambda: prep_attn(stage, 0, pairs, w), w, vec[9:10, :],
        (da, d_o, dq, dk, dv, turned), dx, None, g, 0, vec_grad, copies, lambda: None, planes_first,
    )
    write_vectors((vec_grad, a1_vec, a2_vec), (f0_vec, f1_vec), (f0_bin, f1_bin), g, 1024)
    send_gradients(moves, g, scalars[4], mine, theirs, 0, 1152)
    moves.send(dx, dx_h)
    moves.finish()


def spec(space):
    return pl.BlockSpec(memory_space=space)


def call(kernel, name, inputs, outs, scratch, after=()):
    taken = len(inputs)
    inputs = inputs + [(a, H) for a in after]

    def body(*refs):
        kernel(*refs[:taken], *refs[len(inputs) :])

    return pl.pallas_call(
        body,
        name=name,
        in_specs=[spec(s) for _, s in inputs],
        out_specs=[spec(s) for _, _, s in outs],
        out_shape=[jax.ShapeDtypeStruct(shape, kind) for shape, kind, _ in outs],
        scratch_shapes=scratch,
        compiler_params=pltpu.CompilerParams(vmem_limit_bytes=VMEM),
        cost_estimate=pl.CostEstimate(flops=10**10, bytes_accessed=10**7, transcendentals=0),
    )(*[a for a, _ in inputs])


V, H, S = pltpu.VMEM, pl.ANY, pltpu.SMEM
ROW = ((ALL, D), BF)
WIDE = ((ALL, FF), BF)
LINE = ((ALL, D), F32)
INV = ((ALL, 128), F32)
EXP = ((8 * PAIRS, ROWS, ROWS), BF)
VEC = ((8, D), F32, V)
BIN = ((8, FF), F32, V)


def far(kinds):
    return [(shape, kind, H) for shape, kind in kinds]


def near(kinds):
    return [V(shape, kind) for shape, kind in kinds]


def run_vectors(block):
    return call(vector_kernel, "vectors", [(block, V)], [((32, D), F32, V), BIN], [])


def run_forward(scalars, gathered, vec, bin_vec, src, tgt, og):
    kept = (
        [ROW, LINE] + [ROW, ROW, ROW, ROW, EXP, ROW] * 3 + [ROW] * 4 + [INV] * 4
        + [ROW] * 3 + [WIDE, WIDE]
    )
    outs = far(kept) + [((D, FF), BF, H)] * 2 + [VEC, BIN]
    scratch = near(kept) + near([ROW, ROW, ROW]) + [
        V((8, 1024, 512), BF), V((4, 512, 512), BF),
        V((D, FF), BF), V((FF, D), BF), V((ALL, D), F32), V((ALL, D), BF),
        V((ALL, FF), BF), V((ALL, FF), BF), V((ALL, D), BF),
        V((2, D, FF), BF), V((D, ALL), BF), pltpu.SemaphoreType.DMA((64,)),
    ]
    return call(
        forward_kernel, "forward",
        [(scalars, S), (gathered, H), (vec, V), (bin_vec, V), (src, H), (tgt, H), (og, H)], outs, scratch,
    )


ATTN_DATA = [ROW, INV, ROW, ROW, ROW, ROW, ROW, EXP, ROW]


def attn_data(xh, inv, heads, *rows):
    q, k, v, o, e, r = heads
    return [xh, inv, r, o, q, v, k, e, *rows]


def run_middle(scalars, gathered, vec, grad, cross, own, ffn, after=()):
    kinds = ATTN_DATA + [ROW] + ATTN_DATA + [ROW, INV, WIDE, WIDE, ROW]
    inputs = [(scalars, S), (gathered, H), (vec, V)]
    inputs += [(a, H) for a in (grad, *cross, *own, *ffn)]
    outs = far([LINE, LINE]) + [((D, 4096), BF, H)] * 2 + [VEC, VEC, VEC, BIN]
    scratch = near(kinds) + near([LINE] * 4) + [
        V((8, 1024, 512), BF), V((4, 512, 512), BF), V((D, FF), BF), V((FF, D), BF),
        *near([ROW] * 5), V((2, D, 4096), BF), V((D, ALL), BF), pltpu.SemaphoreType.DMA((56,)),
    ]
    return call(middle_kernel, "middle", inputs, outs, scratch, after)


def run_last(scalars, gathered, vec, sums, data, after=()):
    kinds = [LINE] + ATTN_DATA
    inputs = [(scalars, S), (gathered, H), (vec, V)]
    inputs += [(a, V) for a in sums] + [(a, H) for a in data]
    outs = far([LINE]) + [((D, 1152), BF, H)] * 2
    scratch = near(kinds) + near([LINE]) + [
        V((8, D), F32), V((2, 1024, 512), BF), V((4, 512, 512), BF), *near([ROW] * 5),
        V((2, D, 1152), BF), V((D, ALL), BF), pltpu.SemaphoreType.DMA((24,)),
    ]
    return call(last_kernel, "last", inputs, outs, scratch, after)


def pack_shard(c, attn_proj, attn_out, attn_bias, norm_gain, norm_shift, ffn_in, ffn_out, b_in, b_out):
    attn = jnp.concatenate([attn_proj, attn_out[:, None]], axis=1).reshape(12, 4, 512)
    wide = ffn_in.reshape(2, 4, 4, 512).transpose(0, 2, 1, 3).reshape(8, 4, 512)
    both = lax.all_gather(jnp.concatenate([attn, wide]), "c", axis=1, tiled=True)
    half = lax.dynamic_index_in_dim(both.reshape(10, 2, 8, 512), c, 1, False)
    tall = ffn_out.reshape(2, 2, 8, 512)
    blocks = jnp.concatenate([half[:8], tall[0], half[8:], tall[1]])
    vec = [attn_bias.reshape(9, 4), norm_gain, norm_shift, b_out, jnp.zeros((3, 4), BF)]
    line = jnp.concatenate(vec + [b_in.reshape(8, 4)]).T.reshape(1, 128)
    return blocks.transpose(1, 0, 2).reshape(8, 7168), line


def swap(a):
    return lax.ppermute(a, "c", [(0, 1), (1, 0)])


def pair_sum(mine, theirs):
    return (mine.astype(F32) + swap(theirs).astype(F32)).astype(BF)


def ring_sum(whole):
    return lax.psum_scatter(whole, "x", scatter_dimension=0, tiled=True)


def plane_sum(whole):
    whole = whole.reshape(16, -1, whole.shape[1])
    whole = lax.all_to_all(whole, ("y", "z"), 0, 0, tiled=True)
    return jnp.sum(whole.astype(F32), axis=0)


def line_sum(whole):
    blocks = whole.reshape(4, 8, -1)
    x = lax.axis_index("x")
    total = lax.dynamic_index_in_dim(blocks, x, 0, False)
    for k in range(1, 4):
        part = lax.dynamic_index_in_dim(blocks, (x + k) % 4, 0, False).astype(BF)
        part = lax.ppermute(part, "x", [(i, (i + k) % 4) for i in range(4)])
        total = total + part.astype(F32)
    return total


def per_device(source, target, src_len, tgt_len, out_grad, *weights):
    c = lax.axis_index("c")
    shard, line = pack_shard(c, *weights)
    gathered = lax.all_gather(shard, AXES, axis=0, tiled=True)
    vec, bin_vec = run_vectors(lax.all_gather(line, AXES, axis=0, tiled=True))
    scalars = jnp.concatenate(
        [src_len.reshape(2), tgt_len.reshape(2), c.astype(jnp.int32)[None], jnp.zeros(3, jnp.int32)]
    )
    src, tgt, og = (a.reshape(ALL, D) for a in (source, target, out_grad))
    outs = run_forward(scalars, gathered, vec, bin_vec, src, tgt, og)
    dec, grad = outs[:2]
    heads = [outs[2 + 6 * i : 8 + 6 * i] for i in range(3)]
    xh, inv = outs[20:24], outs[24:28]
    enc, mem, first, act0, slope0, f1_mine, f1_theirs, f1_vec, f1_bin = outs[28:]
    f1 = pair_sum(f1_mine, f1_theirs)
    f1_x = ring_sum(f1)
    d_tgt, d_enc, mid_mine, mid_theirs, a2_vec, a1_vec, f0_vec, f0_bin = run_middle(
        scalars, gathered, vec, grad, attn_data(xh[3], inv[3], heads[2], first, mem),
        attn_data(xh[2], inv[2], heads[1], tgt), [xh[1], inv[1], slope0, act0, enc], (f1,),
    )
    f1_x, mid_mine = lax.optimization_barrier((f1_x, mid_mine))
    mid = pair_sum(mid_mine, mid_theirs)
    mid_x = ring_sum(mid)
    d_src, end_mine, end_theirs = run_last(
        scalars, gathered, vec, (a1_vec, a2_vec, f0_vec, f1_vec, f0_bin, f1_bin),
        [d_enc, *attn_data(xh[0], inv[0], heads[0], src)], (mid,),
    )
    end = plane_sum(pair_sum(end_mine, end_theirs))
    f1_x, end = lax.optimization_barrier((f1_x, end))
    sum_f1 = plane_sum(f1_x)
    mid_x, sum_f1 = lax.optimization_barrier((mid_x, sum_f1))
    sum_mid = plane_sum(mid_x)
    sum_end = line_sum(end)

    cut = sum_end[:, 1024:]
    vecs = cut[:, :24].reshape(8, 3, 2, 4).transpose(1, 0, 2, 3).reshape(24, 2, 4)
    vecs = lax.dynamic_index_in_dim(vecs, c, 1, False)
    g_bin = lax.dynamic_index_in_dim(cut[:2, 32:64].reshape(2, 2, 16), c, 1, False)
    whole = jnp.concatenate([sum_end[:, :1024], sum_mid[:, 1024:2048], sum_mid[:, :1024], sum_mid[:, 2048:], sum_f1], axis=1)
    attn = whole[:, :3072].reshape(2, 4, 6, 512)
    wide = whole[:, 3072:].reshape(8, 2, 4, 512)
    rows = jnp.concatenate([attn, wide[:, :, :2].reshape(2, 4, 4, 512)], axis=2)
    keep = lax.dynamic_index_in_dim(rows, c, 0, False)
    got = swap(lax.dynamic_index_in_dim(rows, 1 - c, 0, False))
    first_half = jnp.where(c == 0, keep, got)
    second_half = jnp.where(c == 0, got, keep)
    a = first_half[:, :6].reshape(4, 3, 2, 512)
    b = second_half[:, :6].reshape(4, 3, 2, 512)
    g_proj = jnp.stack([a[:, :, 0], b[:, :, 0], a[:, :, 1]], axis=0).transpose(2, 0, 1, 3)
    g_out = b[:, :, 1].transpose(1, 0, 2)
    ia = first_half[:, 6:].reshape(4, 2, 2, 512)
    ib = second_half[:, 6:].reshape(4, 2, 2, 512)
    g_in = jnp.stack([ia, ib], axis=3).transpose(1, 0, 2, 3, 4).reshape(2, 4, 2048)
    g_wout = wide[:, :, 2:].transpose(1, 2, 0, 3).reshape(2, 16, 512)
    shape = source.shape
    return (
        dec.reshape(shape), d_src.reshape(shape), d_tgt.reshape(shape),
        g_proj, g_out, vecs[:9].reshape(3, 3, 4), vecs[9:14], vecs[14:19],
        g_in, g_wout, g_bin, vecs[19:21],
    )


def solution(mesh):
    mesh = Mesh(mesh.devices.reshape(4, 4, 4, 2), AXES)
    rows = P(None, AXES, None, None)
    lens = P(None, AXES)
    weights = (
        P(None, None, AXES, None), P(None, AXES, None), P(None, None, AXES), P(None, AXES),
        P(None, AXES), P(None, AXES, None), P(None, AXES, None), P(None, AXES), P(None, AXES),
    )
    return jax.shard_map(
        per_device,
        mesh=mesh,
        in_specs=(rows, rows, lens, lens, rows) + weights,
        out_specs=(rows, rows, rows) + weights,
        check_vma=False,
    )
```

```python
import functools

import jax
import jax.numpy as jnp
from jax import lax
from jax.experimental import pallas as pl
from jax.experimental.pallas import tpu as pltpu
from jax.sharding import Mesh
from jax.sharding import PartitionSpec as P

BF = jnp.bfloat16
F32 = jnp.float32
EPSILON = 1e-05
NEGATIVE = -1000000000.0
AXES = ("x", "y", "z", "c")
CHIPS = ("x", "y", "z")
ROWS = 256
PAIRS = 2
ALL = ROWS * PAIRS
D = 512
FF = 2048
VMEM = 61 * 1024 * 1024
ATTN_NORMS = (0, 2, 3)
FFN_NORMS = (1, 4)


def nn(a, b):
    return jnp.dot(a, b, preferred_element_type=F32)


def nt(a, b):
    return lax.dot_general(a, b, (((1,), (1,)), ((), ())), preferred_element_type=F32)


def tn(a, b):
    return lax.dot_general(a, b, (((0,), (0,)), ((), ())), preferred_element_type=F32)


def rows_of(b):
    return pl.ds(pl.multiple_of(b * ROWS, ROWS), ROWS)


def split_pair(stage, n, store_a, store_b):
    def body(i, carry):
        both = stage[n, pl.ds(pl.multiple_of(128 * i, 128), 128), :].astype(F32).reshape(8, 16, 512)
        rows = pl.ds(pl.multiple_of(64 * i, 64), 64)
        store_a(rows, both[:, :8].reshape(64, 512).astype(BF))
        store_b(rows, both[:, 8:].reshape(64, 512).astype(BF))
        return carry

    lax.fori_loop(0, 8, body, 0, unroll=8)


def prep_attn(stage, n, copies, dst):
    for half in range(2):
        copies[n + half].wait()

        def put(slot):
            def store(rows, value):
                dst[slot, rows, :] = value

            return store

        split_pair(stage, n + half, put(2 * half), put(2 * half + 1))


def prep_ffn(stage, n, copies, w_in, w_out):
    for half in range(2):
        copies[n + half].wait()

        def put(block):
            def store(rows, value):
                w_in[rows, 512 * block : 512 * block + 512] = value

            return store

        split_pair(stage, n + half, put(2 * half), put(2 * half + 1))
    copies[n + 2].wait()
    copies[n + 3].wait()

    def body(i, carry):
        span = pl.ds(pl.multiple_of(64 * i, 64), 64)
        first = stage[n + 2, span, :].astype(F32).reshape(4, 16, 512)
        second = stage[n + 3, span, :].astype(F32).reshape(4, 16, 512)
        whole = jnp.concatenate([first[:, :8], second[:, :8], first[:, 8:], second[:, 8:]], axis=1)
        w_out[pl.ds(pl.multiple_of(128 * i, 128), 128), :] = whole.reshape(128, 512).astype(BF)
        return carry

    lax.fori_loop(0, 16, body, 0, unroll=8)


def vector_kernel(block, vec, bin_vec):
    lines = block[...]
    turned = jnp.transpose(lines.astype(F32)).astype(BF)
    device = lax.broadcasted_iota(jnp.int32, (128, 512), 0)
    place = lax.broadcasted_iota(jnp.int32, (128, 512), 1)
    total = jnp.zeros((32, 512), F32)
    for e in range(4):
        spread = jnp.where(place == 4 * device + e, 1.0, 0.0).astype(BF)
        total = total + nn(turned[32 * e : 32 * e + 32], spread)
    vec[...] = total
    bin_vec[...] = jnp.zeros_like(bin_vec)
    for k in range(4):
        near_by = jnp.where((place + 512 * k) // 16 == device, 1.0, 0.0)
        for j in range(2):
            pick = jnp.where(device == 32 * (place % 4) + 24 + 4 * j + (place % 16) // 4, 1.0, 0.0)
            found = nn(lines, pick.astype(BF)) * near_by
            bin_vec[j : j + 1, 512 * k : 512 * k + 512] = jnp.sum(found, 0, keepdims=True)


def norm_forward(r, gain, shift):
    c = r - jnp.mean(r, -1, keepdims=True)
    inv = lax.rsqrt(jnp.mean(c * c, -1, keepdims=True) + EPSILON)
    xhat = c * inv
    return xhat * gain + shift, xhat, inv


def norm_backward(g, xhat, inv, gain):
    d_gain = jnp.sum(g * xhat, 0, keepdims=True)
    d_shift = jnp.sum(g, 0, keepdims=True)
    gs = g * gain
    dr = inv * (gs - jnp.mean(gs, -1, keepdims=True) - xhat * jnp.mean(gs * xhat, -1, keepdims=True))
    return dr, d_gain, d_shift


def low_half():
    return lax.broadcasted_iota(jnp.int32, (1, 128), 1) < 64


def blocks(size, total, body):
    def step(i, carry):
        body(pl.ds(pl.multiple_of(i * size, size), size))
        return carry

    lax.fori_loop(0, total // size, step, 0, unroll=8)


def attn_forward(x, h, m, w, biases, mask_of, q_ref, k_ref, v_ref, o_ref, e_ref, r_ref, after):
    for n in range(2):
        cols = pl.ds(256 * n, 256)
        part = slice(256 * n, 256 * n + 256)
        q_ref[:, cols] = ((nn(h[...], w[0, :, cols]) + biases[0][:, part]) * 0.125).astype(BF)
        k_ref[:, cols] = nn(m[...], w[1, :, cols]).astype(BF)
        v_ref[:, cols] = (nn(m[...], w[2, :, cols]) + biases[1][:, part]).astype(BF)
    low = low_half()

    def pair(b, carry):
        rows = rows_of(b)
        masked = mask_of(b)
        for j in range(4):
            cols = pl.ds(128 * j, 128)
            q = q_ref[rows, cols]
            k = k_ref[rows, cols]
            v = jnp.concatenate([v_ref[rows, cols], jnp.ones((ROWS, 128), BF)], axis=1)
            parts = []
            for half in range(2):
                mine = low if half == 0 else jnp.logical_not(low)
                s = nt(jnp.where(mine, q, jnp.zeros_like(q)), k) + masked
                e = jnp.exp(s - jnp.max(s, -1, keepdims=True)).astype(BF)
                e_ref[8 * b + 2 * j + half] = e
                parts.append(nn(e, v))
            r = 1.0 / jnp.where(low, parts[0][:, 128:], parts[1][:, 128:])
            r_ref[rows, cols] = r.astype(BF)
            o = jnp.where(low, parts[0][:, :128], parts[1][:, :128]) * r
            o_ref[rows, cols] = o.astype(BF)
        after(rows, b, x(rows) + (nn(o_ref[rows, :], w[3]) + biases[2]))
        return carry

    lax.fori_loop(0, PAIRS, pair, 0, unroll=True)


def attn_backward(b, d_o, q_ref, k_ref, v_ref, o_ref, e_ref, r_ref, dq_ref, dk_ref, dv_ref):
    rows = rows_of(b)
    low = low_half()
    for j in range(4):
        cols = pl.ds(128 * j, 128)
        q = q_ref[rows, cols]
        k = k_ref[rows, cols]
        v = v_ref[rows, cols]
        ds_o = d_o[rows, cols].astype(F32) * r_ref[rows, cols].astype(F32)
        prod = ds_o * o_ref[rows, cols].astype(F32)
        ds_o = ds_o.astype(BF)
        dqs, dks, dvs = [], [], []
        for half in range(2):
            mine = low if half == 0 else jnp.logical_not(low)
            delta = jnp.sum(jnp.where(mine, prod, 0.0), -1, keepdims=True)
            e = e_ref[8 * b + 2 * j + half]
            dp = nt(jnp.where(mine, ds_o, jnp.zeros_like(ds_o)), v)
            ds = (e.astype(F32) * (dp - delta)).astype(BF)
            dvs.append(tn(e, ds_o))
            dqs.append(nn(ds, k))
            dks.append(tn(ds, q))
        dq_ref[rows, cols] = (jnp.where(low, dqs[0], dqs[1]) * 0.125).astype(BF)
        dk_ref[rows, cols] = jnp.where(low, dks[0], dks[1]).astype(BF)
        dv_ref[rows, cols] = jnp.where(low, dvs[0], dvs[1]).astype(BF)


def gelu_both(u):
    c = 0.7978845608028654
    square = u * u
    t = jnp.tanh(c * u * (1.0 + 0.044715 * square))
    half = 0.5 * (1.0 + t)
    act = u * half
    slope = half + (0.5 * c) * u * (1.0 - t * t) * (1.0 + (3.0 * 0.044715) * square)
    return act, slope


def ffn_forward(x, h, w_in, w_out, b_in, b_out, act_ref, slope_ref, after):
    def hidden(cols):
        act, slope = gelu_both(nn(h[...], w_in[:, cols]) + b_in[:, cols])
        act_ref[:, cols] = act.astype(BF)
        slope_ref[:, cols] = slope.astype(BF)

    blocks(256, FF, hidden)

    def pair(b, carry):
        rows = rows_of(b)
        after(rows, b, x(rows) + (nn(act_ref[rows, :], w_out[...]) + b_out))
        return carry

    lax.fori_loop(0, PAIRS, pair, 0, unroll=True)


def ffn_hidden_backward(df, w_out, slope_ref, du_ref, bin_grad):
    def hidden(cols):
        du = nt(df[...], w_out[cols, :]) * slope_ref[:, cols].astype(F32)
        bin_grad[0:1, cols] = jnp.sum(du, 0, keepdims=True)
        du_ref[:, cols] = du.astype(BF)

    blocks(256, FF, hidden)


def ffn_input_backward(dr, w_in, du_ref, dx):
    def pair(b, carry):
        rows = rows_of(b)
        dx[rows, :] = dr[rows, :] + nt(du_ref[rows, :], w_in[...])
        return carry

    lax.fori_loop(0, PAIRS, pair, 0, unroll=True)


def turn(src, cols, dst):
    dst[...] = jnp.transpose(src[:, cols])


def ffn_weight_grads(h_ref, du_ref, act_ref, df_ref, g, turned, base, inner_done):
    turn(h_ref, slice(None), turned)

    def inner(k, carry):
        for n in range(2):
            part = nn(turned[...], du_ref[:, pl.ds(pl.multiple_of(512 * k + 256 * n, 256), 256)])
            at = pl.ds(pl.multiple_of(base + 512 * (k // 2) + 256 * n, 256), 256)
            g[k % 2, :, at] = part.astype(BF)
        return carry

    lax.fori_loop(0, 4, inner, 0, unroll=True)
    inner_done()

    def outer(j, carry):
        turn(act_ref, pl.ds(pl.multiple_of(512 * j, 512), 512), turned)
        rows = pl.ds(pl.multiple_of(128 * j, 128), 128)
        for n in range(2):
            part = nn(turned[...], df_ref[:, 256 * n : 256 * n + 256]).reshape(16, 4, 8, 256)
            for k in range(4):
                at = base + 1024 + 512 * (k % 2) + 256 * n
                g[k // 2, rows, at : at + 256] = part[:, k].reshape(128, 256).astype(BF)
        return carry

    lax.fori_loop(0, 4, outer, 0, unroll=4)


def planes_first(part):
    wide = part.shape[-1]
    return part.reshape(4, 16, 8, wide).transpose(1, 0, 2, 3).reshape(512, wide)


def as_is(part):
    return part


def attn_weight_grads(h_ref, m_ref, o_ref, da_ref, dq_ref, dk_ref, dv_ref, g, turned, base, order):
    def product(side, at, right):
        for n in range(2):
            cols = slice(256 * n, 256 * n + 256)
            start = base + at + 256 * n
            g[side, :, start : start + 256] = order(nn(turned[...], right[:, cols])).astype(BF)

    turn(h_ref, slice(None), turned)
    product(0, 0, dq_ref)
    if m_ref is not h_ref:
        turn(m_ref, slice(None), turned)
    product(1, 0, dk_ref)
    product(0, 512, dv_ref)
    turn(o_ref, slice(None), turned)
    product(1, 512, da_ref)


def send_out(g, core, mine, theirs, sems):
    other = pltpu.make_async_copy(g.at[1 - core], theirs, sems.at[0])
    own = pltpu.make_async_copy(g.at[core], mine, sems.at[1])
    other.start()
    own.start()
    return other, own


class Moves:
    def __init__(self, sems):
        self.sems, self.used, self.open = sems, 0, []

    def start(self, src, dst):
        copy = pltpu.make_async_copy(src, dst, self.sems.at[self.used])
        self.used += 1
        copy.start()
        return copy

    def send(self, src, dst):
        self.open.append(self.start(src, dst))

    def finish(self):
        for copy in self.open:
            copy.wait()


def fetch_pair(moves, gathered, stage, pair, slot):
    return moves.start(gathered.at[:, pl.ds(512 * pair, 512)], stage.at[slot])


def forward_kernel(scalars, gathered, vec, bin_vec, src_h, tgt_h, og_h, *refs):
    (
        dec_h, grad_h,
        q0h, k0h, v0h, o0h, e0h, r0h, q1h, k1h, v1h, o1h, e1h, r1h, q2h, k2h, v2h, o2h, e2h, r2h,
        xh0h, xh1h, xh2h, xh3h, inv0h, inv1h, inv2h, inv3h,
        enc_h, mem_h, first_h, act0h, slope0h, mine, theirs, vec_grad, bin_grad,
        dec, grad_d2,
        q0, k0, v0, o0, e0, r0, q1, k1, v1, o1, e1, r1, q2, k2, v2, o2, e2, r2,
        xh0, xh1, xh2, xh3, inv0, inv1, inv2, inv3,
        enc, mem, first, act0, slope0,
        src, tgt, og, stage, w_attn, w_in, w_out, x32, second,
        act1, slope1, df, g, turned, sems,
    ) = refs
    moves = Moves(sems)
    pairs = {n: fetch_pair(moves, gathered, stage, n, n) for n in (0, 1)}
    src_in = moves.start(src_h, src)

    def bias(layer):
        return [vec[3 * layer + j : 3 * layer + j + 1, :] for j in range(3)]

    def gain(n):
        return vec[9 + n : 10 + n, :]

    def shift(n):
        return vec[14 + n : 15 + n, :]

    def source_keys(b):
        place = lax.broadcasted_iota(jnp.int32, (1, ROWS), 1)
        return jnp.where(place < scalars[b], 0.0, NEGATIVE)

    def target_keys(b):
        at_q = lax.broadcasted_iota(jnp.int32, (ROWS, ROWS), 0)
        at_k = lax.broadcasted_iota(jnp.int32, (ROWS, ROWS), 1)
        live = jnp.logical_and(at_q >= at_k, at_k < scalars[2 + b])
        return jnp.where(live, 0.0, NEGATIVE)

    def keeper(n, xh, inv_ref, low, wide):
        def after(rows, b, r):
            z, xhat, inv = norm_forward(r, gain(n), shift(n))
            xh[rows, :] = xhat.astype(BF)
            inv_ref[rows, :] = jnp.broadcast_to(inv, (ROWS, 128))
            low[rows, :] = z.astype(BF)
            if wide is not None:
                wide[rows, :] = z

        return after

    def from_low(ref):
        return lambda rows: ref[rows, :].astype(F32)

    def from_x32(rows):
        return x32[rows, :]

    src_in.wait()
    prep_attn(stage, 0, [pairs[0], pairs[1]], w_attn)
    for n in range(4):
        pairs[6 + n] = fetch_pair(moves, gathered, stage, 6 + n, 2 + n)
    tgt_in = moves.start(tgt_h, tgt)
    for n in (2, 3):
        pairs[n] = fetch_pair(moves, gathered, stage, n, 4 + n)
    og_in = moves.start(og_h, og)
    pairs[4] = fetch_pair(moves, gathered, stage, 4, 0)
    pairs[5] = fetch_pair(moves, gathered, stage, 5, 1)
    attn_forward(
        from_low(src), src, src, w_attn, bias(0), source_keys, q0, k0, v0, o0, e0, r0,
        keeper(0, xh0, inv0, enc, x32),
    )
    for a, b in ((q0, q0h), (k0, k0h), (v0, v0h), (o0, o0h), (e0, e0h), (r0, r0h),
                 (xh0, xh0h), (inv0, inv0h), (enc, enc_h)):
        moves.send(a, b)
    prep_ffn(stage, 2, [None, None] + [pairs[6 + n] for n in range(4)], w_in, w_out)
    for n in range(4):
        pairs[10 + n] = fetch_pair(moves, gathered, stage, 10 + n, 2 + n)
    ffn_forward(
        from_x32, enc, w_in, w_out, bin_vec.at[0:1], vec[19:20, :], act0, slope0,
        keeper(1, xh1, inv1, mem, None),
    )
    for a, b in ((xh1, xh1h), (inv1, inv1h), (mem, mem_h), (act0, act0h), (slope0, slope0h)):
        moves.send(a, b)
    tgt_in.wait()
    prep_attn(stage, 6, [None] * 6 + [pairs[2], pairs[3]], w_attn)
    attn_forward(
        from_low(tgt), tgt, tgt, w_attn, bias(1), target_keys, q1, k1, v1, o1, e1, r1,
        keeper(2, xh2, inv2, first, x32),
    )
    for a, b in ((q1, q1h), (k1, k1h), (v1, v1h), (o1, o1h), (e1, e1h), (r1, r1h),
                 (xh2, xh2h), (inv2, inv2h), (first, first_h)):
        moves.send(a, b)
    prep_attn(stage, 0, [pairs[4], pairs[5]], w_attn)
    attn_forward(
        from_x32, first, mem, w_attn, bias(2), source_keys, q2, k2, v2, o2, e2, r2,
        keeper(3, xh3, inv3, second, x32),
    )
    for a, b in ((q2, q2h), (k2, k2h), (v2, v2h), (o2, o2h), (e2, e2h), (r2, r2h),
                 (xh3, xh3h), (inv3, inv3h)):
        moves.send(a, b)
    prep_ffn(stage, 2, [None, None] + [pairs[10 + n] for n in range(4)], w_in, w_out)
    vec_grad[...] = jnp.zeros_like(vec_grad)
    bin_grad[...] = jnp.zeros_like(bin_grad)
    og_in.wait()

    def last(rows, b, r):
        z, xhat, inv = norm_forward(r, gain(4), shift(4))
        dec[rows, :] = z.astype(BF)
        at = lax.broadcasted_iota(jnp.int32, (ROWS, 1), 0)
        gz = jnp.where(at < scalars[2 + b], og[rows, :].astype(F32), 0.0)
        dr, d_gain, d_shift = norm_backward(gz, xhat, inv, gain(4))
        vec_grad[0:1, :] += d_gain
        vec_grad[1:2, :] += d_shift
        vec_grad[2:3, :] += jnp.sum(dr, 0, keepdims=True)
        df[rows, :] = dr.astype(BF)
        x32[rows, :] = dr

    ffn_forward(
        from_x32, second, w_in, w_out, bin_vec.at[1:2], vec[20:21, :], act1, slope1, last
    )
    moves.send(dec, dec_h)
    ffn_hidden_backward(df, w_out, slope1, slope1, bin_grad)
    core = scalars[4]

    def inner_done():
        send_gradients(moves, g, core, mine, theirs, 0, 1024)

    ffn_weight_grads(second, slope1, act1, df, g, turned, 0, inner_done)
    send_gradients(moves, g, core, mine, theirs, 1024, 1024)
    ffn_input_backward(x32, w_in, slope1, grad_d2)
    moves.send(grad_d2, grad_h)
    moves.finish()


def norm_rows(vec_grad, grad, xh, inv, gain, low, wide):
    vec_grad[...] = jnp.zeros_like(vec_grad)

    def pair(b, carry):
        rows = rows_of(b)
        dr, d_gain, d_shift = norm_backward(
            grad[rows, :], xh[rows, :].astype(F32), inv[rows, 0:1], gain
        )
        vec_grad[0:1, :] += d_gain
        vec_grad[1:2, :] += d_shift
        vec_grad[2:3, :] += jnp.sum(dr, 0, keepdims=True)
        low[rows, :] = dr.astype(BF)
        wide[rows, :] = dr
        return carry

    lax.fori_loop(0, PAIRS, pair, 0, unroll=True)


def load_attn(moves, far_refs, near_refs):
    far_refs, near_refs = list(far_refs), list(near_refs)
    first = [moves.start(a, b) for a, b in zip(far_refs[:2], near_refs[:2])]
    heads = [moves.start(a, b) for a, b in zip(far_refs[2:8], near_refs[2:8])]
    rows = [moves.start(a, b) for a, b in zip(far_refs[8:], near_refs[8:])]
    return first, heads, rows


def attn_back(grad, data, weights, w, gain, temps, dx, grad_mem, g, base, vec_grad, copies, arrived, order):
    xh, inv, r, o, q, v, k, e, h = data[:9]
    m = data[9] if len(data) > 9 else h
    da, d_o, dq, dk, dv, turned = temps
    first, heads, rows_in = copies
    for copy in first:
        copy.wait()
    norm_rows(vec_grad, grad, xh, inv, gain, da, dx)
    weights()
    for n in range(2):
        cols = pl.ds(256 * n, 256)
        d_o[:, cols] = nt(da[...], w[3, cols, :]).astype(BF)
    for copy in heads:
        copy.wait()
    arrived()

    def body(b, carry):
        attn_backward(b, d_o, q, k, v, o, e, r, dq, dk, dv)
        rows = rows_of(b)
        vec_grad[3:4, :] += jnp.sum(dq[rows, :].astype(F32), 0, keepdims=True)
        vec_grad[4:5, :] += jnp.sum(dv[rows, :].astype(F32), 0, keepdims=True)
        to_m = nt(dk[rows, :], w[1]) + nt(dv[rows, :], w[2])
        to_x = dx[rows, :] + nt(dq[rows, :], w[0])
        if grad_mem is not None:
            grad_mem[rows, :] = to_m
            dx[rows, :] = to_x
        else:
            dx[rows, :] = to_x + to_m
        return carry

    lax.fori_loop(0, PAIRS, body, 0, unroll=True)
    for copy in rows_in:
        copy.wait()
    attn_weight_grads(h, m, o, da, dq, dk, dv, g, turned, base, order)


def send_gradients(moves, g, core, mine, theirs, at, size):
    cols = pl.ds(at, size)
    moves.send(g.at[1 - core, :, cols], theirs.at[:, cols])
    moves.send(g.at[core, :, cols], mine.at[:, cols])


def middle_kernel(scalars, gathered, vec, grad_h, *refs):
    far_cross, far_self, far_ffn = refs[:10], refs[10:19], refs[19:24]
    dtgt_h, denc_h, mine, theirs, cross_vec, self_vec, ffn_vec, bin_grad = refs[24:32]
    near_cross, near_self, near_ffn = refs[32:42], refs[42:51], refs[51:56]
    grad, d1, dtgt, denc, stage, w, w_in, w_out, da, d_o, dq, dk, dv, g, turned, sems = refs[56:]
    moves = Moves(sems)
    core = scalars[4]
    temps = (da, d_o, dq, dk, dv, turned)
    grad_in = moves.start(grad_h, grad)
    cross_pairs = [fetch_pair(moves, gathered, stage, 4 + n, n) for n in range(2)]
    cross_copies = load_attn(moves, far_cross, near_cross)
    self_pairs, self_copies, ffn_pairs, ffn_in = [], [], [None, None], []

    def then_self():
        self_pairs.extend([fetch_pair(moves, gathered, stage, 2 + n, 6 + n) for n in range(2)])
        self_copies.extend(load_attn(moves, far_self, near_self))

    def then_ffn():
        ffn_pairs.extend([fetch_pair(moves, gathered, stage, 6 + n, 2 + n) for n in range(4)])
        ffn_in.extend([moves.start(a, b) for a, b in zip(far_ffn, near_ffn)])

    bin_grad[...] = jnp.zeros_like(bin_grad)
    grad_in.wait()
    attn_back(
        grad, near_cross, lambda: prep_attn(stage, 0, cross_pairs, w), w, vec[12:13, :], temps,
        d1, grad, g, 0, cross_vec, cross_copies, then_self, as_is,
    )
    send_gradients(moves, g, core, mine, theirs, 0, 1024)
    attn_back(
        d1, near_self, lambda: prep_attn(stage, 6, [None] * 6 + self_pairs, w), w, vec[11:12, :],
        temps, dtgt, None, g, 1024, self_vec, self_copies, then_ffn, as_is,
    )
    send_gradients(moves, g, core, mine, theirs, 1024, 1024)
    moves.send(dtgt, dtgt_h)
    for copy in ffn_in:
        copy.wait()
    xh1, inv1, slope, act, enc = near_ffn
    norm_rows(ffn_vec, grad, xh1, inv1, vec[10:11, :], da, grad)
    prep_ffn(stage, 2, ffn_pairs, w_in, w_out)
    ffn_hidden_backward(da, w_out, slope, slope, bin_grad)

    def inner_done():
        send_gradients(moves, g, core, mine, theirs, 2048, 1024)

    ffn_weight_grads(enc, slope, act, da, g, turned, 2048, inner_done)
    send_gradients(moves, g, core, mine, theirs, 3072, 1024)
    ffn_input_backward(grad, w_in, slope, denc)
    moves.send(denc, denc_h)
    moves.finish()


def write_vectors(attn, ffn, ffn_bins, g, at):
    rows = [attn[i][r : r + 1, :] for i in range(3) for r in (3, 4, 2)]
    order = (attn[0], ffn[0], attn[1], attn[2], ffn[1])
    rows += [a[0:1, :] for a in order] + [a[1:2, :] for a in order] + [f[2:3, :] for f in ffn]
    whole = jnp.concatenate(rows + [jnp.zeros((3, 512), F32)], axis=0)
    wide = jnp.concatenate([f[0:1, :] for f in ffn_bins] + [jnp.zeros((6, FF), F32)], axis=0)
    lane = lax.broadcasted_iota(jnp.int32, (8, 128), 1)
    tiles = []
    for p in [16 * x + yz for yz in range(16) for x in range(4)]:
        cols = slice(128 * (p // 16), 128 * (p // 16) + 128)
        tile = jnp.zeros((8, 128), F32)
        for n in range(3):
            turned = pltpu.roll(whole[8 * n : 8 * n + 8, cols], (8 * n - 8 * (p % 16)) % 128, 1)
            tile = jnp.where(lane // 8 == n, turned, tile)
        cols = slice(128 * (p // 4), 128 * (p // 4) + 128)
        turned = pltpu.roll(wide[:, cols], (32 - 32 * (p % 4)) % 128, 1)
        tiles.append(jnp.where(lane // 32 == 1, turned, tile))
    block = jnp.concatenate(tiles, axis=0).astype(BF)
    for side in range(2):
        g[side, :, at : at + 128] = block


def last_kernel(scalars, gathered, vec, a1_vec, a2_vec, f0_vec, f1_vec, f0_bin, f1_bin, *refs):
    far_data, (dx_h, mine, theirs), near_data = refs[:10], refs[10:13], refs[13:23]
    dx, vec_grad, stage, w, da, d_o, dq, dk, dv, g, turned, sems = refs[23:]
    moves = Moves(sems)
    grad_in = moves.start(far_data[0], near_data[0])
    pairs = [fetch_pair(moves, gathered, stage, n, n) for n in range(2)]
    copies = load_attn(moves, far_data[1:], near_data[1:])
    grad_in.wait()
    attn_back(
        near_data[0], near_data[1:], lambda: prep_attn(stage, 0, pairs, w), w, vec[9:10, :],
        (da, d_o, dq, dk, dv, turned), dx, None, g, 0, vec_grad, copies, lambda: None, planes_first,
    )
    write_vectors((vec_grad, a1_vec, a2_vec), (f0_vec, f1_vec), (f0_bin, f1_bin), g, 1024)
    send_gradients(moves, g, scalars[4], mine, theirs, 0, 1152)
    moves.send(dx, dx_h)
    moves.finish()


def spec(space):
    return pl.BlockSpec(memory_space=space)


def call(kernel, name, inputs, outs, scratch, after=()):
    taken = len(inputs)
    inputs = inputs + [(a, H) for a in after]

    def body(*refs):
        kernel(*refs[:taken], *refs[len(inputs) :])

    return pl.pallas_call(
        body,
        name=name,
        in_specs=[spec(s) for _, s in inputs],
        out_specs=[spec(s) for _, _, s in outs],
        out_shape=[jax.ShapeDtypeStruct(shape, kind) for shape, kind, _ in outs],
        scratch_shapes=scratch,
        compiler_params=pltpu.CompilerParams(vmem_limit_bytes=VMEM),
        cost_estimate=pl.CostEstimate(flops=10**10, bytes_accessed=10**7, transcendentals=0),
    )(*[a for a, _ in inputs])


V, H, S = pltpu.VMEM, pl.ANY, pltpu.SMEM
ROW = ((ALL, D), BF)
WIDE = ((ALL, FF), BF)
LINE = ((ALL, D), F32)
INV = ((ALL, 128), F32)
EXP = ((8 * PAIRS, ROWS, ROWS), BF)
VEC = ((8, D), F32, V)
BIN = ((8, FF), F32, V)


def far(kinds):
    return [(shape, kind, H) for shape, kind in kinds]


def near(kinds):
    return [V(shape, kind) for shape, kind in kinds]


def run_vectors(block):
    return call(vector_kernel, "vectors", [(block, V)], [((32, D), F32, V), BIN], [])


def run_forward(scalars, gathered, vec, bin_vec, src, tgt, og):
    kept = (
        [ROW, LINE] + [ROW, ROW, ROW, ROW, EXP, ROW] * 3 + [ROW] * 4 + [INV] * 4
        + [ROW] * 3 + [WIDE, WIDE]
    )
    outs = far(kept) + [((D, FF), BF, H)] * 2 + [VEC, BIN]
    scratch = near(kept) + near([ROW, ROW, ROW]) + [
        V((8, 1024, 512), BF), V((4, 512, 512), BF),
        V((D, FF), BF), V((FF, D), BF), V((ALL, D), F32), V((ALL, D), BF),
        V((ALL, FF), BF), V((ALL, FF), BF), V((ALL, D), BF),
        V((2, D, FF), BF), V((D, ALL), BF), pltpu.SemaphoreType.DMA((64,)),
    ]
    return call(
        forward_kernel, "forward",
        [(scalars, S), (gathered, H), (vec, V), (bin_vec, V), (src, H), (tgt, H), (og, H)], outs, scratch,
    )


ATTN_DATA = [ROW, INV, ROW, ROW, ROW, ROW, ROW, EXP, ROW]


def attn_data(xh, inv, heads, *rows):
    q, k, v, o, e, r = heads
    return [xh, inv, r, o, q, v, k, e, *rows]


def run_middle(scalars, gathered, vec, grad, cross, own, ffn, after=()):
    kinds = ATTN_DATA + [ROW] + ATTN_DATA + [ROW, INV, WIDE, WIDE, ROW]
    inputs = [(scalars, S), (gathered, H), (vec, V)]
    inputs += [(a, H) for a in (grad, *cross, *own, *ffn)]
    outs = far([LINE, LINE]) + [((D, 4096), BF, H)] * 2 + [VEC, VEC, VEC, BIN]
    scratch = near(kinds) + near([LINE] * 4) + [
        V((8, 1024, 512), BF), V((4, 512, 512), BF), V((D, FF), BF), V((FF, D), BF),
        *near([ROW] * 5), V((2, D, 4096), BF), V((D, ALL), BF), pltpu.SemaphoreType.DMA((56,)),
    ]
    return call(middle_kernel, "middle", inputs, outs, scratch, after)


def run_last(scalars, gathered, vec, sums, data, after=()):
    kinds = [LINE] + ATTN_DATA
    inputs = [(scalars, S), (gathered, H), (vec, V)]
    inputs += [(a, V) for a in sums] + [(a, H) for a in data]
    outs = far([LINE]) + [((D, 1152), BF, H)] * 2
    scratch = near(kinds) + near([LINE]) + [
        V((8, D), F32), V((2, 1024, 512), BF), V((4, 512, 512), BF), *near([ROW] * 5),
        V((2, D, 1152), BF), V((D, ALL), BF), pltpu.SemaphoreType.DMA((24,)),
    ]
    return call(last_kernel, "last", inputs, outs, scratch, after)


def pack_shard(c, attn_proj, attn_out, attn_bias, norm_gain, norm_shift, ffn_in, ffn_out, b_in, b_out):
    attn = jnp.concatenate([attn_proj, attn_out[:, None]], axis=1).reshape(12, 4, 512)
    wide = ffn_in.reshape(2, 4, 4, 512).transpose(0, 2, 1, 3).reshape(8, 4, 512)
    both = lax.all_gather(jnp.concatenate([attn, wide]), "c", axis=1, tiled=True)
    half = lax.dynamic_index_in_dim(both.reshape(10, 2, 8, 512), c, 1, False)
    tall = ffn_out.reshape(2, 2, 8, 512)
    blocks = jnp.concatenate([half[:8], tall[0], half[8:], tall[1]])
    vec = [attn_bias.reshape(9, 4), norm_gain, norm_shift, b_out, jnp.zeros((3, 4), BF)]
    line = jnp.concatenate(vec + [b_in.reshape(8, 4)]).T.reshape(1, 128)
    return blocks.transpose(1, 0, 2).reshape(8, 7168), line


def swap(a):
    return lax.ppermute(a, "c", [(0, 1), (1, 0)])


def pair_sum(mine, theirs):
    return (mine.astype(F32) + swap(theirs).astype(F32)).astype(BF)


def ring_sum(whole):
    return lax.psum_scatter(whole, "x", scatter_dimension=0, tiled=True)


def plane_sum(whole):
    whole = whole.reshape(16, -1, whole.shape[1])
    whole = lax.all_to_all(whole, ("y", "z"), 0, 0, tiled=True)
    return jnp.sum(whole.astype(F32), axis=0)


def line_sum(whole):
    blocks = whole.reshape(4, 8, -1)
    x = lax.axis_index("x")
    total = lax.dynamic_index_in_dim(blocks, x, 0, False)
    for k in range(1, 4):
        part = lax.dynamic_index_in_dim(blocks, (x + k) % 4, 0, False).astype(BF)
        part = lax.ppermute(part, "x", [(i, (i + k) % 4) for i in range(4)])
        total = total + part.astype(F32)
    return total


def per_device(source, target, src_len, tgt_len, out_grad, *weights):
    c = lax.axis_index("c")
    shard, line = pack_shard(c, *weights)
    gathered = lax.all_gather(shard, AXES, axis=0, tiled=True)
    vec, bin_vec = run_vectors(lax.all_gather(line, AXES, axis=0, tiled=True))
    scalars = jnp.concatenate(
        [src_len.reshape(2), tgt_len.reshape(2), c.astype(jnp.int32)[None], jnp.zeros(3, jnp.int32)]
    )
    src, tgt, og = (a.reshape(ALL, D) for a in (source, target, out_grad))
    outs = run_forward(scalars, gathered, vec, bin_vec, src, tgt, og)
    dec, grad = outs[:2]
    heads = [outs[2 + 6 * i : 8 + 6 * i] for i in range(3)]
    xh, inv = outs[20:24], outs[24:28]
    enc, mem, first, act0, slope0, f1_mine, f1_theirs, f1_vec, f1_bin = outs[28:]
    f1 = pair_sum(f1_mine, f1_theirs)
    f1_x = ring_sum(f1)
    d_tgt, d_enc, mid_mine, mid_theirs, a2_vec, a1_vec, f0_vec, f0_bin = run_middle(
        scalars, gathered, vec, grad, attn_data(xh[3], inv[3], heads[2], first, mem),
        attn_data(xh[2], inv[2], heads[1], tgt), [xh[1], inv[1], slope0, act0, enc], (f1,),
    )
    f1_x, mid_mine = lax.optimization_barrier((f1_x, mid_mine))
    mid = pair_sum(mid_mine, mid_theirs)
    mid_x = ring_sum(mid)
    d_src, end_mine, end_theirs = run_last(
        scalars, gathered, vec, (a1_vec, a2_vec, f0_vec, f1_vec, f0_bin, f1_bin),
        [d_enc, *attn_data(xh[0], inv[0], heads[0], src)], (mid,),
    )
    end = plane_sum(pair_sum(end_mine, end_theirs))
    f1_x, end = lax.optimization_barrier((f1_x, end))
    sum_f1 = plane_sum(f1_x)
    mid_x, sum_f1 = lax.optimization_barrier((mid_x, sum_f1))
    sum_mid = plane_sum(mid_x)
    sum_end = line_sum(end)

    cut = sum_end[:, 1024:]
    vecs = cut[:, :24].reshape(8, 3, 2, 4).transpose(1, 0, 2, 3).reshape(24, 2, 4)
    vecs = lax.dynamic_index_in_dim(vecs, c, 1, False)
    g_bin = lax.dynamic_index_in_dim(cut[:2, 32:64].reshape(2, 2, 16), c, 1, False)
    whole = jnp.concatenate([sum_end[:, :1024], sum_mid[:, 1024:2048], sum_mid[:, :1024], sum_mid[:, 2048:], sum_f1], axis=1)
    attn = whole[:, :3072].reshape(2, 4, 6, 512)
    wide = whole[:, 3072:].reshape(8, 2, 4, 512)
    rows = jnp.concatenate([attn, wide[:, :, :2].reshape(2, 4, 4, 512)], axis=2)
    keep = lax.dynamic_index_in_dim(rows, c, 0, False)
    got = swap(lax.dynamic_index_in_dim(rows, 1 - c, 0, False))
    first_half = jnp.where(c == 0, keep, got)
    second_half = jnp.where(c == 0, got, keep)
    a = first_half[:, :6].reshape(4, 3, 2, 512)
    b = second_half[:, :6].reshape(4, 3, 2, 512)
    g_proj = jnp.stack([a[:, :, 0], b[:, :, 0], a[:, :, 1]], axis=0).transpose(2, 0, 1, 3)
    g_out = b[:, :, 1].transpose(1, 0, 2)
    ia = first_half[:, 6:].reshape(4, 2, 2, 512)
    ib = second_half[:, 6:].reshape(4, 2, 2, 512)
    g_in = jnp.stack([ia, ib], axis=3).transpose(1, 0, 2, 3, 4).reshape(2, 4, 2048)
    g_wout = wide[:, :, 2:].transpose(1, 2, 0, 3).reshape(2, 16, 512)
    shape = source.shape
    return (
        dec.reshape(shape), d_src.reshape(shape), d_tgt.reshape(shape),
        g_proj, g_out, vecs[:9].reshape(3, 3, 4), vecs[9:14], vecs[14:19],
        g_in, g_wout, g_bin, vecs[19:21],
    )


def solution(mesh):
    mesh = Mesh(mesh.devices.reshape(4, 4, 4, 2), AXES)
    rows = P(None, AXES, None, None)
    lens = P(None, AXES)
    weights = (
        P(None, None, AXES, None), P(None, AXES, None), P(None, None, AXES), P(None, AXES),
        P(None, AXES), P(None, AXES, None), P(None, AXES, None), P(None, AXES), P(None, AXES),
    )
    return jax.shard_map(
        per_device,
        mesh=mesh,
        in_specs=(rows, rows, lens, lens, rows) + weights,
        out_specs=(rows, rows, rows) + weights,
        check_vma=False,
    )
```
